128 devices in a mesh: gz: 32 (over y, x, core), xy: 4 (over z).
Axes of the slice: x: 4, y: 4, z: 4, core: 2. Of those that a mesh axis runs over, the one named last changes fastest.
Arguments:
- patches: bfloat16 [64, 32, 256, 256], P('gz', 'xy'), may hold values from -8 to 8
- offsets: int32 [2, 2, 64, 32], P(None, None, 'gz', 'xy'), may hold values from -2 to 2
- valid: int32 [64, 32], P('gz', 'xy'), may hold values 0 or 1
Outputs:
- positions: float32 [2, 64, 32], P(None, 'gz', 'xy')
- residual: float32 [2, 64, 32], P(None, 'gz', 'xy')
The draws below stay inside these ranges and needn't reach their ends.
All inputs are finite; a program needn't handle non-finite values. No bound on the sum of `valid` on one device may be relied on, other than what follows from the above.
Results may differ from the reference program's by a relative error of at most 0.003.
Values may be sent and summed in bfloat16 or wider, within the bound.
A program may use at most 128 MiB of HBM per device.

```python
import math
import jax
import jax.numpy as jnp
from jax import lax

P_SIZE = 256
COLS = 8
ITERS = 3
SECTIONS = 64
ROWS = 4
NODES = 32


def draw_patches(key, part):
    key = jax.random.fold_in(key, 11)
    values = jax.random.truncated_normal(key, -6.0, 6.0, (SECTIONS, NODES, P_SIZE, P_SIZE), jnp.float32)
    return values.astype(jnp.bfloat16)


def touch_ends(entries, own_key, low, largest):
    longest = entries.shape.index(max(entries.shape))
    spots = []
    for shift in (0, 1):
        where = [jax.random.randint(jax.random.fold_in(own_key, axis), (), 0, length) for axis, length in enumerate(entries.shape)]
        where[longest] = (where[longest] + shift) % entries.shape[longest]
        spots.append(tuple(where))
    return entries.at[spots[0]].set(low).at[spots[1]].set(largest)


def setup_inputs(seed: int = 0) -> dict:
    streams_of = jax.random.split(jax.random.key(seed), 4)
    return {
        "patches": draw_patches(jax.random.fold_in(streams_of[3], 71), 0),
        "offsets": touch_ends(jax.random.randint(streams_of[1], (2, 2, SECTIONS, NODES), -2, 3), jax.random.fold_in(streams_of[1], 1), -2, 2).astype(jnp.int32),
        "valid": touch_ends((jax.random.randint(streams_of[2], (SECTIONS, NODES), 0, 8) < 7).astype(jnp.int32), jax.random.fold_in(streams_of[2], 1), 0, 1),
    }


lam_tether = 0.25
spring_in = 1.0
highest = lax.Precision.HIGHEST


def dft_tables(length):
    counter = jnp.arange(length, dtype=jnp.int32)
    turn_count = jnp.mod(counter[:, None] * counter[None, :], length)
    angles = turn_count.astype(jnp.float32) * (2.0 * math.pi / length)
    return jnp.cos(angles).astype(jnp.bfloat16), jnp.sin(angles).astype(jnp.bfloat16)


def inverse_tables(length):
    counter = jnp.arange(length, dtype=jnp.int32)
    turn_count = jnp.mod(counter[:, None] * counter[None, :], length)
    angles = turn_count.astype(jnp.float32) * (2.0 * math.pi / length)
    return jnp.cos(angles), jnp.sin(angles)


def spectrum(images, cosine_table, sine_table):
    length = images.shape[-1]
    columns_table = jnp.concatenate([cosine_table, sine_table], axis=1).astype(jnp.float32)
    rows_table = jnp.concatenate([cosine_table, sine_table], axis=0).astype(jnp.float32)
    rowwise = jnp.einsum("bmn,nl->bml", images.astype(jnp.float32), columns_table, precision=highest)
    rowwise = rowwise.astype(jnp.bfloat16).astype(jnp.float32)
    stacked = jnp.einsum("km,bml->bkl", rows_table, rowwise, precision=highest)
    real_part = stacked[:, :length, :length] - stacked[:, length:, length:]
    imag_part = -(stacked[:, :length, length:] + stacked[:, length:, :length])
    return real_part.astype(jnp.bfloat16), imag_part.astype(jnp.bfloat16)


def full_map(own_real, own_imag, partner_real, partner_imag, cosine_full, sine_full):
    length = own_real.shape[-1]
    own_re = own_real.astype(jnp.float32)
    own_im = own_imag.astype(jnp.float32)
    par_re = partner_real.astype(jnp.float32)
    par_im = partner_imag.astype(jnp.float32)
    cross_real = own_re * par_re + own_im * par_im
    cross_imag = own_re * par_im - own_im * par_re
    stacked = jnp.concatenate([cross_real, cross_imag], axis=1)
    right_table = jnp.concatenate([cosine_full, sine_full], axis=1)
    mixed = jnp.einsum("nkl,lj->nkj", stacked, right_table, precision=highest)
    half_real = mixed[:, :length, :length] - mixed[:, length:, length:]
    half_imag = mixed[:, :length, length:] + mixed[:, length:, :length]
    left_table = jnp.concatenate([cosine_full, -sine_full], axis=1)
    both = jnp.concatenate([half_real, half_imag], axis=1)
    values = jnp.einsum("ik,nkj->nij", left_table, both, precision=highest)
    return values / float(length * length)


def spring_terms(values, shift_x, shift_y, usable, length):
    scores = values / float(length)
    top = jnp.max(scores, axis=(1, 2), keepdims=True)
    raised = jnp.exp(scores - top)
    prob = raised / jnp.sum(raised, axis=(1, 2), keepdims=True)
    counter = jnp.arange(length, dtype=jnp.int32)
    half = length // 2
    lag_x = (jnp.mod(counter[None, :] - shift_x[:, None] + half, length) - half).astype(jnp.float32)
    lag_y = (jnp.mod(counter[None, :] - shift_y[:, None] + half, length) - half).astype(jnp.float32)
    step_x = jnp.sum(jnp.sum(prob, axis=1) * lag_x, axis=1)
    step_y = jnp.sum(jnp.sum(prob, axis=2) * lag_y, axis=1)
    pick_y = (counter[None, :] == jnp.mod(shift_y, length)[:, None]).astype(jnp.float32)
    pick_x = (counter[None, :] == jnp.mod(shift_x, length)[:, None]).astype(jnp.float32)
    at_offset = jnp.sum(scores * pick_y[:, :, None] * pick_x[:, None, :], axis=(1, 2))
    weight = usable * (0.5 + jax.nn.sigmoid(at_offset))
    target = jnp.stack([shift_x.astype(jnp.float32) + step_x, shift_y.astype(jnp.float32) + step_y])
    return weight, target


def pad_axis(array, axis, before, after):
    widths = [(0, 0)] * array.ndim
    widths[axis] = (before, after)
    return jnp.pad(array, widths)


def reference(patches, offsets, valid):
    sections = patches.shape[0]
    node_count = patches.shape[1]
    length = patches.shape[2]
    cosine_table, sine_table = dft_tables(length)
    cosine_full, sine_full = inverse_tables(length)
    usable_all = valid.astype(jnp.float32)
    order = jnp.arange(sections, dtype=jnp.int32)

    def visit(carry, item):
        near_real, near_imag, far_real, far_imag, near_use, far_use = carry
        images, shifts, usable, where = item
        own_real, own_imag = spectrum(images, cosine_table, sine_table)
        outcome = []
        partners = ((near_real, near_imag, near_use), (far_real, far_imag, far_use))
        for distance in range(2):
            partner_real, partner_imag, partner_use = partners[distance]
            within = (where + distance + 1 < sections).astype(jnp.float32)
            values = full_map(own_real, own_imag, partner_real, partner_imag, cosine_full, sine_full)
            outcome.append(spring_terms(values, shifts[distance, 0], shifts[distance, 1], usable * partner_use * within, length))
        fresh = (own_real, own_imag, near_real, near_imag, usable, near_use)
        return fresh, (outcome[0][0], outcome[1][0], outcome[0][1], outcome[1][1])

    empty_spec = jnp.zeros((node_count, length, length), jnp.bfloat16)
    empty_use = jnp.zeros((node_count,), jnp.float32)
    init = (empty_spec, empty_spec, empty_spec, empty_spec, empty_use, empty_use)
    items = (patches, jnp.moveaxis(offsets, 2, 0), usable_all, order)
    unused, gathered = lax.scan(visit, init, items, reverse=True)
    w_near, w_far, d_near, d_far = gathered

    def grid(array):
        return array.reshape(array.shape[:-1] + (ROWS, COLS))

    weights = [grid(w_near), grid(w_far)]
    targets = [grid(jnp.moveaxis(d_near, 1, 0)), grid(jnp.moveaxis(d_far, 1, 0))]

    def operate(operand):
        result = lam_tether * operand
        row_step = operand[:, :, 1:, :] - operand[:, :, :-1, :]
        result = result + spring_in * (pad_axis(row_step, 2, 1, 0) - pad_axis(row_step, 2, 0, 1))
        col_step = operand[:, :, :, 1:] - operand[:, :, :, :-1]
        result = result + spring_in * (pad_axis(col_step, 3, 1, 0) - pad_axis(col_step, 3, 0, 1))
        for distance in (1, 2):
            weight_now = weights[distance - 1][: sections - distance]
            pulled = weight_now * (operand[:, distance:] - operand[:, :-distance])
            result = result + pad_axis(pulled, 1, distance, 0) - pad_axis(pulled, 1, 0, distance)
        return result

    initial = jnp.cumsum(targets[0], axis=1) - targets[0]
    right_side = lam_tether * initial
    for distance in (1, 2):
        weighted = weights[distance - 1][: sections - distance] * targets[distance - 1][:, : sections - distance]
        right_side = right_side + pad_axis(weighted, 1, distance, 0) - pad_axis(weighted, 1, 0, distance)

    positions = initial
    residual = right_side - operate(initial)
    direction = residual
    norm_now = jnp.sum(residual * residual)
    for iteration in range(ITERS):
        applied = operate(direction)
        step_size = norm_now / jnp.sum(direction * applied)
        positions = positions + step_size * direction
        residual = residual - step_size * applied
        norm_next = jnp.sum(residual * residual)
        direction = residual + (norm_next / norm_now) * direction
        norm_now = norm_next
    return positions.reshape(2, sections, NODES), residual.reshape(2, sections, NODES)
```

```python
import functools
import math

import jax
import jax.numpy as jnp
import numpy as np
from jax import lax
from jax.experimental import pallas as pl
from jax.experimental.pallas import tpu as pltpu
from jax.sharding import PartitionSpec as P

SIZE = 256
HALF = 128
NODES_DEV = 8
COLS = 8
ITERS = 3
LANES = 128
MESH = pl.DeviceIdType.MESH
LAM = 0.25


def tables():
    index = np.arange(SIZE)
    angles = ((index[:, None] * index[None, :]) % SIZE) * (2.0 * math.pi / SIZE)
    rows = np.concatenate([np.cos(angles)[:HALF], np.sin(angles)[:HALF]])
    rows[HALF] = np.cos(angles)[HALF]

    return rows.astype(np.float32), np.ascontiguousarray(rows.T).astype(np.float32)


def split(values):
    high = values.astype(jnp.bfloat16)
    low = (values - high.astype(jnp.float32)).astype(jnp.bfloat16)
    return high, low


def dot(left, right):
    return jnp.dot(left, right, preferred_element_type=jnp.float32)


def pack_spectrum(grid, rows, first):
    a = grid[rows, :HALF]
    c = grid[rows, HALF:]
    lower = slice(HALF + rows.start, HALF + rows.stop)
    d = grid[lower, :HALF]
    b = grid[lower, HALF:]
    col0 = lax.broadcasted_iota(jnp.int32, a.shape, 1) == 0
    plus_re = jnp.where(col0, a, a - b)
    plus_im = jnp.where(col0, d, c + d)
    minus_re = jnp.where(col0, c, a + b)
    minus_im = jnp.where(col0, b, c - d)
    if first:
        row0 = lax.broadcasted_iota(jnp.int32, a.shape, 0) == 0
        plus_re = jnp.where(row0, a, plus_re)
        plus_im = jnp.where(row0, c, plus_im)
        minus_re = jnp.where(row0, d, minus_re)
        minus_im = jnp.where(row0, b, minus_im)
    return plus_re, plus_im, minus_re, minus_im


def cross_terms(own, other, first):
    pr, pj, mr, mj = own
    qr, qj, nr, nj = other
    rr = pr * qr
    jj = pj * qj
    rp = rr + jj
    qp = pr * qj - pj * qr
    mrr = mr * nr
    mjj = mj * nj
    rm = mrr + mjj
    qm = mr * nj - mj * nr
    col0 = lax.broadcasted_iota(jnp.int32, pr.shape, 1) == 0
    cc = rp + jnp.where(col0, 0.0, rm)
    sc = qp - jnp.where(col0, 0.0, qm)
    cs = jnp.where(col0, rm, qp + qm)
    ss = jnp.where(col0, qm, rm - rp)
    if first:
        row0 = lax.broadcasted_iota(jnp.int32, pr.shape, 0) == 0
        corner = jnp.logical_and(row0, col0)
        cc = jnp.where(row0, jnp.where(corner, 0.5 * rr, rp), cc)
        cs = jnp.where(row0, jnp.where(corner, 0.5 * jj, qp), cs)
        sc = jnp.where(row0, jnp.where(corner, 0.5 * mrr, rm), sc)
        ss = jnp.where(row0, jnp.where(corner, 0.5 * mjj, qm), ss)
    return cc, cs, sc, ss


def to_column(row):
    count = NODES_DEV
    wide = jnp.broadcast_to(row, (count, count))
    diagonal = lax.broadcasted_iota(jnp.int32, (count, count), 0) == lax.broadcasted_iota(
        jnp.int32, (count, count), 1
    )
    return jnp.sum(jnp.where(diagonal, wide, 0.0), axis=1, keepdims=True)


def total(values):
    return jnp.sum(jnp.sum(values, axis=0, keepdims=True), axis=1, keepdims=True)


def kernel(
    n_gz, n_xy,
    patches, offsets, valid, rows_table, columns_table,
    positions_out, residual_out,
    right_fwd, left_fwd, right_inv, left_inv, images, spec, mix, maps, lag_rows, stats, nears, shifts, shifts_prior,
    strip, slabs, final,
    image_sems, send_sems, recv_sems, shift_sems, strip_sems, slab_sems,
):
    gz = lax.axis_index("gz")
    xy = lax.axis_index("xy")
    after = lax.rem(gz + 1, n_gz)
    before = lax.rem(gz + n_gz - 1, n_gz)

    def image_copy(section, node):
        return pltpu.make_async_copy(
            patches.at[section, node], images.at[node, section], image_sems.at[section, node]
        )

    @pl.loop(0, NODES_DEV)
    def _(node):
        image_copy(0, node).start()
        image_copy(1, node).start()

    barrier = pltpu.get_barrier_semaphore()

    @pl.loop(1, n_gz)
    def _(step):
        pl.semaphore_signal(
            barrier, inc=1, device_id=(lax.rem(gz + step, n_gz), xy), device_id_type=MESH
        )

    @pl.loop(1, n_xy)
    def _(step):
        pl.semaphore_signal(
            barrier, inc=1, device_id=(gz, lax.rem(xy + step, n_xy)), device_id_type=MESH
        )

    left_fwd[...] = rows_table[...].astype(jnp.bfloat16)
    right_fwd[...] = columns_table[...].astype(jnp.bfloat16)
    high, low = split(rows_table[...])
    right_inv[...] = jnp.concatenate([high, high, low], axis=0)
    high, low = split(columns_table[...] * (2.0 / math.log(2.0) / float(SIZE) ** 3))
    left_inv[...] = jnp.concatenate([high, high, low], axis=1)

    lag = lax.rem(lax.broadcasted_iota(jnp.int32, (SIZE, LANES), 0) + HALF, SIZE) - HALF
    lag_rows[...] = lag.astype(jnp.float32)
    moves = offsets[...].astype(jnp.float32)
    for partner in range(2):
        for section in range(2):
            for component in range(2):
                column = to_column(moves[partner, component, section : section + 1, :])
                place = (partner * 2 + section) * 2 + component
                shifts[place] = jnp.broadcast_to(column, (NODES_DEV, LANES))

    def spectrum_copy(way, node):
        return pltpu.make_async_remote_copy(
            src_ref=spec.at[1 + way, node], dst_ref=spec.at[3 - 3 * way, node],
            send_sem=send_sems.at[way, node], recv_sem=recv_sems.at[way, node],
            device_id=((before, after)[way], xy), device_id_type=MESH,
        )

    def shift_copy():
        return pltpu.make_async_remote_copy(
            src_ref=shifts.at[pl.ds(6, 2)], dst_ref=shifts_prior,
            send_sem=shift_sems.at[0], recv_sem=shift_sems.at[1],
            device_id=(after, xy), device_id_type=MESH,
        )

    @pl.loop(0, NODES_DEV)
    def _(node):
        image_copy(0, node).wait()
        image_copy(1, node).wait()
        both = images[node].reshape(2 * SIZE, SIZE)
        rowwise = dot(both, right_fwd[...]).astype(jnp.bfloat16)
        for section in range(2):
            grid = dot(left_fwd[...], rowwise[section * SIZE : (section + 1) * SIZE])
            for rows, first in ((slice(0, 16), True), (slice(16, HALF), False)):
                parts = pack_spectrum(grid, rows, first)
                for part in range(4):
                    spec[section + 1, node, part, rows, :] = parts[part].astype(jnp.bfloat16)

        @pl.when(node == 0)
        def _():
            pl.semaphore_wait(barrier, n_gz + n_xy - 2)
            shift_copy().start()

        spectrum_copy(0, node).start()
        spectrum_copy(1, node).start()

    core = lax.rem(gz, 2)

    def correlate(slot, one, two, group, node):
        for rows, first in ((slice(0, 16), True), (slice(16, HALF), False)):
            own = [spec[one, node, part, rows, :].astype(jnp.float32) for part in range(4)]
            other = [spec[two, node, part, rows, :].astype(jnp.float32) for part in range(4)]
            terms = cross_terms(own, other, first)
            lower = slice(HALF + rows.start, HALF + rows.stop)
            for part, (where, lanes) in enumerate(
                ((rows, 0), (rows, HALF), (lower, 0), (lower, HALF))
            ):
                high, low = split(terms[part])
                mix[slot, where, lanes : lanes + HALF] = high
                mix[slot, where, SIZE + lanes : SIZE + lanes + HALF] = low
        left = jnp.concatenate([mix[slot], mix[slot, :, :SIZE]], axis=1)
        high, low = split(dot(left, right_inv[...]))
        maps[slot] = dot(left_inv[...], jnp.concatenate([high, low, high], axis=0))
        top = jnp.max(maps[slot], axis=(0, 1), keepdims=True)
        mass, moment, rim = [], [], []
        for side in range(2):
            raised = jnp.exp2(maps[slot, :, side * HALF : (side + 1) * HALF] - top)
            mass.append(jnp.sum(raised, axis=0, keepdims=True))
            moment.append(jnp.sum(raised * lag_rows[...], axis=0, keepdims=True))
            rim.append(raised[HALF - 8 : HALF + 8])
        rim = rim[0] + rim[1]
        stats[group, node] = jnp.concatenate([*mass, *moment, rim[6:10]], axis=0)
        low_lane = lax.broadcasted_iota(jnp.int32, (8, HALF), 1) < HALF // 2
        for place, start in ((0, 0), (1, SIZE - 8)):
            edge = maps[slot, start : start + 8, :]
            nears[group, node, place] = jnp.where(low_lane, edge[:, :HALF], edge[:, HALF:])

    @pl.loop(0, 16)
    def _(step):
        in_own = step < 4
        next_from = 4 + 4 * core
        in_next = jnp.logical_and(step >= next_from, step < next_from + 8)
        prior_from = 12 - 8 * core
        in_prior = jnp.logical_and(step >= prior_from, step < prior_from + 4)
        node_next = jnp.clip(step - next_from, 0, 7)
        node_pair = jnp.where(in_own, 2 * step, jnp.clip(2 * (step - prior_from), 0, 6))
        first_node = jnp.where(in_next, node_next, node_pair)
        second_node = jnp.where(in_next, node_next, node_pair + 1)

        @pl.when(in_next)
        def _():
            spectrum_copy(0, node_next).wait_recv()

        @pl.when(in_prior)
        def _():
            spectrum_copy(1, node_pair).wait_recv()
            spectrum_copy(1, node_pair + 1).wait_recv()

        first_one = jnp.where(in_prior, 0, 1)
        second_one = jnp.where(in_prior, 0, jnp.where(in_next, 2, 1))
        both_two = jnp.where(in_next, 3, 2)
        first_group = jnp.where(in_next, 2, jnp.where(in_prior, 3, 0))
        second_group = jnp.where(in_next, 1, jnp.where(in_prior, 3, 0))
        correlate(0, first_one, both_two, first_group, first_node)
        correlate(1, second_one, both_two, second_group, second_node)

    shift_copy().wait()

    columns = lax.broadcasted_iota(jnp.int32, (NODES_DEV, HALF), 1)
    near_lane = jnp.where(columns < HALF // 2, columns, columns - HALF)
    weights = []
    targets = []
    for group, place in ((0, 0), (1, 2), (2, 4), (3, None)):
        if place is None:
            move_x, move_y = shifts_prior[0], shifts_prior[1]
        else:
            move_x, move_y = shifts[place], shifts[place + 1]
        move_x = move_x.astype(jnp.int32)
        move_y = move_y.astype(jnp.int32)
        whole = 0.0
        sum_x = 0.0
        for side in range(2):
            mass = stats[group, :, side, :]
            lag_x = jnp.bitwise_and(columns + side * HALF - move_x + HALF, SIZE - 1) - HALF + move_x
            whole = whole + mass
            sum_x = sum_x + mass * lag_x.astype(jnp.float32)
        sum_y = stats[group, :, 2, :] + stats[group, :, 3, :]
        for row in range(4):
            plain = HALF - 2 + row if row < 2 else row - 2 - HALF
            lag_y = jnp.bitwise_and(row - 2 - move_y, SIZE - 1) - HALF + move_y
            sum_y = sum_y + stats[group, :, 4 + row, :] * (lag_y - plain).astype(jnp.float32)
        picked = jnp.zeros((NODES_DEV, HALF), jnp.float32)
        for row in range(-2, 3):
            near = nears[group, :, 0 if row >= 0 else 1, row % 8, :]
            picked = picked + jnp.where(move_y == row, near, 0.0)
        picked = jnp.where(near_lane == move_x, picked, 0.0)
        whole = jnp.sum(whole, axis=1, keepdims=True)
        sum_x = jnp.sum(sum_x, axis=1, keepdims=True)
        sum_y = jnp.sum(sum_y, axis=1, keepdims=True)
        score = jnp.sum(picked, axis=1, keepdims=True) * math.log(2.0)
        weights.append(0.5 + 1.0 / (1.0 + jnp.exp(-score)))
        targets.append((sum_x / whole, sum_y / whole))

    lane = lax.broadcasted_iota(jnp.int32, (NODES_DEV, LANES), 1)
    node_lane = jnp.bitwise_and(lane, 31) == NODES_DEV * xy + lax.broadcasted_iota(
        jnp.int32, (NODES_DEV, LANES), 0
    )
    odd = lane >= 64
    second = jnp.bitwise_and(lane, 32) > 0

    def place_row(even_x, even_y, odd_x, odd_y):
        chosen = jnp.where(
            odd, jnp.where(second, odd_y, odd_x), jnp.where(second, even_y, even_x)
        )
        return jnp.sum(jnp.where(node_lane, chosen, 0.0), axis=0, keepdims=True)

    marks = valid[...].astype(jnp.float32)
    mark_even, mark_odd = to_column(marks[0:1, :]), to_column(marks[1:2, :])
    strip[xy] = jnp.concatenate(
        [
            place_row(weights[0], weights[0], weights[1], weights[1]),
            place_row(*targets[0], *targets[1]),
            place_row(weights[2], weights[2], weights[3], weights[3]),
            place_row(*targets[2], *targets[3]),
            place_row(mark_even, mark_even, mark_odd, mark_odd),
            jnp.zeros((3, LANES), jnp.float32),
        ],
        axis=0,
    )

    def strip_copy(step):
        return pltpu.make_async_remote_copy(
            src_ref=strip.at[xy], dst_ref=strip.at[xy],
            send_sem=strip_sems.at[0], recv_sem=strip_sems.at[1],
            device_id=(gz, lax.rem(xy + step, n_xy)), device_id_type=MESH,
        )

    @pl.loop(1, n_xy)
    def _(step):
        strip_copy(step).start()

    others = strip.at[pl.ds(0, n_xy - 1)]
    pltpu.make_async_copy(others, others, strip_sems.at[1]).wait()
    merged = strip[0]
    for place in range(1, n_xy):
        merged = merged + strip[place]
    slabs[gz] = merged

    def slab_copy(step):
        return pltpu.make_async_remote_copy(
            src_ref=slabs.at[gz], dst_ref=slabs.at[gz],
            send_sem=slab_sems.at[0], recv_sem=slab_sems.at[1],
            device_id=(lax.rem(gz + step, n_gz), xy), device_id_type=MESH,
        )

    @pl.loop(1, n_gz)
    def _(step):
        slab_copy(step).start()

    rest = slabs.at[pl.ds(0, n_gz - 1)]
    pltpu.make_async_copy(rest, rest, slab_sems.at[1]).wait()

    shape = (n_gz, LANES)
    lane = lax.broadcasted_iota(jnp.int32, shape, 1)
    row = lax.broadcasted_iota(jnp.int32, shape, 0)
    even = lane < 64

    def up(v):
        return pltpu.roll(v, n_gz - 1, axis=0)

    def down(v):
        return pltpu.roll(v, 1, axis=0)

    def lanes_on(v, by):
        return pltpu.roll(v, by % LANES, axis=1)

    def following(v):
        swapped = lanes_on(v, 64)
        return jnp.where(even, swapped, up(swapped))

    def preceding(v):
        swapped = lanes_on(v, 64)
        return jnp.where(even, down(swapped), swapped)

    last = row == n_gz - 1
    near_weight = slabs[:, 0, :]
    near_target = slabs[:, 1, :]
    far_weight = slabs[:, 2, :]
    far_target = slabs[:, 3, :]
    mark = slabs[:, 4, :]
    far_weight = jnp.where(even, far_weight, up(far_weight))
    far_target = jnp.where(even, far_target, up(far_target))
    near_weight = near_weight * mark * following(mark)
    far_weight = far_weight * mark * up(mark)
    near_weight = jnp.where(jnp.logical_and(last, jnp.logical_not(even)), 0.0, near_weight)
    far_weight = jnp.where(last, 0.0, far_weight)
    near_in = preceding(near_weight)
    far_in = down(far_weight)

    node = jnp.bitwise_and(lane, 31)
    col = jnp.bitwise_and(node, COLS - 1)
    nodes = NODES_DEV * n_xy
    has_right = jnp.where(col < COLS - 1, 1.0, 0.0)
    has_left = jnp.where(col > 0, 1.0, 0.0)
    has_below = jnp.where(node < nodes - COLS, 1.0, 0.0)
    has_above = jnp.where(node >= COLS, 1.0, 0.0)
    diagonal = (
        LAM + has_right + has_left + has_below + has_above
        + near_weight + near_in + far_weight + far_in
    )

    def operate(v):
        beside = (
            has_right * lanes_on(v, -1) + has_left * lanes_on(v, 1)
            + has_below * lanes_on(v, -COLS) + has_above * lanes_on(v, COLS)
        )
        along = near_weight * following(v) + near_in * preceding(v)
        along = along + far_weight * up(v) + far_in * down(v)
        return diagonal * v - beside - along

    swapped = lanes_on(near_target, 64)
    running = near_target + swapped
    by = 1
    while by < n_gz:
        running = running + jnp.where(row >= by, pltpu.roll(running, by, axis=0), 0.0)
        by *= 2
    entering = jnp.where(row >= 1, down(running), 0.0)
    initial = entering + jnp.where(even, 0.0, swapped)
    near_pull = near_weight * near_target
    far_pull = far_weight * far_target
    right_side = LAM * initial + preceding(near_pull) - near_pull + down(far_pull) - far_pull

    position = initial
    residual = right_side - operate(initial)
    direction = residual
    norm = total(residual * residual)
    for iteration in range(ITERS):
        image = operate(direction)
        step = norm / total(direction * image)
        position = position + step * direction
        residual = residual - step * image
        if iteration < ITERS - 1:
            norm_next = total(residual * residual)
            direction = residual + (norm_next / norm) * direction
            norm = norm_next

    final[0] = position
    final[1] = residual
    for place, out in ((0, positions_out), (1, residual_out)):
        own = pltpu.roll(
            final[place, pl.ds(gz, 1), :], lax.rem(LANES - NODES_DEV * xy, LANES), axis=1
        )
        for component in range(2):
            for parity in range(2):
                start = parity * 64 + component * 32
                out[component, parity : parity + 1, :] = own[:, start : start + NODES_DEV]

    @pl.loop(0, NODES_DEV)
    def _(node):
        spectrum_copy(0, node).wait_send()
        spectrum_copy(1, node).wait_send()

    pltpu.make_async_copy(others, others, strip_sems.at[0]).wait()
    pltpu.make_async_copy(rest, rest, slab_sems.at[0]).wait()


def per_device(n_gz, n_xy, patches, offsets, valid):
    vmem = pl.BlockSpec(memory_space=pltpu.VMEM)
    out = jax.ShapeDtypeStruct((2, 2, NODES_DEV), jnp.float32)
    f32, bf16 = jnp.float32, jnp.bfloat16
    return pl.pallas_call(
        functools.partial(kernel, n_gz, n_xy),
        out_shape=(out, out),
        in_specs=[pl.BlockSpec(memory_space=pl.ANY)] + [vmem] * 4,
        out_specs=(vmem, vmem),
        scratch_shapes=[
            pltpu.VMEM((SIZE, SIZE), bf16),
            pltpu.VMEM((SIZE, SIZE), bf16),
            pltpu.VMEM((3 * SIZE, SIZE), bf16),
            pltpu.VMEM((SIZE, 3 * SIZE), bf16),
            pltpu.VMEM((NODES_DEV, 2, SIZE, SIZE), bf16),
            pltpu.VMEM((4, NODES_DEV, 4, HALF, HALF), bf16),
            pltpu.VMEM((2, SIZE, 2 * SIZE), bf16),
            pltpu.VMEM((2, SIZE, SIZE), f32),
            pltpu.VMEM((SIZE, LANES), f32),
            pltpu.VMEM((4, NODES_DEV, 8, LANES), f32),
            pltpu.VMEM((4, NODES_DEV, 2, 8, LANES), f32),
            pltpu.VMEM((8, NODES_DEV, LANES), f32),
            pltpu.VMEM((2, NODES_DEV, LANES), f32),
            pltpu.VMEM((n_xy, 8, LANES), f32),
            pltpu.VMEM((n_gz, 8, LANES), f32),
            pltpu.VMEM((2, n_gz, LANES), f32),
            pltpu.SemaphoreType.DMA((2, NODES_DEV)),
            pltpu.SemaphoreType.DMA((2, NODES_DEV)),
            pltpu.SemaphoreType.DMA((2, NODES_DEV)),
            pltpu.SemaphoreType.DMA((2,)),
            pltpu.SemaphoreType.DMA((2,)),
            pltpu.SemaphoreType.DMA((2,)),
        ],
        compiler_params=pltpu.CompilerParams(
            collective_id=0, has_side_effects=True, vmem_limit_bytes=48 * 1024 * 1024
        ),
    )(patches, offsets, valid, *(jnp.asarray(table) for table in tables()))


def solution(mesh):
    return jax.shard_map(
        functools.partial(per_device, mesh.shape["gz"], mesh.shape["xy"]),
        mesh=mesh,
        in_specs=(P("gz", "xy", None, None), P(None, None, "gz", "xy"), P("gz", "xy")),
        out_specs=(P(None, "gz", "xy"), P(None, "gz", "xy")),
        check_vma=False,
    )
```

```python
import functools
import math

import jax
import jax.numpy as jnp
import numpy as np
from jax import lax
from jax.experimental import pallas as pl
from jax.experimental.pallas import tpu as pltpu
from jax.sharding import PartitionSpec as P

SIZE = 256
HALF = 128
NODES_DEV = 8
COLS = 8
ITERS = 3
LANES = 128
MESH = pl.DeviceIdType.MESH
LAM = 0.25


def tables():
    index = np.arange(SIZE)
    angles = ((index[:, None] * index[None, :]) % SIZE) * (2.0 * math.pi / SIZE)
    rows = np.concatenate([np.cos(angles)[:HALF], np.sin(angles)[:HALF]])
    rows[HALF] = np.cos(angles)[HALF]

    return rows.astype(np.float32), np.ascontiguousarray(rows.T).astype(np.float32)


def split(values):
    high = values.astype(jnp.bfloat16)
    low = (values - high.astype(jnp.float32)).astype(jnp.bfloat16)
    return high, low


def dot(left, right):
    return jnp.dot(left, right, preferred_element_type=jnp.float32)


def pack_spectrum(grid, rows, first):
    a = grid[rows, :HALF]
    c = grid[rows, HALF:]
    lower = slice(HALF + rows.start, HALF + rows.stop)
    d = grid[lower, :HALF]
    b = grid[lower, HALF:]
    col0 = lax.broadcasted_iota(jnp.int32, a.shape, 1) == 0
    plus_re = jnp.where(col0, a, a - b)
    plus_im = jnp.where(col0, d, c + d)
    minus_re = jnp.where(col0, c, a + b)
    minus_im = jnp.where(col0, b, c - d)
    if first:
        row0 = lax.broadcasted_iota(jnp.int32, a.shape, 0) == 0
        plus_re = jnp.where(row0, a, plus_re)
        plus_im = jnp.where(row0, c, plus_im)
        minus_re = jnp.where(row0, d, minus_re)
        minus_im = jnp.where(row0, b, minus_im)
    return plus_re, plus_im, minus_re, minus_im


def cross_terms(own, other, first):
    pr, pj, mr, mj = own
    qr, qj, nr, nj = other
    rr = pr * qr
    jj = pj * qj
    rp = rr + jj
    qp = pr * qj - pj * qr
    mrr = mr * nr
    mjj = mj * nj
    rm = mrr + mjj
    qm = mr * nj - mj * nr
    col0 = lax.broadcasted_iota(jnp.int32, pr.shape, 1) == 0
    cc = rp + jnp.where(col0, 0.0, rm)
    sc = qp - jnp.where(col0, 0.0, qm)
    cs = jnp.where(col0, rm, qp + qm)
    ss = jnp.where(col0, qm, rm - rp)
    if first:
        row0 = lax.broadcasted_iota(jnp.int32, pr.shape, 0) == 0
        corner = jnp.logical_and(row0, col0)
        cc = jnp.where(row0, jnp.where(corner, 0.5 * rr, rp), cc)
        cs = jnp.where(row0, jnp.where(corner, 0.5 * jj, qp), cs)
        sc = jnp.where(row0, jnp.where(corner, 0.5 * mrr, rm), sc)
        ss = jnp.where(row0, jnp.where(corner, 0.5 * mjj, qm), ss)
    return cc, cs, sc, ss


def to_column(row):
    count = NODES_DEV
    wide = jnp.broadcast_to(row, (count, count))
    diagonal = lax.broadcasted_iota(jnp.int32, (count, count), 0) == lax.broadcasted_iota(
        jnp.int32, (count, count), 1
    )
    return jnp.sum(jnp.where(diagonal, wide, 0.0), axis=1, keepdims=True)


def total(values):
    return jnp.sum(jnp.sum(values, axis=0, keepdims=True), axis=1, keepdims=True)


def kernel(
    n_gz, n_xy,
    patches, offsets_hbm, valid_hbm, rows_hbm, columns_hbm,
    positions_out, residual_out,
    offsets, valid, rows_table, columns_table, right_fwd, left_fwd, right_inv, left_inv, images, spec, mix, half_maps, maps, lag_rows, stats, nears, shifts, shifts_prior,
    strip, slabs, final,
    input_sems, image_sems, send_sems, recv_sems, shift_sems, strip_sems, slab_sems,
):
    gz = lax.axis_index("gz")
    xy = lax.axis_index("xy")
    after = lax.rem(gz + 1, n_gz)
    before = lax.rem(gz + n_gz - 1, n_gz)

    def image_copy(section, node):
        return pltpu.make_async_copy(
            patches.at[section, node], images.at[node, section], image_sems.at[section, node]
        )

    inputs = [
        pltpu.make_async_copy(source, target, input_sems.at[place])
        for place, (source, target) in enumerate(
            ((rows_hbm, rows_table), (columns_hbm, columns_table), (offsets_hbm, offsets),
             (valid_hbm, valid))
        )
    ]
    for copy in inputs[:2]:
        copy.start()

    @pl.loop(0, NODES_DEV)
    def _(node):
        image_copy(0, node).start()
        image_copy(1, node).start()

    for copy in inputs[2:]:
        copy.start()

    barrier = pltpu.get_barrier_semaphore()

    @pl.loop(1, n_gz)
    def _(step):
        pl.semaphore_signal(
            barrier, inc=1, device_id=(lax.rem(gz + step, n_gz), xy), device_id_type=MESH
        )

    @pl.loop(1, n_xy)
    def _(step):
        pl.semaphore_signal(
            barrier, inc=1, device_id=(gz, lax.rem(xy + step, n_xy)), device_id_type=MESH
        )

    for copy in inputs:
        copy.wait()

    left_fwd[...] = rows_table[...].astype(jnp.bfloat16)
    right_fwd[...] = columns_table[...].astype(jnp.bfloat16)
    high, low = split(rows_table[...])
    right_inv[...] = jnp.concatenate([high, high, low], axis=0)
    high, low = split(columns_table[...] * (2.0 / math.log(2.0) / float(SIZE) ** 3))
    left_inv[...] = jnp.concatenate([high, high, low], axis=1)

    lag = lax.rem(lax.broadcasted_iota(jnp.int32, (SIZE, LANES), 0) + HALF, SIZE) - HALF
    lag_rows[...] = lag.astype(jnp.float32)
    moves = offsets[...].astype(jnp.float32)
    for partner in range(2):
        for section in range(2):
            for component in range(2):
                column = to_column(moves[partner, component, section : section + 1, :])
                place = (partner * 2 + section) * 2 + component
                shifts[place] = jnp.broadcast_to(column, (NODES_DEV, LANES))

    def spectrum_copy(way, node):
        return pltpu.make_async_remote_copy(
            src_ref=spec.at[1 + way, node], dst_ref=spec.at[3 - 3 * way, node],
            send_sem=send_sems.at[way, node], recv_sem=recv_sems.at[way, node],
            device_id=((before, after)[way], xy), device_id_type=MESH,
        )

    def shift_copy():
        return pltpu.make_async_remote_copy(
            src_ref=shifts.at[pl.ds(6, 2)], dst_ref=shifts_prior,
            send_sem=shift_sems.at[0], recv_sem=shift_sems.at[1],
            device_id=(after, xy), device_id_type=MESH,
        )

    @pl.loop(0, NODES_DEV)
    def _(node):
        image_copy(0, node).wait()
        image_copy(1, node).wait()
        both = images[node].reshape(2 * SIZE, SIZE)
        rowwise = dot(both, right_fwd[...]).astype(jnp.bfloat16)
        for section in range(2):
            grid = dot(left_fwd[...], rowwise[section * SIZE : (section + 1) * SIZE])
            for rows, first in ((slice(0, 16), True), (slice(16, HALF), False)):
                parts = pack_spectrum(grid, rows, first)
                for part in range(4):
                    spec[section + 1, node, part, rows, :] = parts[part].astype(jnp.bfloat16)

        @pl.when(node == 0)
        def _():
            pl.semaphore_wait(barrier, n_gz + n_xy - 2)
            shift_copy().start()

        spectrum_copy(0, node).start()
        spectrum_copy(1, node).start()

    core = lax.rem(gz, 2)

    def plan(step):
        in_own = step < 4
        next_from = 4 + 4 * core
        in_next = jnp.logical_and(step >= next_from, step < next_from + 8)
        prior_from = 12 - 8 * core
        in_prior = jnp.logical_and(step >= prior_from, step < prior_from + 4)
        node_next = jnp.clip(step - next_from, 0, 7)
        node_pair = jnp.where(in_own, 2 * step, jnp.clip(2 * (step - prior_from), 0, 6))
        two = jnp.where(in_next, 3, 2)
        return (
            in_next,
            in_prior,
            (
                jnp.where(in_prior, 0, 1),
                two,
                jnp.where(in_next, node_next, node_pair),
                jnp.where(in_next, 2, jnp.where(in_prior, 3, 0)),
            ),
            (
                jnp.where(in_prior, 0, jnp.where(in_next, 2, 1)),
                two,
                jnp.where(in_next, node_next, node_pair + 1),
                jnp.where(in_next, 1, jnp.where(in_prior, 3, 0)),
            ),
        )

    def await_partners(step):
        in_next, in_prior, (_, _, node, _), (_, _, other, _) = plan(step)

        @pl.when(in_next)
        def _():
            spectrum_copy(0, node).wait_recv()

        @pl.when(in_prior)
        def _():
            spectrum_copy(1, node).wait_recv()
            spectrum_copy(1, other).wait_recv()

    def products(step):
        for slot, (one, two, node, _) in enumerate(plan(step)[2:]):
            for rows, first in ((slice(0, 16), True), (slice(16, HALF), False)):
                own = [spec[one, node, part, rows, :].astype(jnp.float32) for part in range(4)]
                other = [spec[two, node, part, rows, :].astype(jnp.float32) for part in range(4)]
                terms = cross_terms(own, other, first)
                lower = slice(HALF + rows.start, HALF + rows.stop)
                for part, (where, lanes) in enumerate(
                    ((rows, 0), (rows, HALF), (lower, 0), (lower, HALF))
                ):
                    high, low = split(terms[part])
                    mix[slot, where, lanes : lanes + HALF] = high
                    mix[slot, where, SIZE + lanes : SIZE + lanes + HALF] = low
        both = mix[...].reshape(2 * SIZE, 2 * SIZE)
        left = jnp.concatenate([both, both[:, :SIZE]], axis=1)
        high, low = split(dot(left, right_inv[...]))
        for slot in range(2):
            rows = slice(slot * SIZE, (slot + 1) * SIZE)
            half_maps[slot, :SIZE] = high[rows]
            half_maps[slot, SIZE:] = low[rows]

    def statistics(step):
        for slot, (_, _, node, group) in enumerate(plan(step)[2:]):
            right = jnp.concatenate([half_maps[slot], half_maps[slot, :SIZE]], axis=0)
            values = dot(left_inv[...], right)
            maps[slot] = values
            top = jnp.max(values, axis=(0, 1), keepdims=True)
            mass, moment, rim = [], [], []
            for side in range(2):
                raised = jnp.exp2(maps[slot, :, side * HALF : (side + 1) * HALF] - top)
                mass.append(jnp.sum(raised, axis=0, keepdims=True))
                moment.append(jnp.sum(raised * lag_rows[...], axis=0, keepdims=True))
                rim.append(raised[HALF - 8 : HALF + 8])
            rim = rim[0] + rim[1]
            stats[group, node] = jnp.concatenate([*mass, *moment, rim[6:10]], axis=0)
            low_lane = lax.broadcasted_iota(jnp.int32, (8, HALF), 1) < HALF // 2
            for place, start in ((0, 0), (1, SIZE - 8)):
                edge = maps[slot, start : start + 8, :]
                nears[group, node, place] = jnp.where(low_lane, edge[:, :HALF], edge[:, HALF:])

    steps = 16
    products(0)

    @pl.loop(1, steps)
    def _(step):
        await_partners(step)
        statistics(step - 1)
        products(step)

    statistics(steps - 1)

    shift_copy().wait()

    columns = lax.broadcasted_iota(jnp.int32, (NODES_DEV, HALF), 1)
    near_lane = jnp.where(columns < HALF // 2, columns, columns - HALF)
    weights = []
    targets = []
    for group, place in ((0, 0), (1, 2), (2, 4), (3, None)):
        if place is None:
            move_x, move_y = shifts_prior[0], shifts_prior[1]
        else:
            move_x, move_y = shifts[place], shifts[place + 1]
        move_x = move_x.astype(jnp.int32)
        move_y = move_y.astype(jnp.int32)
        whole = 0.0
        sum_x = 0.0
        for side in range(2):
            mass = stats[group, :, side, :]
            lag_x = jnp.bitwise_and(columns + side * HALF - move_x + HALF, SIZE - 1) - HALF + move_x
            whole = whole + mass
            sum_x = sum_x + mass * lag_x.astype(jnp.float32)
        sum_y = stats[group, :, 2, :] + stats[group, :, 3, :]
        for row in range(4):
            plain = HALF - 2 + row if row < 2 else row - 2 - HALF
            lag_y = jnp.bitwise_and(row - 2 - move_y, SIZE - 1) - HALF + move_y
            sum_y = sum_y + stats[group, :, 4 + row, :] * (lag_y - plain).astype(jnp.float32)
        picked = jnp.zeros((NODES_DEV, HALF), jnp.float32)
        for row in range(-2, 3):
            near = nears[group, :, 0 if row >= 0 else 1, row % 8, :]
            picked = picked + jnp.where(move_y == row, near, 0.0)
        picked = jnp.where(near_lane == move_x, picked, 0.0)
        whole = jnp.sum(whole, axis=1, keepdims=True)
        sum_x = jnp.sum(sum_x, axis=1, keepdims=True)
        sum_y = jnp.sum(sum_y, axis=1, keepdims=True)
        score = jnp.sum(picked, axis=1, keepdims=True) * math.log(2.0)
        weights.append(0.5 + 1.0 / (1.0 + jnp.exp(-score)))
        targets.append((sum_x / whole, sum_y / whole))

    lane = lax.broadcasted_iota(jnp.int32, (NODES_DEV, LANES), 1)
    node_lane = jnp.bitwise_and(lane, 31) == NODES_DEV * xy + lax.broadcasted_iota(
        jnp.int32, (NODES_DEV, LANES), 0
    )
    odd = lane >= 64
    second = jnp.bitwise_and(lane, 32) > 0

    def place_row(even_x, even_y, odd_x, odd_y):
        chosen = jnp.where(
            odd, jnp.where(second, odd_y, odd_x), jnp.where(second, even_y, even_x)
        )
        return jnp.sum(jnp.where(node_lane, chosen, 0.0), axis=0, keepdims=True)

    marks = valid[...].astype(jnp.float32)
    mark_even, mark_odd = to_column(marks[0:1, :]), to_column(marks[1:2, :])
    strip[xy] = jnp.concatenate(
        [
            place_row(weights[0], weights[0], weights[1], weights[1]),
            place_row(*targets[0], *targets[1]),
            place_row(weights[2], weights[2], weights[3], weights[3]),
            place_row(*targets[2], *targets[3]),
            place_row(mark_even, mark_even, mark_odd, mark_odd),
            jnp.zeros((3, LANES), jnp.float32),
        ],
        axis=0,
    )

    def strip_copy(step):
        return pltpu.make_async_remote_copy(
            src_ref=strip.at[xy], dst_ref=strip.at[xy],
            send_sem=strip_sems.at[0], recv_sem=strip_sems.at[1],
            device_id=(gz, lax.rem(xy + step, n_xy)), device_id_type=MESH,
        )

    @pl.loop(1, n_xy)
    def _(step):
        strip_copy(step).start()

    others = strip.at[pl.ds(0, n_xy - 1)]
    pltpu.make_async_copy(others, others, strip_sems.at[1]).wait()
    merged = strip[0]
    for place in range(1, n_xy):
        merged = merged + strip[place]
    slabs[gz] = merged

    def slab_copy(step):
        return pltpu.make_async_remote_copy(
            src_ref=slabs.at[gz], dst_ref=slabs.at[gz],
            send_sem=slab_sems.at[0], recv_sem=slab_sems.at[1],
            device_id=(lax.rem(gz + step, n_gz), xy), device_id_type=MESH,
        )

    @pl.loop(1, n_gz)
    def _(step):
        slab_copy(step).start()

    rest = slabs.at[pl.ds(0, n_gz - 1)]
    pltpu.make_async_copy(rest, rest, slab_sems.at[1]).wait()

    shape = (n_gz, LANES)
    lane = lax.broadcasted_iota(jnp.int32, shape, 1)
    row = lax.broadcasted_iota(jnp.int32, shape, 0)
    even = lane < 64

    def up(v):
        return pltpu.roll(v, n_gz - 1, axis=0)

    def down(v):
        return pltpu.roll(v, 1, axis=0)

    def lanes_on(v, by):
        return pltpu.roll(v, by % LANES, axis=1)

    def following(v):
        swapped = lanes_on(v, 64)
        return jnp.where(even, swapped, up(swapped))

    def preceding(v):
        swapped = lanes_on(v, 64)
        return jnp.where(even, down(swapped), swapped)

    last = row == n_gz - 1
    near_weight = slabs[:, 0, :]
    near_target = slabs[:, 1, :]
    far_weight = slabs[:, 2, :]
    far_target = slabs[:, 3, :]
    mark = slabs[:, 4, :]
    far_weight = jnp.where(even, far_weight, up(far_weight))
    far_target = jnp.where(even, far_target, up(far_target))
    near_weight = near_weight * mark * following(mark)
    far_weight = far_weight * mark * up(mark)
    near_weight = jnp.where(jnp.logical_and(last, jnp.logical_not(even)), 0.0, near_weight)
    far_weight = jnp.where(last, 0.0, far_weight)
    near_in = preceding(near_weight)
    far_in = down(far_weight)

    node = jnp.bitwise_and(lane, 31)
    col = jnp.bitwise_and(node, COLS - 1)
    nodes = NODES_DEV * n_xy
    has_right = jnp.where(col < COLS - 1, 1.0, 0.0)
    has_left = jnp.where(col > 0, 1.0, 0.0)
    has_below = jnp.where(node < nodes - COLS, 1.0, 0.0)
    has_above = jnp.where(node >= COLS, 1.0, 0.0)
    diagonal = (
        LAM + has_right + has_left + has_below + has_above
        + near_weight + near_in + far_weight + far_in
    )

    def operate(v):
        beside = (
            has_right * lanes_on(v, -1) + has_left * lanes_on(v, 1)
            + has_below * lanes_on(v, -COLS) + has_above * lanes_on(v, COLS)
        )
        along = near_weight * following(v) + near_in * preceding(v)
        along = along + far_weight * up(v) + far_in * down(v)
        return diagonal * v - beside - along

    swapped = lanes_on(near_target, 64)
    running = near_target + swapped
    by = 1
    while by < n_gz:
        running = running + jnp.where(row >= by, pltpu.roll(running, by, axis=0), 0.0)
        by *= 2
    entering = jnp.where(row >= 1, down(running), 0.0)
    initial = entering + jnp.where(even, 0.0, swapped)
    near_pull = near_weight * near_target
    far_pull = far_weight * far_target
    right_side = LAM * initial + preceding(near_pull) - near_pull + down(far_pull) - far_pull

    position = initial
    residual = right_side - operate(initial)
    direction = residual
    norm = total(residual * residual)
    for iteration in range(ITERS):
        image = operate(direction)
        step = norm / total(direction * image)
        position = position + step * direction
        residual = residual - step * image
        if iteration < ITERS - 1:
            norm_next = total(residual * residual)
            direction = residual + (norm_next / norm) * direction
            norm = norm_next

    final[0] = position
    final[1] = residual
    for place, out in ((0, positions_out), (1, residual_out)):
        own = pltpu.roll(
            final[place, pl.ds(gz, 1), :], lax.rem(LANES - NODES_DEV * xy, LANES), axis=1
        )
        for component in range(2):
            for parity in range(2):
                start = parity * 64 + component * 32
                out[component, parity : parity + 1, :] = own[:, start : start + NODES_DEV]

    @pl.loop(0, NODES_DEV)
    def _(node):
        spectrum_copy(0, node).wait_send()
        spectrum_copy(1, node).wait_send()

    pltpu.make_async_copy(others, others, strip_sems.at[0]).wait()
    pltpu.make_async_copy(rest, rest, slab_sems.at[0]).wait()


def per_device(n_gz, n_xy, patches, offsets, valid):
    vmem = pl.BlockSpec(memory_space=pltpu.VMEM)
    out = jax.ShapeDtypeStruct((2, 2, NODES_DEV), jnp.float32)
    f32, bf16 = jnp.float32, jnp.bfloat16
    return pl.pallas_call(
        functools.partial(kernel, n_gz, n_xy),
        out_shape=(out, out),
        in_specs=[pl.BlockSpec(memory_space=pltpu.HBM)] * 5,
        out_specs=(vmem, vmem),
        scratch_shapes=[
            pltpu.VMEM((2, 2, 2, NODES_DEV), jnp.int32),
            pltpu.VMEM((2, NODES_DEV), jnp.int32),
            pltpu.VMEM((SIZE, SIZE), f32),
            pltpu.VMEM((SIZE, SIZE), f32),
            pltpu.VMEM((SIZE, SIZE), bf16),
            pltpu.VMEM((SIZE, SIZE), bf16),
            pltpu.VMEM((3 * SIZE, SIZE), bf16),
            pltpu.VMEM((SIZE, 3 * SIZE), bf16),
            pltpu.VMEM((NODES_DEV, 2, SIZE, SIZE), bf16),
            pltpu.VMEM((4, NODES_DEV, 4, HALF, HALF), bf16),
            pltpu.VMEM((2, SIZE, 2 * SIZE), bf16),
            pltpu.VMEM((2, 2 * SIZE, SIZE), bf16),
            pltpu.VMEM((2, SIZE, SIZE), f32),
            pltpu.VMEM((SIZE, LANES), f32),
            pltpu.VMEM((4, NODES_DEV, 8, LANES), f32),
            pltpu.VMEM((4, NODES_DEV, 2, 8, LANES), f32),
            pltpu.VMEM((8, NODES_DEV, LANES), f32),
            pltpu.VMEM((2, NODES_DEV, LANES), f32),
            pltpu.VMEM((n_xy, 8, LANES), f32),
            pltpu.VMEM((n_gz, 8, LANES), f32),
            pltpu.VMEM((2, n_gz, LANES), f32),
            pltpu.SemaphoreType.DMA((4,)),
            pltpu.SemaphoreType.DMA((2, NODES_DEV)),
            pltpu.SemaphoreType.DMA((2, NODES_DEV)),
            pltpu.SemaphoreType.DMA((2, NODES_DEV)),
            pltpu.SemaphoreType.DMA((2,)),
            pltpu.SemaphoreType.DMA((2,)),
            pltpu.SemaphoreType.DMA((2,)),
        ],
        compiler_params=pltpu.CompilerParams(
            collective_id=0, has_side_effects=True, vmem_limit_bytes=60 * 1024 * 1024
        ),
    )(patches, offsets, valid, *(jnp.asarray(table) for table in tables()))


def solution(mesh):
    return jax.shard_map(
        functools.partial(per_device, mesh.shape["gz"], mesh.shape["xy"]),
        mesh=mesh,
        in_specs=(P("gz", "xy", None, None), P(None, None, "gz", "xy"), P("gz", "xy")),
        out_specs=(P(None, "gz", "xy"), P(None, "gz", "xy")),
        check_vma=False,
    )
```

```python
import functools
import math

import jax
import jax.numpy as jnp
import numpy as np
from jax import lax
from jax.experimental import pallas as pl
from jax.experimental.pallas import tpu as pltpu
from jax.sharding import PartitionSpec as P

SIZE = 256
HALF = 128
NODES_DEV = 8
COLS = 8
ITERS = 3
LANES = 128
MESH = pl.DeviceIdType.MESH
LAM = 0.25


def tables():
    index = np.arange(SIZE)
    angles = ((index[:, None] * index[None, :]) % SIZE) * (2.0 * math.pi / SIZE)
    rows = np.concatenate([np.cos(angles)[:HALF], np.sin(angles)[:HALF]])
    rows[HALF] = np.cos(angles)[HALF]

    return rows.astype(np.float32), np.ascontiguousarray(rows.T).astype(np.float32)


def split(values):
    high = values.astype(jnp.bfloat16)
    low = (values - high.astype(jnp.float32)).astype(jnp.bfloat16)
    return high, low


def dot(left, right):
    return jnp.dot(left, right, preferred_element_type=jnp.float32)


def pack_spectrum(grid, rows, first):
    a = grid[rows, :HALF]
    c = grid[rows, HALF:]
    lower = slice(HALF + rows.start, HALF + rows.stop)
    d = grid[lower, :HALF]
    b = grid[lower, HALF:]
    col0 = lax.broadcasted_iota(jnp.int32, a.shape, 1) == 0
    plus_re = jnp.where(col0, a, a - b)
    plus_im = jnp.where(col0, d, c + d)
    minus_re = jnp.where(col0, c, a + b)
    minus_im = jnp.where(col0, b, c - d)
    if first:
        row0 = lax.broadcasted_iota(jnp.int32, a.shape, 0) == 0
        plus_re = jnp.where(row0, a, plus_re)
        plus_im = jnp.where(row0, c, plus_im)
        minus_re = jnp.where(row0, d, minus_re)
        minus_im = jnp.where(row0, b, minus_im)
    return plus_re, plus_im, minus_re, minus_im


def cross_terms(own, other, first):
    pr, pj, mr, mj = own
    qr, qj, nr, nj = other
    rr = pr * qr
    jj = pj * qj
    rp = rr + jj
    qp = pr * qj - pj * qr
    mrr = mr * nr
    mjj = mj * nj
    rm = mrr + mjj
    qm = mr * nj - mj * nr
    col0 = lax.broadcasted_iota(jnp.int32, pr.shape, 1) == 0
    cc = rp + jnp.where(col0, 0.0, rm)
    sc = qp - jnp.where(col0, 0.0, qm)
    cs = jnp.where(col0, rm, qp + qm)
    ss = jnp.where(col0, qm, rm - rp)
    if first:
        row0 = lax.broadcasted_iota(jnp.int32, pr.shape, 0) == 0
        corner = jnp.logical_and(row0, col0)
        cc = jnp.where(row0, jnp.where(corner, 0.5 * rr, rp), cc)
        cs = jnp.where(row0, jnp.where(corner, 0.5 * jj, qp), cs)
        sc = jnp.where(row0, jnp.where(corner, 0.5 * mrr, rm), sc)
        ss = jnp.where(row0, jnp.where(corner, 0.5 * mjj, qm), ss)
    return cc, cs, sc, ss


def to_column(row):
    count = NODES_DEV
    wide = jnp.broadcast_to(row, (count, count))
    diagonal = lax.broadcasted_iota(jnp.int32, (count, count), 0) == lax.broadcasted_iota(
        jnp.int32, (count, count), 1
    )
    return jnp.sum(jnp.where(diagonal, wide, 0.0), axis=1, keepdims=True)


def total(values):
    return jnp.sum(jnp.sum(values, axis=0, keepdims=True), axis=1, keepdims=True)


def kernel(
    n_gz, n_xy,
    patches, offsets_hbm, valid_hbm, rows_hbm, columns_hbm,
    solved,
    offsets, valid, rows_table, columns_table, right_fwd, left_fwd, right_inv, left_inv, images, spec, mix, half_maps, maps, lag_rows, stats, nears, shifts, shifts_prior,
    own_row, all_rows, final,
    input_sems, image_sems, send_sems, recv_sems, shift_sems, row_sems, ready,
):
    gz = lax.axis_index("gz")
    xy = lax.axis_index("xy")
    after = lax.rem(gz + 1, n_gz)
    before = lax.rem(gz + n_gz - 1, n_gz)

    def image_copy(section, node):
        return pltpu.make_async_copy(
            patches.at[section, node], images.at[node, section], image_sems.at[section, node]
        )

    inputs = [
        pltpu.make_async_copy(source, target, input_sems.at[place])
        for place, (source, target) in enumerate(
            ((rows_hbm, rows_table), (columns_hbm, columns_table), (offsets_hbm, offsets),
             (valid_hbm, valid))
        )
    ]
    for copy in inputs[:2]:
        copy.start()

    @pl.loop(0, NODES_DEV)
    def _(node):
        image_copy(0, node).start()
        image_copy(1, node).start()

    for copy in inputs[2:]:
        copy.start()

    barrier = pltpu.get_barrier_semaphore()

    me = xy * n_gz + gz
    count = n_gz * n_xy

    row_start = gz - jnp.bitwise_and(gz, 7)
    row_peers = [row_start + jnp.bitwise_and(gz + step, 7) for step in range(1, 8)]
    column_peers = [(jnp.bitwise_and(gz + 8 * step, n_gz - 1), xy) for step in range(1, 4)]
    line_peers = [(gz, jnp.bitwise_and(xy + step, n_xy - 1)) for step in range(1, 4)]
    greeted = [(before, xy), (after, xy)] + [(peer, xy) for peer in row_peers]
    greeted = greeted + column_peers + line_peers
    for peer in greeted:
        pl.semaphore_signal(barrier, inc=1, device_id=peer, device_id_type=MESH)

    for copy in inputs:
        copy.wait()

    left_fwd[...] = rows_table[...].astype(jnp.bfloat16)
    right_fwd[...] = columns_table[...].astype(jnp.bfloat16)
    high, low = split(rows_table[...])
    right_inv[...] = jnp.concatenate([high, high, low], axis=0)
    high, low = split(columns_table[...] * (2.0 / math.log(2.0) / float(SIZE) ** 3))
    left_inv[...] = jnp.concatenate([high, high, low], axis=1)

    lag = lax.rem(lax.broadcasted_iota(jnp.int32, (SIZE, LANES), 0) + HALF, SIZE) - HALF
    lag_rows[...] = lag.astype(jnp.float32)
    moves = offsets[...].astype(jnp.float32)
    for partner in range(2):
        for section in range(2):
            for component in range(2):
                column = to_column(moves[partner, component, section : section + 1, :])
                place = (partner * 2 + section) * 2 + component
                shifts[place] = jnp.broadcast_to(column, (NODES_DEV, LANES))

    def spectrum_copy(way, node):
        return pltpu.make_async_remote_copy(
            src_ref=spec.at[1 + way, node], dst_ref=spec.at[3 - 3 * way, node],
            send_sem=send_sems.at[way, node], recv_sem=recv_sems.at[way, node],
            device_id=((before, after)[way], xy), device_id_type=MESH,
        )

    def shift_copy():
        return pltpu.make_async_remote_copy(
            src_ref=shifts.at[pl.ds(6, 2)], dst_ref=shifts_prior,
            send_sem=shift_sems.at[0], recv_sem=shift_sems.at[1],
            device_id=(after, xy), device_id_type=MESH,
        )

    @pl.loop(0, NODES_DEV)
    def _(node):
        image_copy(0, node).wait()
        image_copy(1, node).wait()
        both = images[node].reshape(2 * SIZE, SIZE)
        rowwise = dot(both, right_fwd[...]).astype(jnp.bfloat16)
        for section in range(2):
            grid = dot(left_fwd[...], rowwise[section * SIZE : (section + 1) * SIZE])
            for rows, first in ((slice(0, 16), True), (slice(16, HALF), False)):
                parts = pack_spectrum(grid, rows, first)
                for part in range(4):
                    spec[section + 1, node, part, rows, :] = parts[part].astype(jnp.bfloat16)

        @pl.when(node == 0)
        def _():
            pl.semaphore_wait(barrier, len(greeted))
            for peer in column_peers:
                pl.semaphore_signal(ready.at[0], inc=1, device_id=peer, device_id_type=MESH)
            shift_copy().start()

        spectrum_copy(0, node).start()
        spectrum_copy(1, node).start()

    core = lax.rem(gz, 2)

    def plan(step):
        in_own = step < 4
        next_from = 4 + 4 * core
        in_next = jnp.logical_and(step >= next_from, step < next_from + 8)
        prior_from = 12 - 8 * core
        in_prior = jnp.logical_and(step >= prior_from, step < prior_from + 4)
        node_next = jnp.clip(step - next_from, 0, 7)
        node_pair = jnp.where(in_own, 2 * step, jnp.clip(2 * (step - prior_from), 0, 6))
        two = jnp.where(in_next, 3, 2)
        return (
            in_next,
            in_prior,
            (
                jnp.where(in_prior, 0, 1),
                two,
                jnp.where(in_next, node_next, node_pair),
                jnp.where(in_next, 2, jnp.where(in_prior, 3, 0)),
            ),
            (
                jnp.where(in_prior, 0, jnp.where(in_next, 2, 1)),
                two,
                jnp.where(in_next, node_next, node_pair + 1),
                jnp.where(in_next, 1, jnp.where(in_prior, 3, 0)),
            ),
        )

    def await_partners(step):
        in_next, in_prior, (_, _, node, _), (_, _, other, _) = plan(step)

        @pl.when(in_next)
        def _():
            spectrum_copy(0, node).wait_recv()

        @pl.when(in_prior)
        def _():
            spectrum_copy(1, node).wait_recv()
            spectrum_copy(1, other).wait_recv()

    def products(step):
        for slot, (one, two, node, _) in enumerate(plan(step)[2:]):
            for rows, first in ((slice(0, 16), True), (slice(16, HALF), False)):
                own = [spec[one, node, part, rows, :].astype(jnp.float32) for part in range(4)]
                other = [spec[two, node, part, rows, :].astype(jnp.float32) for part in range(4)]
                terms = cross_terms(own, other, first)
                lower = slice(HALF + rows.start, HALF + rows.stop)
                for part, (where, lanes) in enumerate(
                    ((rows, 0), (rows, HALF), (lower, 0), (lower, HALF))
                ):
                    high, low = split(terms[part])
                    mix[slot, where, lanes : lanes + HALF] = high
                    mix[slot, where, SIZE + lanes : SIZE + lanes + HALF] = low
        both = mix[...].reshape(2 * SIZE, 2 * SIZE)
        left = jnp.concatenate([both, both[:, :SIZE]], axis=1)
        high, low = split(dot(left, right_inv[...]))
        for slot in range(2):
            rows = slice(slot * SIZE, (slot + 1) * SIZE)
            half_maps[slot, :SIZE] = high[rows]
            half_maps[slot, SIZE:] = low[rows]

    def statistics(step):
        for slot, (_, _, node, group) in enumerate(plan(step)[2:]):
            right = jnp.concatenate([half_maps[slot], half_maps[slot, :SIZE]], axis=0)
            values = dot(left_inv[...], right)
            maps[slot] = values
            top = jnp.max(values, axis=(0, 1), keepdims=True)
            mass, moment, rim = [], [], []
            for side in range(2):
                raised = jnp.exp2(maps[slot, :, side * HALF : (side + 1) * HALF] - top)
                mass.append(jnp.sum(raised, axis=0, keepdims=True))
                moment.append(jnp.sum(raised * lag_rows[...], axis=0, keepdims=True))
                rim.append(raised[HALF - 8 : HALF + 8])
            rim = rim[0] + rim[1]
            stats[group, node] = jnp.concatenate([*mass, *moment, rim[6:10]], axis=0)
            low_lane = lax.broadcasted_iota(jnp.int32, (8, HALF), 1) < HALF // 2
            for place, start in ((0, 0), (1, SIZE - 8)):
                edge = maps[slot, start : start + 8, :]
                nears[group, node, place] = jnp.where(low_lane, edge[:, :HALF], edge[:, HALF:])

    steps = 16
    products(0)

    @pl.loop(1, steps)
    def _(step):
        await_partners(step)

        @pl.when(step == 6)
        def _():
            pl.semaphore_wait(ready.at[0], len(column_peers))
            for peer in line_peers:
                pl.semaphore_signal(ready.at[1], inc=1, device_id=peer, device_id_type=MESH)

        statistics(step - 1)
        products(step)

    statistics(steps - 1)

    shift_copy().wait()

    columns = lax.broadcasted_iota(jnp.int32, (NODES_DEV, HALF), 1)
    near_lane = jnp.where(columns < HALF // 2, columns, columns - HALF)
    weights = []
    targets = []
    for group, place in ((0, 0), (1, 2), (2, 4), (3, None)):
        if place is None:
            move_x, move_y = shifts_prior[0], shifts_prior[1]
        else:
            move_x, move_y = shifts[place], shifts[place + 1]
        move_x = move_x.astype(jnp.int32)
        move_y = move_y.astype(jnp.int32)
        whole = 0.0
        sum_x = 0.0
        for side in range(2):
            mass = stats[group, :, side, :]
            lag_x = jnp.bitwise_and(columns + side * HALF - move_x + HALF, SIZE - 1) - HALF + move_x
            whole = whole + mass
            sum_x = sum_x + mass * lag_x.astype(jnp.float32)
        sum_y = stats[group, :, 2, :] + stats[group, :, 3, :]
        for row in range(4):
            plain = HALF - 2 + row if row < 2 else row - 2 - HALF
            lag_y = jnp.bitwise_and(row - 2 - move_y, SIZE - 1) - HALF + move_y
            sum_y = sum_y + stats[group, :, 4 + row, :] * (lag_y - plain).astype(jnp.float32)
        picked = jnp.zeros((NODES_DEV, HALF), jnp.float32)
        for row in range(-2, 3):
            near = nears[group, :, 0 if row >= 0 else 1, row % 8, :]
            picked = picked + jnp.where(move_y == row, near, 0.0)
        picked = jnp.where(near_lane == move_x, picked, 0.0)
        whole = jnp.sum(whole, axis=1, keepdims=True)
        sum_x = jnp.sum(sum_x, axis=1, keepdims=True)
        sum_y = jnp.sum(sum_y, axis=1, keepdims=True)
        score = jnp.sum(picked, axis=1, keepdims=True) * math.log(2.0)
        weights.append(0.5 + 1.0 / (1.0 + jnp.exp(-score)))
        targets.append((sum_x / whole, sum_y / whole))

    lane = lax.broadcasted_iota(jnp.int32, (NODES_DEV, LANES), 1)
    node_lane = jnp.bitwise_and(lane, 31) == lax.broadcasted_iota(
        jnp.int32, (NODES_DEV, LANES), 0
    )
    odd = lane >= 64
    second = jnp.bitwise_and(lane, 32) > 0

    def place_row(even_x, even_y, odd_x, odd_y):
        chosen = jnp.where(
            odd, jnp.where(second, odd_y, odd_x), jnp.where(second, even_y, even_x)
        )
        return jnp.sum(jnp.where(node_lane, chosen, 0.0), axis=0, keepdims=True)

    marks = valid[...].astype(jnp.float32)
    mark_even, mark_odd = to_column(marks[0:1, :]), to_column(marks[1:2, :])
    row_w = place_row(weights[0], mark_even, weights[1], mark_odd)
    row_t = place_row(*targets[0], *targets[1])
    row_v = place_row(weights[2], weights[2], weights[3], weights[3])
    row_u = place_row(*targets[2], *targets[3])
    row = row_w + pltpu.roll(row_t, 8, axis=1)
    row = row + pltpu.roll(row_v, 16, axis=1) + pltpu.roll(row_u, 24, axis=1)
    own_row[...] = jnp.broadcast_to(row, (8, LANES))

    me = xy * n_gz + gz
    count = n_gz * n_xy
    pl.semaphore_wait(ready.at[1], len(line_peers))
    mine = pltpu.make_async_copy(own_row.at[0:1], all_rows.at[pl.ds(me, 1)], row_sems.at[2])
    mine.start()

    to_z = [jnp.bitwise_and(xy + step, 3) for step in range(4)]
    to_y = [jnp.bitwise_and(gz + 8 * step, 24) for step in range(4)]
    to_x = [jnp.bitwise_and(gz + 2 * step, 6) for step in range(4)]
    to_core = [core, 1 - core]
    hops = (0, 1, 2, 1)
    ways = [(z, y, x, c) for z in range(4) for y in range(4) for x in range(4) for c in range(2)]
    ways.sort(key=lambda way: -hops[way[0]] - hops[way[1]] - hops[way[2]])
    for z, y, x, c in ways:
        if (z, y, x, c) == (0, 0, 0, 0):
            continue
        pltpu.make_async_remote_copy(
            src_ref=own_row.at[0:1], dst_ref=all_rows.at[pl.ds(me, 1)],
            send_sem=row_sems.at[0], recv_sem=row_sems.at[1],
            device_id=(to_y[y] + to_x[x] + to_core[c], to_z[z]), device_id_type=MESH,
        ).start()

    rest = all_rows.at[pl.ds(0, count - 1)]
    mine.wait()
    pltpu.make_async_copy(rest, rest, row_sems.at[1]).wait()

    shape = (n_gz, LANES)
    lane = lax.broadcasted_iota(jnp.int32, shape, 1)
    row = lax.broadcasted_iota(jnp.int32, shape, 0)
    even = lane < 64

    def up(v):
        return pltpu.roll(v, n_gz - 1, axis=0)

    def down(v):
        return pltpu.roll(v, 1, axis=0)

    def lanes_on(v, by):
        return pltpu.roll(v, by % LANES, axis=1)

    def following(v):
        swapped = lanes_on(v, 64)
        return jnp.where(even, swapped, up(swapped))

    def preceding(v):
        swapped = lanes_on(v, 64)
        return jnp.where(even, down(swapped), swapped)

    last = row == n_gz - 1
    window = jnp.bitwise_and(lane, 31) // NODES_DEV
    fields = [0.0] * 4
    for strip in range(n_xy):
        block = all_rows[strip * n_gz : (strip + 1) * n_gz, :]
        for field in range(4):
            moved = lanes_on(block, NODES_DEV * (strip - field)) if strip != field else block
            fields[field] = jnp.where(window == strip, moved, fields[field])
    marked, near_target, far_weight, far_target = fields
    first_part = jnp.bitwise_and(lane, 32) == 0
    near_weight = jnp.where(first_part, marked, lanes_on(marked, 32))
    mark = jnp.where(first_part, lanes_on(marked, -32), marked)
    far_weight = jnp.where(even, far_weight, up(far_weight))
    far_target = jnp.where(even, far_target, up(far_target))
    near_weight = near_weight * mark * following(mark)
    far_weight = far_weight * mark * up(mark)
    near_weight = jnp.where(jnp.logical_and(last, jnp.logical_not(even)), 0.0, near_weight)
    far_weight = jnp.where(last, 0.0, far_weight)
    near_in = preceding(near_weight)
    far_in = down(far_weight)

    node = jnp.bitwise_and(lane, 31)
    col = jnp.bitwise_and(node, COLS - 1)
    nodes = NODES_DEV * n_xy
    has_right = jnp.where(col < COLS - 1, 1.0, 0.0)
    has_left = jnp.where(col > 0, 1.0, 0.0)
    has_below = jnp.where(node < nodes - COLS, 1.0, 0.0)
    has_above = jnp.where(node >= COLS, 1.0, 0.0)
    diagonal = (
        LAM + has_right + has_left + has_below + has_above
        + near_weight + near_in + far_weight + far_in
    )

    def operate(v):
        beside = (
            has_right * lanes_on(v, -1) + has_left * lanes_on(v, 1)
            + has_below * lanes_on(v, -COLS) + has_above * lanes_on(v, COLS)
        )
        along = near_weight * following(v) + near_in * preceding(v)
        along = along + far_weight * up(v) + far_in * down(v)
        return diagonal * v - beside - along

    swapped = lanes_on(near_target, 64)
    running = near_target + swapped
    by = 1
    while by < n_gz:
        running = running + jnp.where(row >= by, pltpu.roll(running, by, axis=0), 0.0)
        by *= 2
    entering = jnp.where(row >= 1, down(running), 0.0)
    initial = entering + jnp.where(even, 0.0, swapped)
    near_pull = near_weight * near_target
    far_pull = far_weight * far_target
    right_side = LAM * initial + preceding(near_pull) - near_pull + down(far_pull) - far_pull

    position = initial
    residual = right_side - operate(initial)
    direction = residual
    norm = total(residual * residual)
    for iteration in range(ITERS):
        image = operate(direction)
        step = norm / total(direction * image)
        position = position + step * direction
        residual = residual - step * image
        if iteration < ITERS - 1:
            norm_next = total(residual * residual)
            direction = residual + (norm_next / norm) * direction
            norm = norm_next

    final[0] = position
    final[1] = residual
    for place in range(2):
        own = pltpu.roll(
            final[place, pl.ds(gz, 1), :], lax.rem(LANES - NODES_DEV * xy, LANES), axis=1
        )
        for component in range(2):
            for parity in range(2):
                start = parity * 64 + component * 32
                solved[place, component, parity : parity + 1, :] = own[:, start : start + NODES_DEV]

    @pl.loop(0, NODES_DEV)
    def _(node):
        spectrum_copy(0, node).wait_send()
        spectrum_copy(1, node).wait_send()

    pltpu.make_async_copy(rest, rest, row_sems.at[0]).wait()


def per_device(n_gz, n_xy, patches, offsets, valid):
    vmem = pl.BlockSpec(memory_space=pltpu.VMEM)
    out = jax.ShapeDtypeStruct((2, 2, 2, NODES_DEV), jnp.float32)
    f32, bf16 = jnp.float32, jnp.bfloat16
    both = pl.pallas_call(
        functools.partial(kernel, n_gz, n_xy),
        out_shape=out,
        in_specs=[pl.BlockSpec(memory_space=pltpu.HBM)] * 5,
        out_specs=vmem,
        scratch_shapes=[
            pltpu.VMEM((2, 2, 2, NODES_DEV), jnp.int32),
            pltpu.VMEM((2, NODES_DEV), jnp.int32),
            pltpu.VMEM((SIZE, SIZE), f32),
            pltpu.VMEM((SIZE, SIZE), f32),
            pltpu.VMEM((SIZE, SIZE), bf16),
            pltpu.VMEM((SIZE, SIZE), bf16),
            pltpu.VMEM((3 * SIZE, SIZE), bf16),
            pltpu.VMEM((SIZE, 3 * SIZE), bf16),
            pltpu.VMEM((NODES_DEV, 2, SIZE, SIZE), bf16),
            pltpu.VMEM((4, NODES_DEV, 4, HALF, HALF), bf16),
            pltpu.VMEM((2, SIZE, 2 * SIZE), bf16),
            pltpu.VMEM((2, 2 * SIZE, SIZE), bf16),
            pltpu.VMEM((2, SIZE, SIZE), f32),
            pltpu.VMEM((SIZE, LANES), f32),
            pltpu.VMEM((4, NODES_DEV, 8, LANES), f32),
            pltpu.VMEM((4, NODES_DEV, 2, 8, LANES), f32),
            pltpu.VMEM((8, NODES_DEV, LANES), f32),
            pltpu.VMEM((2, NODES_DEV, LANES), f32),
            pltpu.VMEM((8, LANES), f32),
            pltpu.VMEM((n_gz * n_xy, LANES), f32),
            pltpu.VMEM((2, n_gz, LANES), f32),
            pltpu.SemaphoreType.DMA((4,)),
            pltpu.SemaphoreType.DMA((2, NODES_DEV)),
            pltpu.SemaphoreType.DMA((2, NODES_DEV)),
            pltpu.SemaphoreType.DMA((2, NODES_DEV)),
            pltpu.SemaphoreType.DMA((2,)),
            pltpu.SemaphoreType.DMA((3,)),
            pltpu.SemaphoreType.REGULAR((2,)),
        ],
        compiler_params=pltpu.CompilerParams(
            collective_id=0, has_side_effects=True, vmem_limit_bytes=60 * 1024 * 1024
        ),
    )(patches, offsets, valid, *(jnp.asarray(table) for table in tables()))
    return both[0], both[1]


def solution(mesh):
    return jax.shard_map(
        functools.partial(per_device, mesh.shape["gz"], mesh.shape["xy"]),
        mesh=mesh,
        in_specs=(P("gz", "xy", None, None), P(None, None, "gz", "xy"), P("gz", "xy")),
        out_specs=(P(None, "gz", "xy"), P(None, "gz", "xy")),
        check_vma=False,
    )
```

```python
import functools
import math

import jax
import jax.numpy as jnp
import numpy as np
from jax import lax
from jax.experimental import pallas as pl
from jax.experimental.pallas import tpu as pltpu
from jax.sharding import PartitionSpec as P

SIZE = 256
HALF = 128
NODES_DEV = 8
COLS = 8
ITERS = 3
LANES = 128
MESH = pl.DeviceIdType.MESH
LAM = 0.25


def tables():
    index = np.arange(SIZE)
    angles = ((index[:, None] * index[None, :]) % SIZE) * (2.0 * math.pi / SIZE)
    rows = np.concatenate([np.cos(angles)[:HALF], np.sin(angles)[:HALF]])
    rows[HALF] = np.cos(angles)[HALF]

    return rows.astype(np.float32), np.ascontiguousarray(rows.T).astype(np.float32)


def split(values):
    high = values.astype(jnp.bfloat16)
    low = (values - high.astype(jnp.float32)).astype(jnp.bfloat16)
    return high, low


def dot(left, right):
    return jnp.dot(left, right, preferred_element_type=jnp.float32)


def pack_spectrum(grid, rows, first):
    a = grid[rows, :HALF]
    c = grid[rows, HALF:]
    lower = slice(HALF + rows.start, HALF + rows.stop)
    d = grid[lower, :HALF]
    b = grid[lower, HALF:]
    col0 = lax.broadcasted_iota(jnp.int32, a.shape, 1) == 0
    plus_re = jnp.where(col0, a, a - b)
    plus_im = jnp.where(col0, d, c + d)
    minus_re = jnp.where(col0, c, a + b)
    minus_im = jnp.where(col0, b, c - d)
    if first:
        row0 = lax.broadcasted_iota(jnp.int32, a.shape, 0) == 0
        plus_re = jnp.where(row0, a, plus_re)
        plus_im = jnp.where(row0, c, plus_im)
        minus_re = jnp.where(row0, d, minus_re)
        minus_im = jnp.where(row0, b, minus_im)
    return plus_re, plus_im, minus_re, minus_im


def cross_terms(own, other, first):
    pr, pj, mr, mj = own
    qr, qj, nr, nj = other
    rr = pr * qr
    jj = pj * qj
    rp = rr + jj
    qp = pr * qj - pj * qr
    mrr = mr * nr
    mjj = mj * nj
    rm = mrr + mjj
    qm = mr * nj - mj * nr
    col0 = lax.broadcasted_iota(jnp.int32, pr.shape, 1) == 0
    cc = rp + jnp.where(col0, 0.0, rm)
    sc = qp - jnp.where(col0, 0.0, qm)
    cs = jnp.where(col0, rm, qp + qm)
    ss = jnp.where(col0, qm, rm - rp)
    if first:
        row0 = lax.broadcasted_iota(jnp.int32, pr.shape, 0) == 0
        corner = jnp.logical_and(row0, col0)
        cc = jnp.where(row0, jnp.where(corner, 0.5 * rr, rp), cc)
        cs = jnp.where(row0, jnp.where(corner, 0.5 * jj, qp), cs)
        sc = jnp.where(row0, jnp.where(corner, 0.5 * mrr, rm), sc)
        ss = jnp.where(row0, jnp.where(corner, 0.5 * mjj, qm), ss)
    return cc, cs, sc, ss


def to_column(row):
    count = NODES_DEV
    wide = jnp.broadcast_to(row, (count, count))
    diagonal = lax.broadcasted_iota(jnp.int32, (count, count), 0) == lax.broadcasted_iota(
        jnp.int32, (count, count), 1
    )
    return jnp.sum(jnp.where(diagonal, wide, 0.0), axis=1, keepdims=True)


def total(values):
    return jnp.sum(jnp.sum(values, axis=0, keepdims=True), axis=1, keepdims=True)


def kernel(
    n_gz, n_xy,
    patches, offsets_hbm, valid_hbm, rows_hbm, columns_hbm,
    solved,
    offsets, valid, rows_table, columns_table, right_fwd, left_fwd, right_inv, left_inv, images, row_spectra, spec, mix, half_maps, maps, lag_rows, stats, nears, shifts, shifts_prior,
    lag_columns, lag_rims, picks,
    own_row, all_rows, final,
    input_sems, image_sems, send_sems, recv_sems, shift_sems, row_sems, ready,
):
    gz = lax.axis_index("gz")
    xy = lax.axis_index("xy")
    after = jnp.bitwise_and(gz + 1, n_gz - 1)
    before = jnp.bitwise_and(gz - 1 + n_gz, n_gz - 1)

    core = jnp.bitwise_and(gz, 1)
    barrier = pltpu.get_barrier_semaphore()

    me = xy * n_gz + gz
    count = n_gz * n_xy

    row_start = gz - jnp.bitwise_and(gz, 7)
    row_peers = [row_start + jnp.bitwise_and(gz + step, 7) for step in range(1, 8)]
    column_peers = [(jnp.bitwise_and(gz + 8 * step, n_gz - 1), xy) for step in range(1, 4)]
    line_peers = [(gz, jnp.bitwise_and(xy + step, n_xy - 1)) for step in range(1, 4)]
    greeted = [(before, xy), (after, xy)] + [(peer, xy) for peer in row_peers]
    greeted = greeted + column_peers + line_peers
    for peer in greeted:
        pl.semaphore_signal(barrier, inc=1, device_id=peer, device_id_type=MESH)

    def image_copy(section, node):
        return pltpu.make_async_copy(
            patches.at[section, node], images.at[node, section], image_sems.at[section, node]
        )

    inputs = [
        pltpu.make_async_copy(source, target, input_sems.at[place])
        for place, (source, target) in enumerate(
            ((rows_hbm, rows_table), (columns_hbm, columns_table), (offsets_hbm, offsets),
             (valid_hbm, valid))
        )
    ]
    for copy in inputs[:2]:
        copy.start()

    @pl.loop(0, NODES_DEV)
    def _(node):
        image_copy(0, node).start()
        image_copy(1, node).start()

    for copy in inputs[2:]:
        copy.start()

    for copy in inputs:
        copy.wait()

    left_fwd[...] = rows_table[...].astype(jnp.bfloat16)
    right_fwd[...] = columns_table[...].astype(jnp.bfloat16)
    high, low = split(rows_table[...])
    right_inv[...] = jnp.concatenate([high, high, low], axis=0)
    high, low = split(columns_table[...] * (2.0 / math.log(2.0) / float(SIZE) ** 3))
    left_inv[...] = jnp.concatenate([high, high, low], axis=1)

    lag = lax.rem(lax.broadcasted_iota(jnp.int32, (SIZE, LANES), 0) + HALF, SIZE) - HALF
    lag_rows[...] = lag.astype(jnp.float32)
    moves = offsets[...].astype(jnp.float32)
    for partner in range(2):
        for section in range(2):
            for component in range(2):
                column = to_column(moves[partner, component, section : section + 1, :])
                place = (partner * 2 + section) * 2 + component
                shifts[place] = jnp.broadcast_to(column, (NODES_DEV, LANES))

    def spectrum_copy(way, node, half=None):
        part = slice(None) if half is None else pl.ds(half * (HALF // 2), HALF // 2)
        place = node + (half or 0)
        return pltpu.make_async_remote_copy(
            src_ref=spec.at[1 + way, node, :, part], dst_ref=spec.at[3 - 3 * way, node, :, part],
            send_sem=send_sems.at[way, place], recv_sem=recv_sems.at[way, place],
            device_id=(jnp.bitwise_and(gz + 2 * way - 1 + n_gz, n_gz - 1), xy),
            device_id_type=MESH,
        )

    def shift_copy():
        return pltpu.make_async_remote_copy(
            src_ref=shifts.at[pl.ds(6, 2)], dst_ref=shifts_prior,
            send_sem=shift_sems.at[0], recv_sem=shift_sems.at[1],
            device_id=(after, xy), device_id_type=MESH,
        )

    def transform_rows(node):
        both = images[node].reshape(2 * SIZE, SIZE)
        row_spectra[...] = dot(both, right_fwd[...]).astype(jnp.bfloat16)

    def transform_columns(node):
        for section in range(2):
            grid = dot(left_fwd[...], row_spectra[section * SIZE : (section + 1) * SIZE])
            for rows, first in ((slice(0, 16), True), (slice(16, HALF), False)):
                parts = pack_spectrum(grid, rows, first)
                for part in range(4):
                    spec[section + 1, node, part, rows, :] = parts[part].astype(jnp.bfloat16)

    def await_images(node):
        image_copy(0, node).wait()
        image_copy(1, node).wait()

    def send(node):
        spectrum_copy(core, node).start()
        spectrum_copy(1 - core, node).start()

    await_images(0)
    transform_rows(0)

    @pl.loop(1, NODES_DEV)
    def _(node):
        await_images(node)
        transform_columns(node - 1)
        transform_rows(node)

        @pl.when(node == 1)
        def _():
            pl.semaphore_wait(barrier, len(greeted))

        send(node - 1)

        @pl.when(node == 1)
        def _():
            shift_copy().start()
            for peer in column_peers:
                pl.semaphore_signal(ready.at[0], inc=1, device_id=peer, device_id_type=MESH)

    def plan(step):
        in_own = step < 4
        next_from = 4 + 4 * core
        in_next = jnp.logical_and(step >= next_from, step < next_from + 8)
        prior_from = 12 - 8 * core
        in_prior = jnp.logical_and(step >= prior_from, step < prior_from + 4)
        node_next = jnp.clip(step - next_from, 0, 7)
        node_pair = jnp.where(in_own, 2 * step, jnp.clip(2 * (step - prior_from), 0, 6))
        two = jnp.where(in_next, 3, 2)
        return (
            in_next,
            in_prior,
            (
                jnp.where(in_prior, 0, 1),
                two,
                jnp.where(in_next, node_next, node_pair),
                jnp.where(in_next, 2, jnp.where(in_prior, 3, 0)),
            ),
            (
                jnp.where(in_prior, 0, jnp.where(in_next, 2, 1)),
                two,
                jnp.where(in_next, node_next, node_pair + 1),
                jnp.where(in_next, 1, jnp.where(in_prior, 3, 0)),
            ),
        )

    def await_partners(step):
        in_next, in_prior, (_, _, node, _), (_, _, other, _) = plan(step)

        @pl.when(jnp.logical_and(in_next, node < NODES_DEV - 1))
        def _():
            spectrum_copy(0, node).wait_recv()

        @pl.when(jnp.logical_and(in_next, node == NODES_DEV - 1))
        def _():
            spectrum_copy(0, NODES_DEV - 1, 0).wait_recv()
            spectrum_copy(0, NODES_DEV - 1, 1).wait_recv()

        @pl.when(in_prior)
        def _():
            spectrum_copy(1, node).wait_recv()

        @pl.when(jnp.logical_and(in_prior, other < NODES_DEV - 1))
        def _():
            spectrum_copy(1, other).wait_recv()

        @pl.when(jnp.logical_and(in_prior, other == NODES_DEV - 1))
        def _():
            spectrum_copy(1, NODES_DEV - 1, 0).wait_recv()
            spectrum_copy(1, NODES_DEV - 1, 1).wait_recv()

    def products(step, begin=0, end=HALF):
        spans = [(slice(begin, end), False)]
        if begin == 0:
            spans = [(slice(0, 16), True), (slice(16, end), False)]
        for slot, (one, two, node, _) in enumerate(plan(step)[2:]):
            for rows, first in spans:
                own = [spec[one, node, part, rows, :].astype(jnp.float32) for part in range(4)]
                other = [spec[two, node, part, rows, :].astype(jnp.float32) for part in range(4)]
                terms = cross_terms(own, other, first)
                lower = slice(HALF + rows.start, HALF + rows.stop)
                for part, (where, lanes) in enumerate(
                    ((rows, 0), (rows, HALF), (lower, 0), (lower, HALF))
                ):
                    high, low = split(terms[part])
                    mix[slot, where, lanes : lanes + HALF] = high
                    mix[slot, where, SIZE + lanes : SIZE + lanes + HALF] = low
        for slot in range(2):
            left = jnp.concatenate(
                [mix[slot, begin:end], mix[slot, HALF + begin : HALF + end]], axis=0
            )
            left = jnp.concatenate([left, left[:, :SIZE]], axis=1)
            count = end - begin
            for place, values in enumerate(split(dot(left, right_inv[...]))):
                start = place * SIZE + begin
                half_maps[slot, start : start + count] = values[:count]
                half_maps[slot, start + HALF : start + HALF + count] = values[count:]

    def statistics(step):
        for slot, (_, _, node, group) in enumerate(plan(step)[2:]):
            right = jnp.concatenate([half_maps[slot], half_maps[slot, :SIZE]], axis=0)
            values = dot(left_inv[...], right)
            maps[slot] = values
            top = jnp.max(values, axis=(0, 1), keepdims=True)
            mass, moment, rim = [], [], []
            for side in range(2):
                raised = jnp.exp2(maps[slot, :, side * HALF : (side + 1) * HALF] - top)
                mass.append(jnp.sum(raised, axis=0, keepdims=True))
                moment.append(jnp.sum(raised * lag_rows[...], axis=0, keepdims=True))
                rim.append(raised[HALF - 8 : HALF + 8])
            rim = rim[0] + rim[1]
            stats[group, node] = jnp.concatenate([*mass, *moment, rim[6:10]], axis=0)
            low_lane = lax.broadcasted_iota(jnp.int32, (8, HALF), 1) < HALF // 2
            for place, start in ((0, 0), (1, SIZE - 8)):
                edge = maps[slot, start : start + 8, :]
                nears[group, node, place] = jnp.where(low_lane, edge[:, :HALF], edge[:, HALF:])

    def offset_tables():
        shift_copy().wait_recv()
        columns = lax.broadcasted_iota(jnp.int32, (NODES_DEV, HALF), 1)
        near_lane = jnp.where(columns < HALF // 2, columns, columns - HALF)
        for group, place in ((0, 0), (1, 2), (2, 4), (3, None)):
            if place is None:
                move_x, move_y = shifts_prior[0], shifts_prior[1]
            else:
                move_x, move_y = shifts[place], shifts[place + 1]
            move_x = move_x.astype(jnp.int32)
            move_y = move_y.astype(jnp.int32)
            for side in range(2):
                lag = jnp.bitwise_and(columns + side * HALF - move_x + HALF, SIZE - 1)
                lag_columns[group, side] = (lag - HALF + move_x).astype(jnp.float32)
            for row in range(4):
                plain = HALF - 2 + row if row < 2 else row - 2 - HALF
                lag = jnp.bitwise_and(row - 2 - move_y, SIZE - 1) - HALF + move_y
                lag_rims[group, row] = (lag - plain).astype(jnp.float32)
            here = near_lane == move_x
            for row in range(-2, 3):
                found = jnp.logical_and(here, move_y == row)
                picks[group, row + 2] = jnp.where(found, 1.0, 0.0)

    steps = 16
    transform_columns(NODES_DEV - 1)
    products(0)
    for half in range(2):
        spectrum_copy(core, NODES_DEV - 1, half).start()
        spectrum_copy(1 - core, NODES_DEV - 1, half).start()

    @pl.loop(1, steps - 1)
    def _(step):
        await_partners(step)

        @pl.when(step == 6)
        def _():
            pl.semaphore_wait(ready.at[0], len(column_peers))
            for peer in line_peers:
                pl.semaphore_signal(ready.at[1], inc=1, device_id=peer, device_id_type=MESH)

        statistics(step - 1)
        products(step)

    statistics(steps - 2)
    offset_tables()
    last = NODES_DEV - 1

    @pl.when(core == 0)
    def _():
        spectrum_copy(1, last - 1).wait_recv()
        spectrum_copy(1, last, 0).wait_recv()

    @pl.when(core == 1)
    def _():
        spectrum_copy(0, last, 0).wait_recv()

    products(steps - 1, 0, HALF // 2)
    spectrum_copy(1 - core, last, 1).wait_recv()
    products(steps - 1, HALF // 2, HALF)
    statistics(steps - 1)


    weights = []
    targets = []
    for group in range(4):
        mass = [stats[group, :, side, :] for side in range(2)]
        whole = mass[0] + mass[1]
        sum_x = mass[0] * lag_columns[group, 0] + mass[1] * lag_columns[group, 1]
        sum_y = stats[group, :, 2, :] + stats[group, :, 3, :]
        for row in range(4):
            sum_y = sum_y + stats[group, :, 4 + row, :] * lag_rims[group, row]
        picked = 0.0
        for row in range(-2, 3):
            near = nears[group, :, 0 if row >= 0 else 1, row % 8, :]
            picked = picked + jnp.where(picks[group, row + 2] > 0.5, near, 0.0)
        whole = jnp.sum(whole, axis=1, keepdims=True)
        sum_x = jnp.sum(sum_x, axis=1, keepdims=True)
        sum_y = jnp.sum(sum_y, axis=1, keepdims=True)
        score = jnp.sum(picked, axis=1, keepdims=True) * math.log(2.0)
        weights.append(0.5 + 1.0 / (1.0 + jnp.exp(-score)))
        targets.append((sum_x / whole, sum_y / whole))

    lane = lax.broadcasted_iota(jnp.int32, (NODES_DEV, LANES), 1)
    node_lane = jnp.bitwise_and(lane, 31) == lax.broadcasted_iota(
        jnp.int32, (NODES_DEV, LANES), 0
    )
    odd = lane >= 64
    second = jnp.bitwise_and(lane, 32) > 0

    def place_row(even_x, even_y, odd_x, odd_y):
        chosen = jnp.where(
            odd, jnp.where(second, odd_y, odd_x), jnp.where(second, even_y, even_x)
        )
        return jnp.sum(jnp.where(node_lane, chosen, 0.0), axis=0, keepdims=True)

    marks = valid[...].astype(jnp.float32)
    mark_even, mark_odd = to_column(marks[0:1, :]), to_column(marks[1:2, :])
    row_w = place_row(weights[0], mark_even, weights[1], mark_odd)
    row_t = place_row(*targets[0], *targets[1])
    row_v = place_row(weights[2], weights[2], weights[3], weights[3])
    row_u = place_row(*targets[2], *targets[3])
    row = row_w + pltpu.roll(row_t, 8, axis=1)
    row = row + pltpu.roll(row_v, 16, axis=1) + pltpu.roll(row_u, 24, axis=1)
    own_row[...] = jnp.broadcast_to(row, (8, LANES))

    me = xy * n_gz + gz
    count = n_gz * n_xy
    pl.semaphore_wait(ready.at[1], len(line_peers))
    mine = pltpu.make_async_copy(own_row.at[0:1], all_rows.at[pl.ds(me, 1)], row_sems.at[2])
    mine.start()

    to_z = [jnp.bitwise_and(xy + step, 3) for step in range(4)]
    to_y = [jnp.bitwise_and(gz + 8 * step, 24) for step in range(4)]
    to_x = [jnp.bitwise_and(gz + 2 * step, 6) for step in range(4)]
    to_core = [core, 1 - core]
    hops = (0, 1, 2, 1)
    ways = [(z, y, x, c) for z in range(4) for y in range(4) for x in range(4) for c in range(2)]
    ways.sort(key=lambda way: -hops[way[0]] - hops[way[1]] - hops[way[2]])
    for z, y, x, c in ways:
        if (z, y, x, c) == (0, 0, 0, 0):
            continue
        pltpu.make_async_remote_copy(
            src_ref=own_row.at[0:1], dst_ref=all_rows.at[pl.ds(me, 1)],
            send_sem=row_sems.at[0], recv_sem=row_sems.at[1],
            device_id=(to_y[y] + to_x[x] + to_core[c], to_z[z]), device_id_type=MESH,
        ).start()

    shape = (n_gz, LANES)
    lane = lax.broadcasted_iota(jnp.int32, shape, 1)
    row = lax.broadcasted_iota(jnp.int32, shape, 0)
    even = lane < 64

    def up(v):
        return pltpu.roll(v, n_gz - 1, axis=0)

    def down(v):
        return pltpu.roll(v, 1, axis=0)

    def lanes_on(v, by):
        return pltpu.roll(v, by % LANES, axis=1)

    def following(v):
        swapped = lanes_on(v, 64)
        return jnp.where(even, swapped, up(swapped))

    def preceding(v):
        swapped = lanes_on(v, 64)
        return jnp.where(even, down(swapped), swapped)

    node = jnp.bitwise_and(lane, 31)
    col = jnp.bitwise_and(node, COLS - 1)
    nodes = NODES_DEV * n_xy
    has_right = jnp.where(col < COLS - 1, 1.0, 0.0)
    has_left = jnp.where(col > 0, 1.0, 0.0)
    has_below = jnp.where(node < nodes - COLS, 1.0, 0.0)
    has_above = jnp.where(node >= COLS, 1.0, 0.0)
    shift_copy().wait_send()

    @pl.loop(0, NODES_DEV - 1)
    def _(node):
        spectrum_copy(0, node).wait_send()
        spectrum_copy(1, node).wait_send()

    for half in range(2):
        spectrum_copy(0, NODES_DEV - 1, half).wait_send()
        spectrum_copy(1, NODES_DEV - 1, half).wait_send()

    rest = all_rows.at[pl.ds(0, count - 1)]
    mine.wait()
    pltpu.make_async_copy(rest, rest, row_sems.at[1]).wait()
    pltpu.make_async_copy(rest, rest, row_sems.at[0]).wait()

    final_row = row == n_gz - 1
    window = jnp.bitwise_and(lane, 31) // NODES_DEV
    fields = [0.0] * 4
    for strip in range(n_xy):
        block = all_rows[strip * n_gz : (strip + 1) * n_gz, :]
        for field in range(4):
            moved = lanes_on(block, NODES_DEV * (strip - field)) if strip != field else block
            fields[field] = jnp.where(window == strip, moved, fields[field])
    marked, near_target, far_weight, far_target = fields
    first_part = jnp.bitwise_and(lane, 32) == 0
    near_weight = jnp.where(first_part, marked, lanes_on(marked, 32))
    mark = jnp.where(first_part, lanes_on(marked, -32), marked)
    far_weight = jnp.where(even, far_weight, up(far_weight))
    far_target = jnp.where(even, far_target, up(far_target))
    near_weight = near_weight * mark * following(mark)
    far_weight = far_weight * mark * up(mark)
    near_weight = jnp.where(jnp.logical_and(final_row, jnp.logical_not(even)), 0.0, near_weight)
    far_weight = jnp.where(final_row, 0.0, far_weight)
    near_in = preceding(near_weight)
    far_in = down(far_weight)

    diagonal = (
        LAM + has_right + has_left + has_below + has_above
        + near_weight + near_in + far_weight + far_in
    )

    def operate(v):
        beside = (
            has_right * lanes_on(v, -1) + has_left * lanes_on(v, 1)
            + has_below * lanes_on(v, -COLS) + has_above * lanes_on(v, COLS)
        )
        along = near_weight * following(v) + near_in * preceding(v)
        along = along + far_weight * up(v) + far_in * down(v)
        return diagonal * v - beside - along

    swapped = lanes_on(near_target, 64)
    running = near_target + swapped
    by = 1
    while by < n_gz:
        running = running + jnp.where(row >= by, pltpu.roll(running, by, axis=0), 0.0)
        by *= 2
    entering = jnp.where(row >= 1, down(running), 0.0)
    initial = entering + jnp.where(even, 0.0, swapped)
    near_pull = near_weight * near_target
    far_pull = far_weight * far_target
    right_side = LAM * initial + preceding(near_pull) - near_pull + down(far_pull) - far_pull

    position = initial
    residual = right_side - operate(initial)
    direction = residual
    norm = total(residual * residual)
    for iteration in range(ITERS):
        image = operate(direction)
        step = norm / total(direction * image)
        position = position + step * direction
        residual = residual - step * image
        if iteration < ITERS - 1:
            norm_next = total(residual * residual)
            direction = residual + (norm_next / norm) * direction
            norm = norm_next

    final[0] = position
    final[1] = residual
    for place in range(2):
        own = pltpu.roll(
            final[place, pl.ds(gz, 1), :], lax.rem(LANES - NODES_DEV * xy, LANES), axis=1
        )
        for component in range(2):
            for parity in range(2):
                start = parity * 64 + component * 32
                solved[place, component, parity : parity + 1, :] = own[:, start : start + NODES_DEV]


def per_device(n_gz, n_xy, patches, offsets, valid):
    vmem = pl.BlockSpec(memory_space=pltpu.VMEM)
    out = jax.ShapeDtypeStruct((2, 2, 2, NODES_DEV), jnp.float32)
    f32, bf16 = jnp.float32, jnp.bfloat16
    both = pl.pallas_call(
        functools.partial(kernel, n_gz, n_xy),
        out_shape=out,
        in_specs=[pl.BlockSpec(memory_space=pltpu.HBM)] * 5,
        out_specs=vmem,
        scratch_shapes=[
            pltpu.VMEM((2, 2, 2, NODES_DEV), jnp.int32),
            pltpu.VMEM((2, NODES_DEV), jnp.int32),
            pltpu.VMEM((SIZE, SIZE), f32),
            pltpu.VMEM((SIZE, SIZE), f32),
            pltpu.VMEM((SIZE, SIZE), bf16),
            pltpu.VMEM((SIZE, SIZE), bf16),
            pltpu.VMEM((3 * SIZE, SIZE), bf16),
            pltpu.VMEM((SIZE, 3 * SIZE), bf16),
            pltpu.VMEM((NODES_DEV, 2, SIZE, SIZE), bf16),
            pltpu.VMEM((2 * SIZE, SIZE), bf16),
            pltpu.VMEM((4, NODES_DEV, 4, HALF, HALF), bf16),
            pltpu.VMEM((2, SIZE, 2 * SIZE), bf16),
            pltpu.VMEM((2, 2 * SIZE, SIZE), bf16),
            pltpu.VMEM((2, SIZE, SIZE), f32),
            pltpu.VMEM((SIZE, LANES), f32),
            pltpu.VMEM((4, NODES_DEV, 8, LANES), f32),
            pltpu.VMEM((4, NODES_DEV, 2, 8, LANES), f32),
            pltpu.VMEM((8, NODES_DEV, LANES), f32),
            pltpu.VMEM((2, NODES_DEV, LANES), f32),
            pltpu.VMEM((4, 2, NODES_DEV, LANES), f32),
            pltpu.VMEM((4, 4, NODES_DEV, LANES), f32),
            pltpu.VMEM((4, 5, NODES_DEV, LANES), f32),
            pltpu.VMEM((8, LANES), f32),
            pltpu.VMEM((n_gz * n_xy, LANES), f32),
            pltpu.VMEM((2, n_gz, LANES), f32),
            pltpu.SemaphoreType.DMA((4,)),
            pltpu.SemaphoreType.DMA((2, NODES_DEV)),
            pltpu.SemaphoreType.DMA((2, NODES_DEV + 1)),
            pltpu.SemaphoreType.DMA((2, NODES_DEV + 1)),
            pltpu.SemaphoreType.DMA((2,)),
            pltpu.SemaphoreType.DMA((3,)),
            pltpu.SemaphoreType.REGULAR((2,)),
        ],
        compiler_params=pltpu.CompilerParams(
            collective_id=0, has_side_effects=True, vmem_limit_bytes=48 * 1024 * 1024
        ),
    )(*(pltpu.with_memory_space_constraint(arg, pltpu.HBM) for arg in (patches, offsets, valid, *(jnp.asarray(table) for table in tables()))))
    return both[0], both[1]


def solution(mesh):
    return jax.shard_map(
        functools.partial(per_device, mesh.shape["gz"], mesh.shape["xy"]),
        mesh=mesh,
        in_specs=(P("gz", "xy", None, None), P(None, None, "gz", "xy"), P("gz", "xy")),
        out_specs=(P(None, "gz", "xy"), P(None, "gz", "xy")),
        check_vma=False,
    )
```

```python
import functools
import math

import jax
import jax.numpy as jnp
import numpy as np
from jax import lax
from jax.experimental import pallas as pl
from jax.experimental.pallas import tpu as pltpu
from jax.sharding import PartitionSpec as P

SIZE = 256
HALF = 128
NODES_DEV = 8
COLS = 8
ITERS = 3
LANES = 128
GREETED = 3
CUT = 96
MESH = pl.DeviceIdType.MESH
LAM = 0.25


def tables():
    index = np.arange(SIZE)
    angles = ((index[:, None] * index[None, :]) % SIZE) * (2.0 * math.pi / SIZE)
    rows = np.concatenate([np.cos(angles)[:HALF], np.sin(angles)[:HALF]])
    rows[HALF] = np.cos(angles)[HALF]

    return rows.astype(np.float32), np.ascontiguousarray(rows.T).astype(np.float32)


def split(values):
    high = values.astype(jnp.bfloat16)
    low = (values - high.astype(jnp.float32)).astype(jnp.bfloat16)
    return high, low


def dot(left, right):
    return jnp.dot(left, right, preferred_element_type=jnp.float32)


def pack_spectrum(grid, rows, first):
    a = grid[rows, :HALF]
    c = grid[rows, HALF:]
    lower = slice(HALF + rows.start, HALF + rows.stop)
    d = grid[lower, :HALF]
    b = grid[lower, HALF:]
    col0 = lax.broadcasted_iota(jnp.int32, a.shape, 1) == 0
    plus_re = jnp.where(col0, a, a - b)
    plus_im = jnp.where(col0, d, c + d)
    minus_re = jnp.where(col0, c, a + b)
    minus_im = jnp.where(col0, b, c - d)
    if first:
        row0 = lax.broadcasted_iota(jnp.int32, a.shape, 0) == 0
        plus_re = jnp.where(row0, a, plus_re)
        plus_im = jnp.where(row0, c, plus_im)
        minus_re = jnp.where(row0, d, minus_re)
        minus_im = jnp.where(row0, b, minus_im)
    return plus_re, plus_im, minus_re, minus_im


def cross_terms(own, other, first):
    pr, pj, mr, mj = own
    qr, qj, nr, nj = other
    rr = pr * qr
    jj = pj * qj
    rp = rr + jj
    qp = pr * qj - pj * qr
    mrr = mr * nr
    mjj = mj * nj
    rm = mrr + mjj
    qm = mr * nj - mj * nr
    col0 = lax.broadcasted_iota(jnp.int32, pr.shape, 1) == 0
    cc = rp + jnp.where(col0, 0.0, rm)
    sc = qp - jnp.where(col0, 0.0, qm)
    cs = jnp.where(col0, rm, qp + qm)
    ss = jnp.where(col0, qm, rm - rp)
    if first:
        row0 = lax.broadcasted_iota(jnp.int32, pr.shape, 0) == 0
        corner = jnp.logical_and(row0, col0)
        cc = jnp.where(row0, jnp.where(corner, 0.5 * rr, rp), cc)
        cs = jnp.where(row0, jnp.where(corner, 0.5 * jj, qp), cs)
        sc = jnp.where(row0, jnp.where(corner, 0.5 * mrr, rm), sc)
        ss = jnp.where(row0, jnp.where(corner, 0.5 * mjj, qm), ss)
    return cc, cs, sc, ss


def to_column(row):
    count = NODES_DEV
    wide = jnp.broadcast_to(row, (count, count))
    diagonal = lax.broadcasted_iota(jnp.int32, (count, count), 0) == lax.broadcasted_iota(
        jnp.int32, (count, count), 1
    )
    return jnp.sum(jnp.where(diagonal, wide, 0.0), axis=1, keepdims=True)


def total(values):
    return jnp.sum(jnp.sum(values, axis=0, keepdims=True), axis=1, keepdims=True)


def kernel(
    n_gz, n_xy,
    patches, offsets_hbm, valid_hbm, rows_hbm, columns_hbm,
    solved,
    offsets, valid, rows_table, columns_table, right_fwd, left_fwd, right_inv, left_inv, images, row_spectra, spec, mix, half_maps, maps, lag_rows, stats, nears, shifts, shifts_prior,
    lag_columns, lag_rims, picks, marked_lanes,
    own_row, all_rows, final,
    input_sems, image_sems, send_sems, recv_sems, shift_sems, row_sems, ready,
):
    gz = lax.axis_index("gz")
    xy = lax.axis_index("xy")
    after = jnp.bitwise_and(gz + 1, n_gz - 1)
    before = jnp.bitwise_and(gz - 1 + n_gz, n_gz - 1)

    core = jnp.bitwise_and(gz, 1)
    barrier = pltpu.get_barrier_semaphore()

    me = xy * n_gz + gz
    count = n_gz * n_xy

    row_start = gz - jnp.bitwise_and(gz, 7)
    row_peers = [row_start + jnp.bitwise_and(gz + step, 7) for step in range(1, 8)]
    column_peers = [(jnp.bitwise_and(gz + 8 * step, n_gz - 1), xy) for step in range(1, 4)]
    line_peers = [(gz, jnp.bitwise_and(xy + step, n_xy - 1)) for step in range(1, 4)]
    greeted = [(before, xy), (after, xy)] + [(peer, xy) for peer in row_peers]
    greeted = greeted + column_peers + line_peers
    for peer in greeted:
        pl.semaphore_signal(barrier, inc=1, device_id=peer, device_id_type=MESH)

    def image_copy(node):
        return pltpu.make_async_copy(
            patches.at[:, node], images.at[node], image_sems.at[jnp.minimum(node, 1)]
        )

    inputs = [
        pltpu.make_async_copy(source, target, input_sems.at[place])
        for place, (source, target) in enumerate(
            ((rows_hbm, rows_table), (columns_hbm, columns_table), (offsets_hbm, offsets),
             (valid_hbm, valid))
        )
    ]
    for copy in inputs[:2]:
        copy.start()

    @pl.loop(0, NODES_DEV)
    def _(node):
        image_copy(node).start()

    for copy in inputs[2:]:
        copy.start()

    for copy in inputs:
        copy.wait()

    left_fwd[...] = rows_table[...].astype(jnp.bfloat16)
    right_fwd[...] = columns_table[...].astype(jnp.bfloat16)
    high, low = split(rows_table[...])
    right_inv[...] = jnp.concatenate([high, high, low], axis=0)
    high, low = split(columns_table[...] * (2.0 / math.log(2.0) / float(SIZE) ** 3))
    left_inv[...] = jnp.concatenate([high, high, low], axis=1)

    lag = lax.rem(lax.broadcasted_iota(jnp.int32, (SIZE, LANES), 0) + HALF, SIZE) - HALF
    lag_rows[...] = lag.astype(jnp.float32)
    moves = offsets[...].astype(jnp.float32)
    for partner in range(2):
        for section in range(2):
            for component in range(2):
                column = to_column(moves[partner, component, section : section + 1, :])
                place = (partner * 2 + section) * 2 + component
                shifts[place] = jnp.broadcast_to(column, (NODES_DEV, LANES))

    def spectrum_copy(way, node, piece=None):
        part = slice(None) if piece is None else pl.ds(*((0, CUT), (CUT, HALF - CUT))[piece])
        place = node + (piece or 0)
        return pltpu.make_async_remote_copy(
            src_ref=spec.at[1 + way, node, :, part], dst_ref=spec.at[3 - 3 * way, node, :, part],
            send_sem=send_sems.at[way], recv_sem=recv_sems.at[way, place],
            device_id=(jnp.bitwise_and(gz + 2 * way - 1 + n_gz, n_gz - 1), xy),
            device_id_type=MESH,
        )

    def shift_copy():
        return pltpu.make_async_remote_copy(
            src_ref=shifts.at[pl.ds(6, 2)], dst_ref=shifts_prior,
            send_sem=shift_sems.at[0], recv_sem=shift_sems.at[1],
            device_id=(after, xy), device_id_type=MESH,
        )

    def transform_rows(node):
        both = images[node].reshape(2 * SIZE, SIZE)
        row_spectra[...] = dot(both, right_fwd[...]).astype(jnp.bfloat16)

    def transform_columns(node):
        for section in range(2):
            grid = dot(left_fwd[...], row_spectra[section * SIZE : (section + 1) * SIZE])
            for rows, first in ((slice(0, 16), True), (slice(16, HALF), False)):
                parts = pack_spectrum(grid, rows, first)
                for part in range(4):
                    spec[section + 1, node, part, rows, :] = parts[part].astype(jnp.bfloat16)

    def send(node):
        spectrum_copy(core, node).start()
        spectrum_copy(1 - core, node).start()

    image_copy(0).wait()
    transform_rows(0)
    others = images.at[pl.ds(1, NODES_DEV - 1)]
    pltpu.make_async_copy(others, others, image_sems.at[1]).wait()

    @pl.loop(1, NODES_DEV)
    def _(node):
        transform_columns(node - 1)
        transform_rows(node)

        @pl.when(node == GREETED)
        def _():
            pl.semaphore_wait(barrier, len(greeted))
            pl.loop(0, GREETED - 1)(send)

        @pl.when(node >= GREETED)
        def _():
            send(node - 1)

        @pl.when(node == GREETED)
        def _():
            shift_copy().start()
            for peer in column_peers:
                pl.semaphore_signal(ready.at[0], inc=1, device_id=peer, device_id_type=MESH)

    def plan(step):
        in_own = step < 4
        next_from = 4 + 4 * core
        in_next = jnp.logical_and(step >= next_from, step < next_from + 8)
        prior_from = 12 - 8 * core
        in_prior = jnp.logical_and(step >= prior_from, step < prior_from + 4)
        node_next = jnp.clip(step - next_from, 0, 7)
        node_pair = jnp.where(in_own, 2 * step, jnp.clip(2 * (step - prior_from), 0, 6))
        two = jnp.where(in_next, 3, 2)
        return (
            in_next,
            in_prior,
            (
                jnp.where(in_prior, 0, 1),
                two,
                jnp.where(in_next, node_next, node_pair),
                jnp.where(in_next, 2, jnp.where(in_prior, 3, 0)),
            ),
            (
                jnp.where(in_prior, 0, jnp.where(in_next, 2, 1)),
                two,
                jnp.where(in_next, node_next, node_pair + 1),
                jnp.where(in_next, 1, jnp.where(in_prior, 3, 0)),
            ),
        )

    def await_partners(step):
        in_next, in_prior, (_, _, node, _), (_, _, other, _) = plan(step)

        @pl.when(jnp.logical_and(in_next, node < NODES_DEV - 1))
        def _():
            spectrum_copy(0, node).wait_recv()

        @pl.when(jnp.logical_and(in_next, node == NODES_DEV - 1))
        def _():
            spectrum_copy(0, NODES_DEV - 1, 0).wait_recv()
            spectrum_copy(0, NODES_DEV - 1, 1).wait_recv()

        @pl.when(in_prior)
        def _():
            spectrum_copy(1, node).wait_recv()

        @pl.when(jnp.logical_and(in_prior, other < NODES_DEV - 1))
        def _():
            spectrum_copy(1, other).wait_recv()

        @pl.when(jnp.logical_and(in_prior, other == NODES_DEV - 1))
        def _():
            spectrum_copy(1, NODES_DEV - 1, 0).wait_recv()
            spectrum_copy(1, NODES_DEV - 1, 1).wait_recv()

    def products(step, begin=0, end=HALF):
        spans = [(slice(begin, end), False)]
        if begin == 0:
            spans = [(slice(0, 16), True), (slice(16, end), False)]
        for slot, (one, two, node, _) in enumerate(plan(step)[2:]):
            for rows, first in spans:
                own = [spec[one, node, part, rows, :].astype(jnp.float32) for part in range(4)]
                other = [spec[two, node, part, rows, :].astype(jnp.float32) for part in range(4)]
                terms = cross_terms(own, other, first)
                lower = slice(HALF + rows.start, HALF + rows.stop)
                for part, (where, lanes) in enumerate(
                    ((rows, 0), (rows, HALF), (lower, 0), (lower, HALF))
                ):
                    high, low = split(terms[part])
                    mix[slot, where, lanes : lanes + HALF] = high
                    mix[slot, where, SIZE + lanes : SIZE + lanes + HALF] = low
        for slot in range(2):
            left = jnp.concatenate(
                [mix[slot, begin:end], mix[slot, HALF + begin : HALF + end]], axis=0
            )
            left = jnp.concatenate([left, left[:, :SIZE]], axis=1)
            count = end - begin
            for place, values in enumerate(split(dot(left, right_inv[...]))):
                start = place * SIZE + begin
                half_maps[slot, start : start + count] = values[:count]
                half_maps[slot, start + HALF : start + HALF + count] = values[count:]

    def statistics(step):
        for slot, (_, _, node, group) in enumerate(plan(step)[2:]):
            right = jnp.concatenate([half_maps[slot], half_maps[slot, :SIZE]], axis=0)
            values = dot(left_inv[...], right)
            maps[slot] = values
            top = jnp.max(values, axis=(0, 1), keepdims=True)
            mass, moment, rim = [], [], []
            for side in range(2):
                raised = jnp.exp2(maps[slot, :, side * HALF : (side + 1) * HALF] - top)
                mass.append(jnp.sum(raised, axis=0, keepdims=True))
                moment.append(jnp.sum(raised * lag_rows[...], axis=0, keepdims=True))
                rim.append(raised[HALF - 8 : HALF + 8])
            rim = rim[0] + rim[1]
            stats[group, node] = jnp.concatenate([*mass, *moment, rim[6:10]], axis=0)
            low_lane = lax.broadcasted_iota(jnp.int32, (8, HALF), 1) < HALF // 2
            for place, start in ((0, 0), (1, SIZE - 8)):
                edge = maps[slot, start : start + 8, :]
                nears[group, node, place] = jnp.where(low_lane, edge[:, :HALF], edge[:, HALF:])

    def offset_tables():
        shift_copy().wait_recv()
        columns = lax.broadcasted_iota(jnp.int32, (NODES_DEV, HALF), 1)
        near_lane = jnp.where(columns < HALF // 2, columns, columns - HALF)
        marks = valid[...].astype(jnp.float32)
        even_mark, odd_mark = to_column(marks[0:1, :]), to_column(marks[1:2, :])
        marked_lanes[...] = jnp.where(columns >= 64, odd_mark, even_mark)
        for group, place in ((0, 0), (1, 2), (2, 4), (3, None)):
            if place is None:
                move_x, move_y = shifts_prior[0], shifts_prior[1]
            else:
                move_x, move_y = shifts[place], shifts[place + 1]
            move_x = move_x.astype(jnp.int32)
            move_y = move_y.astype(jnp.int32)
            for side in range(2):
                lag = jnp.bitwise_and(columns + side * HALF - move_x + HALF, SIZE - 1)
                lag_columns[group, side] = (lag - HALF + move_x).astype(jnp.float32)
            for row in range(4):
                plain = HALF - 2 + row if row < 2 else row - 2 - HALF
                lag = jnp.bitwise_and(row - 2 - move_y, SIZE - 1) - HALF + move_y
                lag_rims[group, row] = (lag - plain).astype(jnp.float32)
            here = near_lane == move_x
            for row in range(-2, 3):
                found = jnp.logical_and(here, move_y == row)
                picks[group, row + 2] = jnp.where(found, 1.0, 0.0)

    steps = 16
    transform_columns(NODES_DEV - 1)
    products(0)
    for piece in range(2):
        spectrum_copy(core, NODES_DEV - 1, piece).start()
        spectrum_copy(1 - core, NODES_DEV - 1, piece).start()

    @pl.loop(1, steps - 1)
    def _(step):
        await_partners(step)

        @pl.when(step == 6)
        def _():
            pl.semaphore_wait(ready.at[0], len(column_peers))
            for peer in line_peers:
                pl.semaphore_signal(ready.at[1], inc=1, device_id=peer, device_id_type=MESH)

        statistics(step - 1)
        products(step)

    statistics(steps - 2)
    offset_tables()
    last = NODES_DEV - 1

    @pl.when(core == 0)
    def _():
        spectrum_copy(1, last - 1).wait_recv()
        spectrum_copy(1, last, 0).wait_recv()

    @pl.when(core == 1)
    def _():
        spectrum_copy(0, last, 0).wait_recv()

    products(steps - 1, 0, CUT)
    spectrum_copy(1 - core, last, 1).wait_recv()
    products(steps - 1, CUT, HALF)
    statistics(steps - 1)


    weights = []
    targets = []
    for group in range(4):
        mass = [stats[group, :, side, :] for side in range(2)]
        whole = mass[0] + mass[1]
        sum_x = mass[0] * lag_columns[group, 0] + mass[1] * lag_columns[group, 1]
        sum_y = stats[group, :, 2, :] + stats[group, :, 3, :]
        for row in range(4):
            sum_y = sum_y + stats[group, :, 4 + row, :] * lag_rims[group, row]
        picked = 0.0
        for row in range(-2, 3):
            near = nears[group, :, 0 if row >= 0 else 1, row % 8, :]
            picked = picked + jnp.where(picks[group, row + 2] > 0.5, near, 0.0)
        whole = jnp.sum(whole, axis=1, keepdims=True)
        sum_x = jnp.sum(sum_x, axis=1, keepdims=True)
        sum_y = jnp.sum(sum_y, axis=1, keepdims=True)
        score = jnp.sum(picked, axis=1, keepdims=True) * math.log(2.0)
        weights.append(0.5 + 1.0 / (1.0 + jnp.exp(-score)))
        targets.append((sum_x / whole, sum_y / whole))

    lane = lax.broadcasted_iota(jnp.int32, (NODES_DEV, LANES), 1)
    window_of_lane = lax.shift_right_logical(lane, 3)
    node_of_lane = jnp.bitwise_and(lane, NODES_DEV - 1) == lax.broadcasted_iota(
        jnp.int32, (NODES_DEV, LANES), 0
    )

    def own_columns():
        for parity in range(2):
            for component in range(2):
                start = 8 * parity + 4 * component
                if component == 0:
                    yield start, weights[parity]
                yield start + 1, targets[parity][component]
                yield start + 2, weights[2 + parity]
                yield start + 3, targets[2 + parity][component]

    tile = marked_lanes[...]
    for place, column in own_columns():
        tile = jnp.where(window_of_lane == place, column, tile)
    row = jnp.sum(jnp.where(node_of_lane, tile, 0.0), axis=0, keepdims=True)
    own_row[...] = jnp.broadcast_to(row, (8, LANES))

    me = xy * n_gz + gz
    count = n_gz * n_xy
    pl.semaphore_wait(ready.at[1], len(line_peers))
    mine = pltpu.make_async_copy(own_row.at[0:1], all_rows.at[pl.ds(me, 1)], row_sems.at[2])
    mine.start()

    to_y = [jnp.bitwise_and(gz + 8 * step, 24) for step in range(4)]
    to_x = [jnp.bitwise_and(gz + 2 * step, 6) for step in range(4)]
    to_core = [core, 1 - core]
    hops = (0, 1, 2, 1)
    ways = [(y, x, c) for y in range(4) for x in range(4) for c in range(2)]
    ways.sort(key=lambda way: -hops[way[0]] - hops[way[1]])

    def send_row(peer, line):
        pltpu.make_async_remote_copy(
            src_ref=own_row.at[0:1], dst_ref=all_rows.at[pl.ds(me, 1)],
            send_sem=row_sems.at[0], recv_sem=row_sems.at[1],
            device_id=(peer, line), device_id_type=MESH,
        ).start()

    for line in range(n_xy):
        for y, x, c in ways:
            peer = to_y[y] + to_x[x] + to_core[c]
            if (y, x, c) == (0, 0, 0):
                pl.when(xy != line)(functools.partial(send_row, peer, line))
            else:
                send_row(peer, line)

    shape = (n_gz, LANES)
    lane = lax.broadcasted_iota(jnp.int32, shape, 1)
    row = lax.broadcasted_iota(jnp.int32, shape, 0)
    even = lane < 64

    def up(v):
        return pltpu.roll(v, n_gz - 1, axis=0)

    def down(v):
        return pltpu.roll(v, 1, axis=0)

    def lanes_on(v, by):
        return pltpu.roll(v, by % LANES, axis=1)

    def following(v):
        swapped = lanes_on(v, 64)
        return jnp.where(even, swapped, up(swapped))

    def preceding(v):
        swapped = lanes_on(v, 64)
        return jnp.where(even, down(swapped), swapped)

    node = jnp.bitwise_and(lane, 31)
    col = jnp.bitwise_and(node, COLS - 1)
    nodes = NODES_DEV * n_xy
    has_right = jnp.where(col < COLS - 1, 1.0, 0.0)
    has_left = jnp.where(col > 0, 1.0, 0.0)
    has_below = jnp.where(node < nodes - COLS, 1.0, 0.0)
    has_above = jnp.where(node >= COLS, 1.0, 0.0)
    shift_copy().wait_send()

    for way in range(2):
        pltpu.make_async_copy(spec.at[1 + way], spec.at[1 + way], send_sems.at[way]).wait()

    rest = all_rows.at[pl.ds(0, count - 1)]
    mine.wait()
    pltpu.make_async_copy(rest, rest, row_sems.at[1]).wait()
    pltpu.make_async_copy(rest, rest, row_sems.at[0]).wait()

    final_row = row == n_gz - 1
    window = jnp.bitwise_and(lane, 31) // NODES_DEV
    fields = [0.0] * 4
    for strip in range(n_xy):
        block = all_rows[strip * n_gz : (strip + 1) * n_gz, :]
        for field in range(4):
            moved = lanes_on(block, NODES_DEV * (strip - field)) if strip != field else block
            fields[field] = jnp.where(window == strip, moved, fields[field])
    marked, near_target, far_weight, far_target = fields
    first_part = jnp.bitwise_and(lane, 32) == 0
    near_weight = jnp.where(first_part, marked, lanes_on(marked, 32))
    mark = jnp.where(first_part, lanes_on(marked, -32), marked)
    far_weight = jnp.where(even, far_weight, up(far_weight))
    far_target = jnp.where(even, far_target, up(far_target))
    near_weight = near_weight * mark * following(mark)
    far_weight = far_weight * mark * up(mark)
    near_weight = jnp.where(jnp.logical_and(final_row, jnp.logical_not(even)), 0.0, near_weight)
    far_weight = jnp.where(final_row, 0.0, far_weight)
    near_in = preceding(near_weight)
    far_in = down(far_weight)

    diagonal = (
        LAM + has_right + has_left + has_below + has_above
        + near_weight + near_in + far_weight + far_in
    )

    def operate(v):
        beside = (
            has_right * lanes_on(v, -1) + has_left * lanes_on(v, 1)
            + has_below * lanes_on(v, -COLS) + has_above * lanes_on(v, COLS)
        )
        along = near_weight * following(v) + near_in * preceding(v)
        along = along + far_weight * up(v) + far_in * down(v)
        return diagonal * v - beside - along

    swapped = lanes_on(near_target, 64)
    running = near_target + swapped
    by = 1
    while by < n_gz:
        running = running + jnp.where(row >= by, pltpu.roll(running, by, axis=0), 0.0)
        by *= 2
    entering = jnp.where(row >= 1, down(running), 0.0)
    initial = entering + jnp.where(even, 0.0, swapped)
    near_pull = near_weight * near_target
    far_pull = far_weight * far_target
    right_side = LAM * initial + preceding(near_pull) - near_pull + down(far_pull) - far_pull

    position = initial
    residual = right_side - operate(initial)
    direction = residual
    norm = total(residual * residual)
    for iteration in range(ITERS):
        image = operate(direction)
        step = norm / total(direction * image)
        position = position + step * direction
        residual = residual - step * image
        if iteration < ITERS - 1:
            norm_next = total(residual * residual)
            direction = residual + (norm_next / norm) * direction
            norm = norm_next

    final[0] = position
    final[1] = residual
    for place in range(2):
        own = pltpu.roll(
            final[place, pl.ds(gz, 1), :], lax.rem(LANES - NODES_DEV * xy, LANES), axis=1
        )
        for component in range(2):
            for parity in range(2):
                start = parity * 64 + component * 32
                solved[place, component, parity : parity + 1, :] = own[:, start : start + NODES_DEV]


def per_device(n_gz, n_xy, patches, offsets, valid):
    vmem = pl.BlockSpec(memory_space=pltpu.VMEM)
    out = jax.ShapeDtypeStruct((2, 2, 2, NODES_DEV), jnp.float32)
    f32, bf16 = jnp.float32, jnp.bfloat16
    both = pl.pallas_call(
        functools.partial(kernel, n_gz, n_xy),
        out_shape=out,
        in_specs=[pl.BlockSpec(memory_space=pltpu.HBM)] * 5,
        out_specs=vmem,
        scratch_shapes=[
            pltpu.VMEM((2, 2, 2, NODES_DEV), jnp.int32),
            pltpu.VMEM((2, NODES_DEV), jnp.int32),
            pltpu.VMEM((SIZE, SIZE), f32),
            pltpu.VMEM((SIZE, SIZE), f32),
            pltpu.VMEM((SIZE, SIZE), bf16),
            pltpu.VMEM((SIZE, SIZE), bf16),
            pltpu.VMEM((3 * SIZE, SIZE), bf16),
            pltpu.VMEM((SIZE, 3 * SIZE), bf16),
            pltpu.VMEM((NODES_DEV, 2, SIZE, SIZE), bf16),
            pltpu.VMEM((2 * SIZE, SIZE), bf16),
            pltpu.VMEM((4, NODES_DEV, 4, HALF, HALF), bf16),
            pltpu.VMEM((2, SIZE, 2 * SIZE), bf16),
            pltpu.VMEM((2, 2 * SIZE, SIZE), bf16),
            pltpu.VMEM((2, SIZE, SIZE), f32),
            pltpu.VMEM((SIZE, LANES), f32),
            pltpu.VMEM((4, NODES_DEV, 8, LANES), f32),
            pltpu.VMEM((4, NODES_DEV, 2, 8, LANES), f32),
            pltpu.VMEM((8, NODES_DEV, LANES), f32),
            pltpu.VMEM((2, NODES_DEV, LANES), f32),
            pltpu.VMEM((4, 2, NODES_DEV, LANES), f32),
            pltpu.VMEM((4, 4, NODES_DEV, LANES), f32),
            pltpu.VMEM((4, 5, NODES_DEV, LANES), f32),
            pltpu.VMEM((NODES_DEV, LANES), f32),
            pltpu.VMEM((8, LANES), f32),
            pltpu.VMEM((n_gz * n_xy, LANES), f32),
            pltpu.VMEM((2, n_gz, LANES), f32),
            pltpu.SemaphoreType.DMA((4,)),
            pltpu.SemaphoreType.DMA((2,)),
            pltpu.SemaphoreType.DMA((2,)),
            pltpu.SemaphoreType.DMA((2, NODES_DEV + 1)),
            pltpu.SemaphoreType.DMA((2,)),
            pltpu.SemaphoreType.DMA((3,)),
            pltpu.SemaphoreType.REGULAR((2,)),
        ],
        compiler_params=pltpu.CompilerParams(
            collective_id=0, has_side_effects=True, vmem_limit_bytes=48 * 1024 * 1024
        ),
    )(*(pltpu.with_memory_space_constraint(arg, pltpu.HBM) for arg in (patches, offsets, valid, *(jnp.asarray(table) for table in tables()))))
    return both[0], both[1]


def solution(mesh):
    return jax.shard_map(
        functools.partial(per_device, mesh.shape["gz"], mesh.shape["xy"]),
        mesh=mesh,
        in_specs=(P("gz", "xy", None, None), P(None, None, "gz", "xy"), P("gz", "xy")),
        out_specs=(P(None, "gz", "xy"), P(None, "gz", "xy")),
        check_vma=False,
    )
```

```python
import functools
import math

import jax
import jax.numpy as jnp
import numpy as np
from jax import lax
from jax.experimental import pallas as pl
from jax.experimental.pallas import tpu as pltpu
from jax.sharding import PartitionSpec as P

SIZE = 256
HALF = 128
NODES_DEV = 8
COLS = 8
ITERS = 3
LANES = 128
GREETED = 3
CUT = 96
CHUNK = 32
MESH = pl.DeviceIdType.MESH
LAM = 0.25


def tables():
    index = np.arange(SIZE)
    angles = ((index[:, None] * index[None, :]) % SIZE) * (2.0 * math.pi / SIZE)
    rows = np.concatenate([np.cos(angles)[:HALF], np.sin(angles)[:HALF]])
    rows[HALF] = np.cos(angles)[HALF]

    return rows.astype(np.float32), np.ascontiguousarray(rows.T).astype(np.float32)


def split(values):
    high = values.astype(jnp.bfloat16)
    low = (values - high.astype(jnp.float32)).astype(jnp.bfloat16)
    return high, low


def dot(left, right):
    return jnp.dot(left, right, preferred_element_type=jnp.float32)


def pack_spectrum(grid, rows, first):
    a = grid[rows, :HALF]
    c = grid[rows, HALF:]
    lower = slice(HALF + rows.start, HALF + rows.stop)
    d = grid[lower, :HALF]
    b = grid[lower, HALF:]
    col0 = lax.broadcasted_iota(jnp.int32, a.shape, 1) == 0
    plus_re = jnp.where(col0, a, a - b)
    plus_im = jnp.where(col0, d, c + d)
    minus_re = jnp.where(col0, c, a + b)
    minus_im = jnp.where(col0, b, c - d)
    if first:
        row0 = lax.broadcasted_iota(jnp.int32, a.shape, 0) == 0
        plus_re = jnp.where(row0, a, plus_re)
        plus_im = jnp.where(row0, c, plus_im)
        minus_re = jnp.where(row0, d, minus_re)
        minus_im = jnp.where(row0, b, minus_im)
    return plus_re, plus_im, minus_re, minus_im


def cross_terms(own, other, first):
    pr, pj, mr, mj = own
    qr, qj, nr, nj = other
    rr = pr * qr
    jj = pj * qj
    rp = rr + jj
    qp = pr * qj - pj * qr
    mrr = mr * nr
    mjj = mj * nj
    rm = mrr + mjj
    qm = mr * nj - mj * nr
    col0 = lax.broadcasted_iota(jnp.int32, pr.shape, 1) == 0
    cc = rp + jnp.where(col0, 0.0, rm)
    sc = qp - jnp.where(col0, 0.0, qm)
    cs = jnp.where(col0, rm, qp + qm)
    ss = jnp.where(col0, qm, rm - rp)
    if first:
        row0 = lax.broadcasted_iota(jnp.int32, pr.shape, 0) == 0
        corner = jnp.logical_and(row0, col0)
        cc = jnp.where(row0, jnp.where(corner, 0.5 * rr, rp), cc)
        cs = jnp.where(row0, jnp.where(corner, 0.5 * jj, qp), cs)
        sc = jnp.where(row0, jnp.where(corner, 0.5 * mrr, rm), sc)
        ss = jnp.where(row0, jnp.where(corner, 0.5 * mjj, qm), ss)
    return cc, cs, sc, ss


def to_column(row):
    count = NODES_DEV
    wide = jnp.broadcast_to(row, (count, count))
    diagonal = lax.broadcasted_iota(jnp.int32, (count, count), 0) == lax.broadcasted_iota(
        jnp.int32, (count, count), 1
    )
    return jnp.sum(jnp.where(diagonal, wide, 0.0), axis=1, keepdims=True)


def total(values):
    return jnp.sum(jnp.sum(values, axis=0, keepdims=True), axis=1, keepdims=True)


def kernel(
    n_gz, n_xy,
    patches, offsets_hbm, valid_hbm, rows_hbm, columns_hbm,
    solved,
    offsets, valid, rows_table, columns_table, right_fwd, left_fwd, right_inv, left_inv, images, row_spectra, spec, mix, half_maps, maps, lag_rows, stats, nears, shifts, shifts_prior,
    lag_columns, lag_rims, picks, marked_lanes,
    own_row, all_rows, final,
    input_sems, image_sems, send_sems, recv_sems, shift_sems, row_sems, ready,
):
    gz = lax.axis_index("gz")
    xy = lax.axis_index("xy")
    after = jnp.bitwise_and(gz + 1, n_gz - 1)
    before = jnp.bitwise_and(gz - 1 + n_gz, n_gz - 1)

    core = jnp.bitwise_and(gz, 1)
    def image_copy(node):
        return pltpu.make_async_copy(
            patches.at[:, node], images.at[node], image_sems.at[jnp.minimum(node, 1)]
        )

    inputs = [
        pltpu.make_async_copy(source, target, input_sems.at[place])
        for place, (source, target) in enumerate(
            ((rows_hbm, rows_table), (columns_hbm, columns_table), (offsets_hbm, offsets),
             (valid_hbm, valid))
        )
    ]
    for copy in inputs[:2]:
        copy.start()

    image_copy(0).start()

    barrier = pltpu.get_barrier_semaphore()

    me = xy * n_gz + gz
    count = n_gz * n_xy

    row_start = gz - jnp.bitwise_and(gz, 7)
    row_peers = [row_start + jnp.bitwise_and(gz + step, 7) for step in range(1, 8)]
    column_peers = [(jnp.bitwise_and(gz + 8 * step, n_gz - 1), xy) for step in range(1, 4)]
    line_peers = [(gz, jnp.bitwise_and(xy + step, n_xy - 1)) for step in range(1, 4)]
    greeted = [(before, xy), (after, xy)] + [(peer, xy) for peer in row_peers]
    greeted = greeted + column_peers + line_peers
    for peer in greeted:
        pl.semaphore_signal(barrier, inc=1, device_id=peer, device_id_type=MESH)

    @pl.loop(1, NODES_DEV)
    def _(node):
        image_copy(node).start()

    for copy in inputs[2:]:
        copy.start()

    lag = lax.rem(lax.broadcasted_iota(jnp.int32, (SIZE, LANES), 0) + HALF, SIZE) - HALF
    lag_rows[...] = lag.astype(jnp.float32)

    for copy in inputs:
        copy.wait()

    left_fwd[...] = rows_table[...].astype(jnp.bfloat16)
    right_fwd[...] = columns_table[...].astype(jnp.bfloat16)
    high, low = split(rows_table[...])
    right_inv[...] = jnp.concatenate([high, high, low], axis=0)
    high, low = split(columns_table[...] * (2.0 / math.log(2.0) / float(SIZE) ** 3))
    left_inv[...] = jnp.concatenate([high, high, low], axis=1)

    moves = offsets[...].astype(jnp.float32)
    for partner in range(2):
        for section in range(2):
            for component in range(2):
                column = to_column(moves[partner, component, section : section + 1, :])
                place = (partner * 2 + section) * 2 + component
                shifts[place] = jnp.broadcast_to(column, (NODES_DEV, LANES))

    def spectrum_copy(way, node, piece=None):
        part = slice(None) if piece is None else pl.ds(*((0, CUT), (CUT, HALF - CUT))[piece])
        place = node + (piece or 0)
        return pltpu.make_async_remote_copy(
            src_ref=spec.at[1 + way, node, :, part], dst_ref=spec.at[3 - 3 * way, node, :, part],
            send_sem=send_sems.at[way], recv_sem=recv_sems.at[way, place],
            device_id=(jnp.bitwise_and(gz + 2 * way - 1 + n_gz, n_gz - 1), xy),
            device_id_type=MESH,
        )

    def shift_copy():
        return pltpu.make_async_remote_copy(
            src_ref=shifts.at[pl.ds(6, 2)], dst_ref=shifts_prior,
            send_sem=shift_sems.at[0], recv_sem=shift_sems.at[1],
            device_id=(after, xy), device_id_type=MESH,
        )

    def transform_rows(node):
        both = images[node].reshape(2 * SIZE, SIZE)
        row_spectra[...] = dot(both, right_fwd[...]).astype(jnp.bfloat16)

    def transform_columns(node):
        for section in range(2):
            grid = dot(left_fwd[...], row_spectra[section * SIZE : (section + 1) * SIZE])
            for rows, first in ((slice(0, 16), True), (slice(16, HALF), False)):
                parts = pack_spectrum(grid, rows, first)
                for part in range(4):
                    spec[section + 1, node, part, rows, :] = parts[part].astype(jnp.bfloat16)

    def send(node):
        spectrum_copy(core, node).start()
        spectrum_copy(1 - core, node).start()

    image_copy(0).wait()
    transform_rows(0)
    others = images.at[pl.ds(1, NODES_DEV - 1)]
    pltpu.make_async_copy(others, others, image_sems.at[1]).wait()

    @pl.loop(1, NODES_DEV)
    def _(node):
        transform_columns(node - 1)
        transform_rows(node)

        @pl.when(node == GREETED)
        def _():
            pl.semaphore_wait(barrier, len(greeted))
            pl.loop(0, GREETED - 1)(send)

        @pl.when(node >= GREETED)
        def _():
            send(node - 1)

        @pl.when(node == GREETED)
        def _():
            shift_copy().start()
            for peer in column_peers:
                pl.semaphore_signal(ready.at[0], inc=1, device_id=peer, device_id_type=MESH)

    def plan(step):
        in_own = step < 4
        next_from = 4 + 4 * core
        in_next = jnp.logical_and(step >= next_from, step < next_from + 8)
        prior_from = 12 - 8 * core
        in_prior = jnp.logical_and(step >= prior_from, step < prior_from + 4)
        node_next = jnp.clip(step - next_from, 0, 7)
        node_pair = jnp.where(in_own, 2 * step, jnp.clip(2 * (step - prior_from), 0, 6))
        two = jnp.where(in_next, 3, 2)
        return (
            in_next,
            in_prior,
            (
                jnp.where(in_prior, 0, 1),
                two,
                jnp.where(in_next, node_next, node_pair),
                jnp.where(in_next, 2, jnp.where(in_prior, 3, 0)),
            ),
            (
                jnp.where(in_prior, 0, jnp.where(in_next, 2, 1)),
                two,
                jnp.where(in_next, node_next, node_pair + 1),
                jnp.where(in_next, 1, jnp.where(in_prior, 3, 0)),
            ),
        )

    def await_partners(step):
        in_next, in_prior, (_, _, node, _), (_, _, other, _) = plan(step)

        @pl.when(jnp.logical_and(in_next, node < NODES_DEV - 1))
        def _():
            spectrum_copy(0, node).wait_recv()

        @pl.when(jnp.logical_and(in_next, node == NODES_DEV - 1))
        def _():
            spectrum_copy(0, NODES_DEV - 1, 0).wait_recv()
            spectrum_copy(0, NODES_DEV - 1, 1).wait_recv()

        @pl.when(in_prior)
        def _():
            spectrum_copy(1, node).wait_recv()

        @pl.when(jnp.logical_and(in_prior, other < NODES_DEV - 1))
        def _():
            spectrum_copy(1, other).wait_recv()

        @pl.when(jnp.logical_and(in_prior, other == NODES_DEV - 1))
        def _():
            spectrum_copy(1, NODES_DEV - 1, 0).wait_recv()
            spectrum_copy(1, NODES_DEV - 1, 1).wait_recv()

    def products(step, begin=0, end=HALF):
        spans = [(slice(begin, end), False)]
        if begin == 0:
            spans = [(slice(0, 16), True), (slice(16, end), False)]
        for slot, (one, two, node, _) in enumerate(plan(step)[2:]):
            for rows, first in spans:
                own = [spec[one, node, part, rows, :].astype(jnp.float32) for part in range(4)]
                other = [spec[two, node, part, rows, :].astype(jnp.float32) for part in range(4)]
                terms = cross_terms(own, other, first)
                lower = slice(HALF + rows.start, HALF + rows.stop)
                for part, (where, lanes) in enumerate(
                    ((rows, 0), (rows, HALF), (lower, 0), (lower, HALF))
                ):
                    high, low = split(terms[part])
                    mix[slot, where, lanes : lanes + HALF] = high
                    mix[slot, where, SIZE + lanes : SIZE + lanes + HALF] = low
        for slot in range(2):
            left = jnp.concatenate(
                [mix[slot, begin:end], mix[slot, HALF + begin : HALF + end]], axis=0
            )
            left = jnp.concatenate([left, left[:, :SIZE]], axis=1)
            count = end - begin
            for place, values in enumerate(split(dot(left, right_inv[...]))):
                start = place * SIZE + begin
                half_maps[slot, start : start + count] = values[:count]
                half_maps[slot, start + HALF : start + HALF + count] = values[count:]

    def statistics(step):
        for slot, (_, _, node, group) in enumerate(plan(step)[2:]):
            right = jnp.concatenate([half_maps[slot], half_maps[slot, :SIZE]], axis=0)
            values = dot(left_inv[...], right)
            maps[slot] = values
            top = jnp.max(values, axis=(0, 1), keepdims=True)
            mass, moment, rim = [], [], []
            for side in range(2):
                lanes = slice(side * HALF, (side + 1) * HALF)
                part_mass, part_moment = 0.0, 0.0
                for begin in range(0, SIZE, CHUNK):
                    rows = slice(begin, begin + CHUNK)
                    raised = jnp.exp2(maps[slot, rows, lanes] - top)
                    shape = (CHUNK // 8, 8, HALF)
                    part_mass += jnp.sum(raised.reshape(shape), axis=0)
                    part_moment += jnp.sum((raised * lag_rows[rows, :]).reshape(shape), axis=0)
                    if begin == HALF - CHUNK:
                        above = raised[CHUNK - 8 :]
                    if begin == HALF:
                        rim.append(jnp.concatenate([above, raised[:8]], axis=0))
                mass.append(jnp.sum(part_mass, axis=0, keepdims=True))
                moment.append(jnp.sum(part_moment, axis=0, keepdims=True))
            rim = rim[0] + rim[1]
            stats[group, node] = jnp.concatenate([*mass, *moment, rim[6:10]], axis=0)
            low_lane = lax.broadcasted_iota(jnp.int32, (8, HALF), 1) < HALF // 2
            for place, start in ((0, 0), (1, SIZE - 8)):
                edge = maps[slot, start : start + 8, :]
                nears[group, node, place] = jnp.where(low_lane, edge[:, :HALF], edge[:, HALF:])

    def offset_tables():
        shift_copy().wait_recv()
        columns = lax.broadcasted_iota(jnp.int32, (NODES_DEV, HALF), 1)
        near_lane = jnp.where(columns < HALF // 2, columns, columns - HALF)
        marks = valid[...].astype(jnp.float32)
        even_mark, odd_mark = to_column(marks[0:1, :]), to_column(marks[1:2, :])
        marked_lanes[...] = jnp.where(columns >= 64, odd_mark, even_mark)
        for group, place in ((0, 0), (1, 2), (2, 4), (3, None)):
            if place is None:
                move_x, move_y = shifts_prior[0], shifts_prior[1]
            else:
                move_x, move_y = shifts[place], shifts[place + 1]
            move_x = move_x.astype(jnp.int32)
            move_y = move_y.astype(jnp.int32)
            for side in range(2):
                lag = jnp.bitwise_and(columns + side * HALF - move_x + HALF, SIZE - 1)
                lag_columns[group, side] = (lag - HALF + move_x).astype(jnp.float32)
            for row in range(4):
                plain = HALF - 2 + row if row < 2 else row - 2 - HALF
                lag = jnp.bitwise_and(row - 2 - move_y, SIZE - 1) - HALF + move_y
                lag_rims[group, row] = (lag - plain).astype(jnp.float32)
            here = near_lane == move_x
            for row in range(-2, 3):
                found = jnp.logical_and(here, move_y == row)
                picks[group, row + 2] = jnp.where(found, 1.0, 0.0)

    steps = 16
    transform_columns(NODES_DEV - 1)
    products(0)
    for piece in range(2):
        spectrum_copy(core, NODES_DEV - 1, piece).start()
        spectrum_copy(1 - core, NODES_DEV - 1, piece).start()

    @pl.loop(1, steps - 1)
    def _(step):
        await_partners(step)

        @pl.when(step == 6)
        def _():
            pl.semaphore_wait(ready.at[0], len(column_peers))
            for peer in line_peers:
                pl.semaphore_signal(ready.at[1], inc=1, device_id=peer, device_id_type=MESH)

        statistics(step - 1)
        products(step)

    statistics(steps - 2)
    offset_tables()
    last = NODES_DEV - 1

    @pl.when(core == 0)
    def _():
        spectrum_copy(1, last - 1).wait_recv()
        spectrum_copy(1, last, 0).wait_recv()

    @pl.when(core == 1)
    def _():
        spectrum_copy(0, last, 0).wait_recv()

    products(steps - 1, 0, CUT)
    spectrum_copy(1 - core, last, 1).wait_recv()
    products(steps - 1, CUT, HALF)
    statistics(steps - 1)


    weights = []
    targets = []
    for group in range(4):
        mass = [stats[group, :, side, :] for side in range(2)]
        whole = mass[0] + mass[1]
        sum_x = mass[0] * lag_columns[group, 0] + mass[1] * lag_columns[group, 1]
        sum_y = stats[group, :, 2, :] + stats[group, :, 3, :]
        for row in range(4):
            sum_y = sum_y + stats[group, :, 4 + row, :] * lag_rims[group, row]
        picked = 0.0
        for row in range(-2, 3):
            near = nears[group, :, 0 if row >= 0 else 1, row % 8, :]
            picked = picked + jnp.where(picks[group, row + 2] > 0.5, near, 0.0)
        whole = jnp.sum(whole, axis=1, keepdims=True)
        sum_x = jnp.sum(sum_x, axis=1, keepdims=True)
        sum_y = jnp.sum(sum_y, axis=1, keepdims=True)
        score = jnp.sum(picked, axis=1, keepdims=True) * math.log(2.0)
        weights.append(0.5 + 1.0 / (1.0 + jnp.exp(-score)))
        targets.append((sum_x / whole, sum_y / whole))

    lane = lax.broadcasted_iota(jnp.int32, (NODES_DEV, LANES), 1)
    window_of_lane = lax.shift_right_logical(lane, 3)
    node_of_lane = jnp.bitwise_and(lane, NODES_DEV - 1) == lax.broadcasted_iota(
        jnp.int32, (NODES_DEV, LANES), 0
    )

    def own_columns():
        for parity in range(2):
            for component in range(2):
                start = 8 * parity + 4 * component
                if component == 0:
                    yield start, weights[parity]
                yield start + 1, targets[parity][component]
                yield start + 2, weights[2 + parity]
                yield start + 3, targets[2 + parity][component]

    tile = marked_lanes[...]
    for place, column in own_columns():
        tile = jnp.where(window_of_lane == place, column, tile)
    row = jnp.sum(jnp.where(node_of_lane, tile, 0.0), axis=0, keepdims=True)
    own_row[...] = jnp.broadcast_to(row, (8, LANES))

    me = xy * n_gz + gz
    count = n_gz * n_xy
    pl.semaphore_wait(ready.at[1], len(line_peers))
    mine = pltpu.make_async_copy(own_row.at[0:1], all_rows.at[pl.ds(me, 1)], row_sems.at[2])
    mine.start()

    to_y = [jnp.bitwise_and(gz + 8 * step, 24) for step in range(4)]
    to_x = [jnp.bitwise_and(gz + 2 * step, 6) for step in range(4)]
    to_core = [core, 1 - core]
    hops = (0, 1, 2, 1)
    ways = [(y, x, c) for y in range(4) for x in range(4) for c in range(2)]
    ways.sort(key=lambda way: -hops[way[0]] - hops[way[1]])

    def send_row(peer, line):
        pltpu.make_async_remote_copy(
            src_ref=own_row.at[0:1], dst_ref=all_rows.at[pl.ds(me, 1)],
            send_sem=row_sems.at[0], recv_sem=row_sems.at[1],
            device_id=(peer, line), device_id_type=MESH,
        ).start()

    for line in range(n_xy):
        for y, x, c in ways:
            peer = to_y[y] + to_x[x] + to_core[c]
            if (y, x, c) == (0, 0, 0):
                pl.when(xy != line)(functools.partial(send_row, peer, line))
            else:
                send_row(peer, line)

    shape = (n_gz, LANES)
    lane = lax.broadcasted_iota(jnp.int32, shape, 1)
    row = lax.broadcasted_iota(jnp.int32, shape, 0)
    even = lane < 64

    def up(v):
        return pltpu.roll(v, n_gz - 1, axis=0)

    def down(v):
        return pltpu.roll(v, 1, axis=0)

    def lanes_on(v, by):
        return pltpu.roll(v, by % LANES, axis=1)

    def following(v):
        swapped = lanes_on(v, 64)
        return jnp.where(even, swapped, up(swapped))

    def preceding(v):
        swapped = lanes_on(v, 64)
        return jnp.where(even, down(swapped), swapped)

    node = jnp.bitwise_and(lane, 31)
    col = jnp.bitwise_and(node, COLS - 1)
    nodes = NODES_DEV * n_xy
    has_right = jnp.where(col < COLS - 1, 1.0, 0.0)
    has_left = jnp.where(col > 0, 1.0, 0.0)
    has_below = jnp.where(node < nodes - COLS, 1.0, 0.0)
    has_above = jnp.where(node >= COLS, 1.0, 0.0)
    shift_copy().wait_send()

    for way in range(2):
        pltpu.make_async_copy(spec.at[1 + way], spec.at[1 + way], send_sems.at[way]).wait()

    rest = all_rows.at[pl.ds(0, count - 1)]
    mine.wait()
    pltpu.make_async_copy(rest, rest, row_sems.at[1]).wait()
    pltpu.make_async_copy(rest, rest, row_sems.at[0]).wait()

    final_row = row == n_gz - 1
    window = jnp.bitwise_and(lane, 31) // NODES_DEV
    fields = [0.0] * 4
    for strip in range(n_xy):
        block = all_rows[strip * n_gz : (strip + 1) * n_gz, :]
        for field in range(4):
            moved = lanes_on(block, NODES_DEV * (strip - field)) if strip != field else block
            fields[field] = jnp.where(window == strip, moved, fields[field])
    marked, near_target, far_weight, far_target = fields
    first_part = jnp.bitwise_and(lane, 32) == 0
    near_weight = jnp.where(first_part, marked, lanes_on(marked, 32))
    mark = jnp.where(first_part, lanes_on(marked, -32), marked)
    far_weight = jnp.where(even, far_weight, up(far_weight))
    far_target = jnp.where(even, far_target, up(far_target))
    near_weight = near_weight * mark * following(mark)
    far_weight = far_weight * mark * up(mark)
    near_weight = jnp.where(jnp.logical_and(final_row, jnp.logical_not(even)), 0.0, near_weight)
    far_weight = jnp.where(final_row, 0.0, far_weight)
    near_in = preceding(near_weight)
    far_in = down(far_weight)

    diagonal = (
        LAM + has_right + has_left + has_below + has_above
        + near_weight + near_in + far_weight + far_in
    )

    def operate(v):
        beside = (
            has_right * lanes_on(v, -1) + has_left * lanes_on(v, 1)
            + has_below * lanes_on(v, -COLS) + has_above * lanes_on(v, COLS)
        )
        along = near_weight * following(v) + near_in * preceding(v)
        along = along + far_weight * up(v) + far_in * down(v)
        return diagonal * v - beside - along

    swapped = lanes_on(near_target, 64)
    running = near_target + swapped
    by = 1
    while by < n_gz:
        running = running + jnp.where(row >= by, pltpu.roll(running, by, axis=0), 0.0)
        by *= 2
    entering = jnp.where(row >= 1, down(running), 0.0)
    initial = entering + jnp.where(even, 0.0, swapped)
    near_pull = near_weight * near_target
    far_pull = far_weight * far_target
    right_side = LAM * initial + preceding(near_pull) - near_pull + down(far_pull) - far_pull

    position = initial
    residual = right_side - operate(initial)
    direction = residual
    norm = total(residual * residual)
    for iteration in range(ITERS):
        image = operate(direction)
        step = norm / total(direction * image)
        position = position + step * direction
        residual = residual - step * image
        if iteration < ITERS - 1:
            norm_next = total(residual * residual)
            direction = residual + (norm_next / norm) * direction
            norm = norm_next

    final[0] = position
    final[1] = residual
    for place in range(2):
        own = pltpu.roll(
            final[place, pl.ds(gz, 1), :], lax.rem(LANES - NODES_DEV * xy, LANES), axis=1
        )
        for component in range(2):
            for parity in range(2):
                start = parity * 64 + component * 32
                solved[place, component, parity : parity + 1, :] = own[:, start : start + NODES_DEV]


def per_device(n_gz, n_xy, patches, offsets, valid):
    vmem = pl.BlockSpec(memory_space=pltpu.VMEM)
    out = jax.ShapeDtypeStruct((2, 2, 2, NODES_DEV), jnp.float32)
    f32, bf16 = jnp.float32, jnp.bfloat16
    both = pl.pallas_call(
        functools.partial(kernel, n_gz, n_xy),
        out_shape=out,
        in_specs=[pl.BlockSpec(memory_space=pltpu.HBM)] * 5,
        out_specs=vmem,
        scratch_shapes=[
            pltpu.VMEM((2, 2, 2, NODES_DEV), jnp.int32),
            pltpu.VMEM((2, NODES_DEV), jnp.int32),
            pltpu.VMEM((SIZE, SIZE), f32),
            pltpu.VMEM((SIZE, SIZE), f32),
            pltpu.VMEM((SIZE, SIZE), bf16),
            pltpu.VMEM((SIZE, SIZE), bf16),
            pltpu.VMEM((3 * SIZE, SIZE), bf16),
            pltpu.VMEM((SIZE, 3 * SIZE), bf16),
            pltpu.VMEM((NODES_DEV, 2, SIZE, SIZE), bf16),
            pltpu.VMEM((2 * SIZE, SIZE), bf16),
            pltpu.VMEM((4, NODES_DEV, 4, HALF, HALF), bf16),
            pltpu.VMEM((2, SIZE, 2 * SIZE), bf16),
            pltpu.VMEM((2, 2 * SIZE, SIZE), bf16),
            pltpu.VMEM((2, SIZE, SIZE), f32),
            pltpu.VMEM((SIZE, LANES), f32),
            pltpu.VMEM((4, NODES_DEV, 8, LANES), f32),
            pltpu.VMEM((4, NODES_DEV, 2, 8, LANES), f32),
            pltpu.VMEM((8, NODES_DEV, LANES), f32),
            pltpu.VMEM((2, NODES_DEV, LANES), f32),
            pltpu.VMEM((4, 2, NODES_DEV, LANES), f32),
            pltpu.VMEM((4, 4, NODES_DEV, LANES), f32),
            pltpu.VMEM((4, 5, NODES_DEV, LANES), f32),
            pltpu.VMEM((NODES_DEV, LANES), f32),
            pltpu.VMEM((8, LANES), f32),
            pltpu.VMEM((n_gz * n_xy, LANES), f32),
            pltpu.VMEM((2, n_gz, LANES), f32),
            pltpu.SemaphoreType.DMA((4,)),
            pltpu.SemaphoreType.DMA((2,)),
            pltpu.SemaphoreType.DMA((2,)),
            pltpu.SemaphoreType.DMA((2, NODES_DEV + 1)),
            pltpu.SemaphoreType.DMA((2,)),
            pltpu.SemaphoreType.DMA((3,)),
            pltpu.SemaphoreType.REGULAR((2,)),
        ],
        compiler_params=pltpu.CompilerParams(
            collective_id=0, has_side_effects=True, vmem_limit_bytes=48 * 1024 * 1024
        ),
    )(*(pltpu.with_memory_space_constraint(arg, pltpu.HBM) for arg in (patches, offsets, valid, *(jnp.asarray(table) for table in tables()))))
    return both[0], both[1]


def solution(mesh):
    return jax.shard_map(
        functools.partial(per_device, mesh.shape["gz"], mesh.shape["xy"]),
        mesh=mesh,
        in_specs=(P("gz", "xy", None, None), P(None, None, "gz", "xy"), P("gz", "xy")),
        out_specs=(P(None, "gz", "xy"), P(None, "gz", "xy")),
        check_vma=False,
    )
```

```python
import functools
import math

import jax
import jax.numpy as jnp
import numpy as np
from jax import lax
from jax.experimental import pallas as pl
from jax.experimental.pallas import tpu as pltpu
from jax.sharding import PartitionSpec as P

SIZE = 256
HALF = 128
NODES_DEV = 8
COLS = 8
ITERS = 3
LANES = 128
GREETED = 3
CUT = 96
CHUNK = 32
MESH = pl.DeviceIdType.MESH
LAM = 0.25


def tables():
    index = np.arange(SIZE)
    angles = ((index[:, None] * index[None, :]) % SIZE) * (2.0 * math.pi / SIZE)
    rows = np.concatenate([np.cos(angles)[:HALF], np.sin(angles)[:HALF]])
    rows[HALF] = np.cos(angles)[HALF]

    return rows.astype(np.float32), np.ascontiguousarray(rows.T).astype(np.float32)


def split(values):
    high = values.astype(jnp.bfloat16)
    low = (values - high.astype(jnp.float32)).astype(jnp.bfloat16)
    return high, low


def dot(left, right):
    return jnp.dot(left, right, preferred_element_type=jnp.float32)


def pack_spectrum(grid, rows, first):
    a = grid[rows, :HALF]
    c = grid[rows, HALF:]
    lower = slice(HALF + rows.start, HALF + rows.stop)
    d = grid[lower, :HALF]
    b = grid[lower, HALF:]
    col0 = lax.broadcasted_iota(jnp.int32, a.shape, 1) == 0
    plus_re = jnp.where(col0, a, a - b)
    plus_im = jnp.where(col0, d, c + d)
    minus_re = jnp.where(col0, c, a + b)
    minus_im = jnp.where(col0, b, c - d)
    if first:
        row0 = lax.broadcasted_iota(jnp.int32, a.shape, 0) == 0
        plus_re = jnp.where(row0, a, plus_re)
        plus_im = jnp.where(row0, c, plus_im)
        minus_re = jnp.where(row0, d, minus_re)
        minus_im = jnp.where(row0, b, minus_im)
    return plus_re, plus_im, minus_re, minus_im


def cross_terms(own, other, first):
    pr, pj, mr, mj = own
    qr, qj, nr, nj = other
    rr = pr * qr
    jj = pj * qj
    rp = rr + jj
    qp = pr * qj - pj * qr
    mrr = mr * nr
    mjj = mj * nj
    rm = mrr + mjj
    qm = mr * nj - mj * nr
    col0 = lax.broadcasted_iota(jnp.int32, pr.shape, 1) == 0
    cc = rp + jnp.where(col0, 0.0, rm)
    sc = qp - jnp.where(col0, 0.0, qm)
    cs = jnp.where(col0, rm, qp + qm)
    ss = jnp.where(col0, qm, rm - rp)
    if first:
        row0 = lax.broadcasted_iota(jnp.int32, pr.shape, 0) == 0
        corner = jnp.logical_and(row0, col0)
        cc = jnp.where(row0, jnp.where(corner, 0.5 * rr, rp), cc)
        cs = jnp.where(row0, jnp.where(corner, 0.5 * jj, qp), cs)
        sc = jnp.where(row0, jnp.where(corner, 0.5 * mrr, rm), sc)
        ss = jnp.where(row0, jnp.where(corner, 0.5 * mjj, qm), ss)
    return cc, cs, sc, ss


def to_column(row):
    count = NODES_DEV
    wide = jnp.broadcast_to(row, (count, count))
    diagonal = lax.broadcasted_iota(jnp.int32, (count, count), 0) == lax.broadcasted_iota(
        jnp.int32, (count, count), 1
    )
    return jnp.sum(jnp.where(diagonal, wide, 0.0), axis=1, keepdims=True)


def total(values):
    return jnp.sum(jnp.sum(values, axis=0, keepdims=True), axis=1, keepdims=True)


def kernel(
    n_gz, n_xy,
    patches, offsets_hbm, valid_hbm, rows_hbm, columns_hbm,
    solved,
    offsets, valid, rows_table, columns_table, right_fwd, left_fwd, right_inv, left_inv, images, row_spectra, spec, mix, half_maps, maps, lag_rows, stats, nears, shifts, shifts_prior,
    lag_columns, lag_rims, picks, marked_lanes,
    own_row, all_rows, final,
    input_sems, image_sems, send_sems, recv_sems, shift_sems, row_sems, ready,
):
    gz = lax.axis_index("gz")
    xy = lax.axis_index("xy")
    after = jnp.bitwise_and(gz + 1, n_gz - 1)
    before = jnp.bitwise_and(gz - 1 + n_gz, n_gz - 1)

    core = jnp.bitwise_and(gz, 1)
    def image_copy(node):
        return pltpu.make_async_copy(
            patches.at[:, node], images.at[node], image_sems.at[jnp.minimum(node, 1)]
        )

    inputs = [
        pltpu.make_async_copy(source, target, input_sems.at[place])
        for place, (source, target) in enumerate(
            ((rows_hbm, rows_table), (columns_hbm, columns_table), (offsets_hbm, offsets),
             (valid_hbm, valid))
        )
    ]
    for copy in inputs[:2]:
        copy.start()

    image_copy(0).start()

    barrier = pltpu.get_barrier_semaphore()

    me = xy * n_gz + gz
    count = n_gz * n_xy

    row_start = gz - jnp.bitwise_and(gz, 7)
    row_peers = [row_start + jnp.bitwise_and(gz + step, 7) for step in range(1, 8)]
    column_peers = [(jnp.bitwise_and(gz + 8 * step, n_gz - 1), xy) for step in range(1, 4)]
    line_peers = [(gz, jnp.bitwise_and(xy + step, n_xy - 1)) for step in range(1, 4)]
    greeted = [(before, xy), (after, xy)] + [(peer, xy) for peer in row_peers]
    greeted = greeted + column_peers + line_peers
    for peer in greeted:
        pl.semaphore_signal(barrier, inc=1, device_id=peer, device_id_type=MESH)

    @pl.loop(1, NODES_DEV)
    def _(node):
        image_copy(node).start()

    for copy in inputs[2:]:
        copy.start()

    lag = lax.rem(lax.broadcasted_iota(jnp.int32, (SIZE, LANES), 0) + HALF, SIZE) - HALF
    lag_rows[...] = lag.astype(jnp.float32)

    for copy in inputs:
        copy.wait()

    left_fwd[...] = rows_table[...].astype(jnp.bfloat16)
    right_fwd[...] = columns_table[...].astype(jnp.bfloat16)
    high, low = split(rows_table[...])
    right_inv[...] = jnp.concatenate([high, high, low], axis=0)
    high, low = split(columns_table[...] * (2.0 / math.log(2.0) / float(SIZE) ** 3))
    left_inv[...] = jnp.concatenate([high, high, low], axis=1)

    moves = offsets[...].astype(jnp.float32)
    for partner in range(2):
        for section in range(2):
            for component in range(2):
                column = to_column(moves[partner, component, section : section + 1, :])
                place = (partner * 2 + section) * 2 + component
                shifts[place] = jnp.broadcast_to(column, (NODES_DEV, LANES))

    def spectrum_copy(way, node, piece=None):
        part = slice(None) if piece is None else pl.ds(*((0, CUT), (CUT, HALF - CUT))[piece])
        place = node + (piece or 0)
        return pltpu.make_async_remote_copy(
            src_ref=spec.at[1 + way, node, :, part], dst_ref=spec.at[3 - 3 * way, node, :, part],
            send_sem=send_sems.at[way], recv_sem=recv_sems.at[jnp.where(way == core, 1 + place, 0)],
            device_id=(jnp.bitwise_and(gz + 2 * way - 1 + n_gz, n_gz - 1), xy),
            device_id_type=MESH,
        )

    def shift_copy():
        return pltpu.make_async_remote_copy(
            src_ref=shifts.at[pl.ds(6, 2)], dst_ref=shifts_prior,
            send_sem=shift_sems.at[0], recv_sem=shift_sems.at[1],
            device_id=(after, xy), device_id_type=MESH,
        )

    def transform_rows(node):
        both = images[node].reshape(2 * SIZE, SIZE)
        row_spectra[...] = dot(both, right_fwd[...]).astype(jnp.bfloat16)

    def transform_columns(node):
        for section in range(2):
            grid = dot(left_fwd[...], row_spectra[section * SIZE : (section + 1) * SIZE])
            for rows, first in ((slice(0, 16), True), (slice(16, HALF), False)):
                parts = pack_spectrum(grid, rows, first)
                for part in range(4):
                    spec[section + 1, node, part, rows, :] = parts[part].astype(jnp.bfloat16)

    def send(node):
        spectrum_copy(core, node).start()
        spectrum_copy(1 - core, node).start()

    image_copy(0).wait()
    transform_rows(0)
    others = images.at[pl.ds(1, NODES_DEV - 1)]
    pltpu.make_async_copy(others, others, image_sems.at[1]).wait()

    @pl.loop(1, NODES_DEV)
    def _(node):
        transform_columns(node - 1)
        transform_rows(node)

        @pl.when(node == GREETED)
        def _():
            pl.semaphore_wait(barrier, len(greeted))
            pl.loop(0, GREETED - 1)(send)

        @pl.when(node >= GREETED)
        def _():
            send(node - 1)

        @pl.when(node == GREETED)
        def _():
            shift_copy().start()
            for peer in column_peers:
                pl.semaphore_signal(ready.at[0], inc=1, device_id=peer, device_id_type=MESH)

    def plan(step):
        in_own = step < 4
        next_from = 4 + 4 * core
        in_next = jnp.logical_and(step >= next_from, step < next_from + 8)
        prior_from = 12 - 8 * core
        in_prior = jnp.logical_and(step >= prior_from, step < prior_from + 4)
        node_next = jnp.clip(step - next_from, 0, 7)
        node_pair = jnp.where(in_own, 2 * step, jnp.clip(2 * (step - prior_from), 0, 6))
        two = jnp.where(in_next, 3, 2)
        return (
            in_next,
            in_prior,
            (
                jnp.where(in_prior, 0, 1),
                two,
                jnp.where(in_next, node_next, node_pair),
                jnp.where(in_next, 2, jnp.where(in_prior, 3, 0)),
            ),
            (
                jnp.where(in_prior, 0, jnp.where(in_next, 2, 1)),
                two,
                jnp.where(in_next, node_next, node_pair + 1),
                jnp.where(in_next, 1, jnp.where(in_prior, 3, 0)),
            ),
        )

    near_slot, far_slot = 3 - 3 * core, 3 * core

    def await_far(node, piece=None):
        part = slice(None) if piece is None else pl.ds(*((0, CUT), (CUT, HALF - CUT))[piece])
        landed = spec.at[far_slot, node, :, part]
        pltpu.make_async_copy(landed, landed, recv_sems.at[1 + node + (piece or 0)]).wait()

    def await_partners(step):
        in_next, in_prior, (_, _, node, _), (_, _, other, _) = plan(step)

        @pl.when(step == 4)
        def _():
            landed = spec.at[near_slot]
            pltpu.make_async_copy(landed, landed, recv_sems.at[0]).wait()

        @pl.when(jnp.logical_and(in_next, core == 1))
        def _():
            await_far(node)

        @pl.when(jnp.logical_and(in_prior, core == 0))
        def _():
            await_far(node)
            await_far(other)

    def products(step, begin=0, end=HALF):
        spans = [(slice(begin, end), False)]
        if begin == 0:
            spans = [(slice(0, 16), True), (slice(16, end), False)]
        for slot, (one, two, node, _) in enumerate(plan(step)[2:]):
            for rows, first in spans:
                own = [spec[one, node, part, rows, :].astype(jnp.float32) for part in range(4)]
                other = [spec[two, node, part, rows, :].astype(jnp.float32) for part in range(4)]
                terms = cross_terms(own, other, first)
                lower = slice(HALF + rows.start, HALF + rows.stop)
                for part, (where, lanes) in enumerate(
                    ((rows, 0), (rows, HALF), (lower, 0), (lower, HALF))
                ):
                    high, low = split(terms[part])
                    mix[slot, where, lanes : lanes + HALF] = high
                    mix[slot, where, SIZE + lanes : SIZE + lanes + HALF] = low
        for slot in range(2):
            left = jnp.concatenate(
                [mix[slot, begin:end], mix[slot, HALF + begin : HALF + end]], axis=0
            )
            left = jnp.concatenate([left, left[:, :SIZE]], axis=1)
            count = end - begin
            for place, values in enumerate(split(dot(left, right_inv[...]))):
                start = place * SIZE + begin
                half_maps[slot, start : start + count] = values[:count]
                half_maps[slot, start + HALF : start + HALF + count] = values[count:]

    def statistics(step):
        for slot, (_, _, node, group) in enumerate(plan(step)[2:]):
            right = jnp.concatenate([half_maps[slot], half_maps[slot, :SIZE]], axis=0)
            values = dot(left_inv[...], right)
            maps[slot] = values
            top = jnp.max(values, axis=(0, 1), keepdims=True)
            mass, moment, rim = [], [], []
            for side in range(2):
                lanes = slice(side * HALF, (side + 1) * HALF)
                part_mass, part_moment = 0.0, 0.0
                for begin in range(0, SIZE, CHUNK):
                    rows = slice(begin, begin + CHUNK)
                    raised = jnp.exp2(maps[slot, rows, lanes] - top)
                    shape = (CHUNK // 8, 8, HALF)
                    part_mass += jnp.sum(raised.reshape(shape), axis=0)
                    part_moment += jnp.sum((raised * lag_rows[rows, :]).reshape(shape), axis=0)
                    if begin == HALF - CHUNK:
                        above = raised[CHUNK - 8 :]
                    if begin == HALF:
                        rim.append(jnp.concatenate([above, raised[:8]], axis=0))
                mass.append(jnp.sum(part_mass, axis=0, keepdims=True))
                moment.append(jnp.sum(part_moment, axis=0, keepdims=True))
            rim = rim[0] + rim[1]
            stats[group, node] = jnp.concatenate([*mass, *moment, rim[6:10]], axis=0)
            low_lane = lax.broadcasted_iota(jnp.int32, (8, HALF), 1) < HALF // 2
            for place, start in ((0, 0), (1, SIZE - 8)):
                edge = maps[slot, start : start + 8, :]
                nears[group, node, place] = jnp.where(low_lane, edge[:, :HALF], edge[:, HALF:])

    def offset_tables():
        shift_copy().wait_recv()
        columns = lax.broadcasted_iota(jnp.int32, (NODES_DEV, HALF), 1)
        near_lane = jnp.where(columns < HALF // 2, columns, columns - HALF)
        marks = valid[...].astype(jnp.float32)
        even_mark, odd_mark = to_column(marks[0:1, :]), to_column(marks[1:2, :])
        marked_lanes[...] = jnp.where(columns >= 64, odd_mark, even_mark)
        for group, place in ((0, 0), (1, 2), (2, 4), (3, None)):
            if place is None:
                move_x, move_y = shifts_prior[0], shifts_prior[1]
            else:
                move_x, move_y = shifts[place], shifts[place + 1]
            move_x = move_x.astype(jnp.int32)
            move_y = move_y.astype(jnp.int32)
            for side in range(2):
                lag = jnp.bitwise_and(columns + side * HALF - move_x + HALF, SIZE - 1)
                lag_columns[group, side] = (lag - HALF + move_x).astype(jnp.float32)
            for row in range(4):
                plain = HALF - 2 + row if row < 2 else row - 2 - HALF
                lag = jnp.bitwise_and(row - 2 - move_y, SIZE - 1) - HALF + move_y
                lag_rims[group, row] = (lag - plain).astype(jnp.float32)
            here = near_lane == move_x
            for row in range(-2, 3):
                found = jnp.logical_and(here, move_y == row)
                picks[group, row + 2] = jnp.where(found, 1.0, 0.0)

    steps = 16
    transform_columns(NODES_DEV - 1)
    products(0)
    for piece in range(2):
        spectrum_copy(core, NODES_DEV - 1, piece).start()
        spectrum_copy(1 - core, NODES_DEV - 1, piece).start()

    @pl.loop(1, steps - 1)
    def _(step):
        await_partners(step)

        @pl.when(step == 6)
        def _():
            pl.semaphore_wait(ready.at[0], len(column_peers))
            for peer in line_peers:
                pl.semaphore_signal(ready.at[1], inc=1, device_id=peer, device_id_type=MESH)

        statistics(step - 1)
        products(step)

    statistics(steps - 2)
    offset_tables()
    last = NODES_DEV - 1

    @pl.when(core == 0)
    def _():
        await_far(last - 1)

    await_far(last, 0)
    products(steps - 1, 0, CUT)
    await_far(last, 1)
    products(steps - 1, CUT, HALF)
    statistics(steps - 1)


    weights = []
    targets = []
    for group in range(4):
        mass = [stats[group, :, side, :] for side in range(2)]
        whole = mass[0] + mass[1]
        sum_x = mass[0] * lag_columns[group, 0] + mass[1] * lag_columns[group, 1]
        sum_y = stats[group, :, 2, :] + stats[group, :, 3, :]
        for row in range(4):
            sum_y = sum_y + stats[group, :, 4 + row, :] * lag_rims[group, row]
        picked = 0.0
        for row in range(-2, 3):
            near = nears[group, :, 0 if row >= 0 else 1, row % 8, :]
            picked = picked + jnp.where(picks[group, row + 2] > 0.5, near, 0.0)
        whole = jnp.sum(whole, axis=1, keepdims=True)
        sum_x = jnp.sum(sum_x, axis=1, keepdims=True)
        sum_y = jnp.sum(sum_y, axis=1, keepdims=True)
        score = jnp.sum(picked, axis=1, keepdims=True) * math.log(2.0)
        weights.append(0.5 + 1.0 / (1.0 + jnp.exp(-score)))
        targets.append((sum_x / whole, sum_y / whole))

    lane = lax.broadcasted_iota(jnp.int32, (NODES_DEV, LANES), 1)
    window_of_lane = lax.shift_right_logical(lane, 3)
    node_of_lane = jnp.bitwise_and(lane, NODES_DEV - 1) == lax.broadcasted_iota(
        jnp.int32, (NODES_DEV, LANES), 0
    )

    def own_columns():
        for parity in range(2):
            for component in range(2):
                start = 8 * parity + 4 * component
                if component == 0:
                    yield start, weights[parity]
                yield start + 1, targets[parity][component]
                yield start + 2, weights[2 + parity]
                yield start + 3, targets[2 + parity][component]

    tile = marked_lanes[...]
    for place, column in own_columns():
        tile = jnp.where(window_of_lane == place, column, tile)
    row = jnp.sum(jnp.where(node_of_lane, tile, 0.0), axis=0, keepdims=True)
    own_row[...] = jnp.broadcast_to(row, (8, LANES))

    me = xy * n_gz + gz
    count = n_gz * n_xy
    pl.semaphore_wait(ready.at[1], len(line_peers))
    mine = pltpu.make_async_copy(own_row.at[0:1], all_rows.at[pl.ds(me, 1)], row_sems.at[2])
    mine.start()

    to_y = [jnp.bitwise_and(gz + 8 * step, 24) for step in range(4)]
    to_x = [jnp.bitwise_and(gz + 2 * step, 6) for step in range(4)]
    to_core = [core, 1 - core]
    hops = (0, 1, 2, 1)
    ways = [(y, x, c) for y in range(4) for x in range(4) for c in range(2)]
    ways.sort(key=lambda way: -hops[way[0]] - hops[way[1]])

    def send_row(peer, line):
        pltpu.make_async_remote_copy(
            src_ref=own_row.at[0:1], dst_ref=all_rows.at[pl.ds(me, 1)],
            send_sem=row_sems.at[0], recv_sem=row_sems.at[1],
            device_id=(peer, line), device_id_type=MESH,
        ).start()

    for line in range(n_xy):
        for y, x, c in ways:
            peer = to_y[y] + to_x[x] + to_core[c]
            if (y, x, c) == (0, 0, 0):
                pl.when(xy != line)(functools.partial(send_row, peer, line))
            else:
                send_row(peer, line)

    shape = (n_gz, LANES)
    lane = lax.broadcasted_iota(jnp.int32, shape, 1)
    row = lax.broadcasted_iota(jnp.int32, shape, 0)
    even = lane < 64

    def up(v):
        return pltpu.roll(v, n_gz - 1, axis=0)

    def down(v):
        return pltpu.roll(v, 1, axis=0)

    def lanes_on(v, by):
        return pltpu.roll(v, by % LANES, axis=1)

    def following(v):
        swapped = lanes_on(v, 64)
        return jnp.where(even, swapped, up(swapped))

    def preceding(v):
        swapped = lanes_on(v, 64)
        return jnp.where(even, down(swapped), swapped)

    node = jnp.bitwise_and(lane, 31)
    col = jnp.bitwise_and(node, COLS - 1)
    nodes = NODES_DEV * n_xy
    has_right = jnp.where(col < COLS - 1, 1.0, 0.0)
    has_left = jnp.where(col > 0, 1.0, 0.0)
    has_below = jnp.where(node < nodes - COLS, 1.0, 0.0)
    has_above = jnp.where(node >= COLS, 1.0, 0.0)
    shift_copy().wait_send()

    for way in range(2):
        pltpu.make_async_copy(spec.at[1 + way], spec.at[1 + way], send_sems.at[way]).wait()

    rest = all_rows.at[pl.ds(0, count - 1)]
    mine.wait()
    pltpu.make_async_copy(rest, rest, row_sems.at[1]).wait()
    pltpu.make_async_copy(rest, rest, row_sems.at[0]).wait()

    final_row = row == n_gz - 1
    window = jnp.bitwise_and(lane, 31) // NODES_DEV
    fields = [0.0] * 4
    for strip in range(n_xy):
        block = all_rows[strip * n_gz : (strip + 1) * n_gz, :]
        for field in range(4):
            moved = lanes_on(block, NODES_DEV * (strip - field)) if strip != field else block
            fields[field] = jnp.where(window == strip, moved, fields[field])
    marked, near_target, far_weight, far_target = fields
    first_part = jnp.bitwise_and(lane, 32) == 0
    near_weight = jnp.where(first_part, marked, lanes_on(marked, 32))
    mark = jnp.where(first_part, lanes_on(marked, -32), marked)
    far_weight = jnp.where(even, far_weight, up(far_weight))
    far_target = jnp.where(even, far_target, up(far_target))
    near_weight = near_weight * mark * following(mark)
    far_weight = far_weight * mark * up(mark)
    near_weight = jnp.where(jnp.logical_and(final_row, jnp.logical_not(even)), 0.0, near_weight)
    far_weight = jnp.where(final_row, 0.0, far_weight)
    near_in = preceding(near_weight)
    far_in = down(far_weight)

    diagonal = (
        LAM + has_right + has_left + has_below + has_above
        + near_weight + near_in + far_weight + far_in
    )

    def operate(v):
        beside = (
            has_right * lanes_on(v, -1) + has_left * lanes_on(v, 1)
            + has_below * lanes_on(v, -COLS) + has_above * lanes_on(v, COLS)
        )
        along = near_weight * following(v) + near_in * preceding(v)
        along = along + far_weight * up(v) + far_in * down(v)
        return diagonal * v - beside - along

    swapped = lanes_on(near_target, 64)
    running = near_target + swapped
    by = 1
    while by < n_gz:
        running = running + jnp.where(row >= by, pltpu.roll(running, by, axis=0), 0.0)
        by *= 2
    entering = jnp.where(row >= 1, down(running), 0.0)
    initial = entering + jnp.where(even, 0.0, swapped)
    near_pull = near_weight * near_target
    far_pull = far_weight * far_target
    right_side = LAM * initial + preceding(near_pull) - near_pull + down(far_pull) - far_pull

    position = initial
    residual = right_side - operate(initial)
    direction = residual
    norm = total(residual * residual)
    for iteration in range(ITERS):
        image = operate(direction)
        step = norm / total(direction * image)
        position = position + step * direction
        residual = residual - step * image
        if iteration < ITERS - 1:
            norm_next = total(residual * residual)
            direction = residual + (norm_next / norm) * direction
            norm = norm_next

    final[0] = position
    final[1] = residual
    for place in range(2):
        own = pltpu.roll(
            final[place, pl.ds(gz, 1), :], lax.rem(LANES - NODES_DEV * xy, LANES), axis=1
        )
        for component in range(2):
            for parity in range(2):
                start = parity * 64 + component * 32
                solved[place, component, parity : parity + 1, :] = own[:, start : start + NODES_DEV]


def per_device(n_gz, n_xy, patches, offsets, valid):
    vmem = pl.BlockSpec(memory_space=pltpu.VMEM)
    out = jax.ShapeDtypeStruct((2, 2, 2, NODES_DEV), jnp.float32)
    f32, bf16 = jnp.float32, jnp.bfloat16
    both = pl.pallas_call(
        functools.partial(kernel, n_gz, n_xy),
        out_shape=out,
        in_specs=[pl.BlockSpec(memory_space=pltpu.HBM)] * 5,
        out_specs=vmem,
        scratch_shapes=[
            pltpu.VMEM((2, 2, 2, NODES_DEV), jnp.int32),
            pltpu.VMEM((2, NODES_DEV), jnp.int32),
            pltpu.VMEM((SIZE, SIZE), f32),
            pltpu.VMEM((SIZE, SIZE), f32),
            pltpu.VMEM((SIZE, SIZE), bf16),
            pltpu.VMEM((SIZE, SIZE), bf16),
            pltpu.VMEM((3 * SIZE, SIZE), bf16),
            pltpu.VMEM((SIZE, 3 * SIZE), bf16),
            pltpu.VMEM((NODES_DEV, 2, SIZE, SIZE), bf16),
            pltpu.VMEM((2 * SIZE, SIZE), bf16),
            pltpu.VMEM((4, NODES_DEV, 4, HALF, HALF), bf16),
            pltpu.VMEM((2, SIZE, 2 * SIZE), bf16),
            pltpu.VMEM((2, 2 * SIZE, SIZE), bf16),
            pltpu.VMEM((2, SIZE, SIZE), f32),
            pltpu.VMEM((SIZE, LANES), f32),
            pltpu.VMEM((4, NODES_DEV, 8, LANES), f32),
            pltpu.VMEM((4, NODES_DEV, 2, 8, LANES), f32),
            pltpu.VMEM((8, NODES_DEV, LANES), f32),
            pltpu.VMEM((2, NODES_DEV, LANES), f32),
            pltpu.VMEM((4, 2, NODES_DEV, LANES), f32),
            pltpu.VMEM((4, 4, NODES_DEV, LANES), f32),
            pltpu.VMEM((4, 5, NODES_DEV, LANES), f32),
            pltpu.VMEM((NODES_DEV, LANES), f32),
            pltpu.VMEM((8, LANES), f32),
            pltpu.VMEM((n_gz * n_xy, LANES), f32),
            pltpu.VMEM((2, n_gz, LANES), f32),
            pltpu.SemaphoreType.DMA((4,)),
            pltpu.SemaphoreType.DMA((2,)),
            pltpu.SemaphoreType.DMA((2,)),
            pltpu.SemaphoreType.DMA((NODES_DEV + 2,)),
            pltpu.SemaphoreType.DMA((2,)),
            pltpu.SemaphoreType.DMA((3,)),
            pltpu.SemaphoreType.REGULAR((2,)),
        ],
        compiler_params=pltpu.CompilerParams(
            collective_id=0, has_side_effects=True, vmem_limit_bytes=48 * 1024 * 1024
        ),
    )(*(pltpu.with_memory_space_constraint(arg, pltpu.HBM) for arg in (patches, offsets, valid, *(jnp.asarray(table) for table in tables()))))
    return both[0], both[1]


def solution(mesh):
    return jax.shard_map(
        functools.partial(per_device, mesh.shape["gz"], mesh.shape["xy"]),
        mesh=mesh,
        in_specs=(P("gz", "xy", None, None), P(None, None, "gz", "xy"), P("gz", "xy")),
        out_specs=(P(None, "gz", "xy"), P(None, "gz", "xy")),
        check_vma=False,
    )
```

```python
import functools
import math

import jax
import jax.numpy as jnp
import numpy as np
from jax import lax
from jax.experimental import pallas as pl
from jax.experimental.pallas import tpu as pltpu
from jax.sharding import PartitionSpec as P

SIZE = 256
HALF = 128
NODES_DEV = 8
COLS = 8
ITERS = 3
LANES = 128
GREETED = 3
CUT = 96
CHUNK = 32
MESH = pl.DeviceIdType.MESH
LAM = 0.25


def tables():
    index = np.arange(SIZE)
    angles = ((index[:, None] * index[None, :]) % SIZE) * (2.0 * math.pi / SIZE)
    rows = np.concatenate([np.cos(angles)[:HALF], np.sin(angles)[:HALF]])
    rows[HALF] = np.cos(angles)[HALF]

    return rows.astype(np.float32), np.ascontiguousarray(rows.T).astype(np.float32)


def split(values):
    high = values.astype(jnp.bfloat16)
    low = (values - high.astype(jnp.float32)).astype(jnp.bfloat16)
    return high, low


def dot(left, right):
    return jnp.dot(left, right, preferred_element_type=jnp.float32)


def pack_spectrum(grid, rows, first):
    a = grid[rows, :HALF]
    c = grid[rows, HALF:]
    lower = slice(HALF + rows.start, HALF + rows.stop)
    d = grid[lower, :HALF]
    b = grid[lower, HALF:]
    col0 = lax.broadcasted_iota(jnp.int32, a.shape, 1) == 0
    plus_re = jnp.where(col0, a, a - b)
    plus_im = jnp.where(col0, d, c + d)
    minus_re = jnp.where(col0, c, a + b)
    minus_im = jnp.where(col0, b, c - d)
    if first:
        row0 = lax.broadcasted_iota(jnp.int32, a.shape, 0) == 0
        plus_re = jnp.where(row0, a, plus_re)
        plus_im = jnp.where(row0, c, plus_im)
        minus_re = jnp.where(row0, d, minus_re)
        minus_im = jnp.where(row0, b, minus_im)
    return plus_re, plus_im, minus_re, minus_im


def cross_terms(own, other, first):
    pr, pj, mr, mj = own
    qr, qj, nr, nj = other
    rr = pr * qr
    jj = pj * qj
    rp = rr + jj
    qp = pr * qj - pj * qr
    mrr = mr * nr
    mjj = mj * nj
    rm = mrr + mjj
    qm = mr * nj - mj * nr
    col0 = lax.broadcasted_iota(jnp.int32, pr.shape, 1) == 0
    cc = rp + jnp.where(col0, 0.0, rm)
    sc = qp - jnp.where(col0, 0.0, qm)
    cs = jnp.where(col0, rm, qp + qm)
    ss = jnp.where(col0, qm, rm - rp)
    if first:
        row0 = lax.broadcasted_iota(jnp.int32, pr.shape, 0) == 0
        corner = jnp.logical_and(row0, col0)
        cc = jnp.where(row0, jnp.where(corner, 0.5 * rr, rp), cc)
        cs = jnp.where(row0, jnp.where(corner, 0.5 * jj, qp), cs)
        sc = jnp.where(row0, jnp.where(corner, 0.5 * mrr, rm), sc)
        ss = jnp.where(row0, jnp.where(corner, 0.5 * mjj, qm), ss)
    return cc, cs, sc, ss


def to_column(row):
    count = NODES_DEV
    wide = jnp.broadcast_to(row, (count, count))
    diagonal = lax.broadcasted_iota(jnp.int32, (count, count), 0) == lax.broadcasted_iota(
        jnp.int32, (count, count), 1
    )
    return jnp.sum(jnp.where(diagonal, wide, 0.0), axis=1, keepdims=True)


def total(values):
    return jnp.sum(jnp.sum(values, axis=0, keepdims=True), axis=1, keepdims=True)


def kernel(
    n_gz, n_xy,
    patches, offsets_hbm, valid_hbm, rows_hbm, columns_hbm,
    solved,
    offsets, valid, rows_table, columns_table, right_fwd, left_fwd, right_inv, left_inv, images, row_spectra, spec, mix, half_maps, maps, lag_rows, stats, nears, shifts, shifts_prior,
    lag_columns, lag_rims, picks, marked_lanes,
    own_row, all_rows, final,
    input_sems, image_sems, send_sems, recv_sems, shift_sems, row_sems, ready,
):
    gz = lax.axis_index("gz")
    xy = lax.axis_index("xy")
    after = jnp.bitwise_and(gz + 1, n_gz - 1)
    before = jnp.bitwise_and(gz - 1 + n_gz, n_gz - 1)

    core = jnp.bitwise_and(gz, 1)
    def image_copy(node):
        return pltpu.make_async_copy(
            patches.at[:, node], images.at[node], image_sems.at[jnp.minimum(node, 1)]
        )

    inputs = [
        pltpu.make_async_copy(source, target, input_sems.at[place])
        for place, (source, target) in enumerate(
            ((rows_hbm, rows_table), (columns_hbm, columns_table), (offsets_hbm, offsets),
             (valid_hbm, valid))
        )
    ]
    for copy in inputs[:2]:
        copy.start()

    image_copy(0).start()

    barrier = pltpu.get_barrier_semaphore()

    me = xy * n_gz + gz
    count = n_gz * n_xy

    row_start = gz - jnp.bitwise_and(gz, 7)
    row_peers = [row_start + jnp.bitwise_and(gz + step, 7) for step in range(1, 8)]
    column_peers = [(jnp.bitwise_and(gz + 8 * step, n_gz - 1), xy) for step in range(1, 4)]
    line_peers = [(gz, jnp.bitwise_and(xy + step, n_xy - 1)) for step in range(1, 4)]
    greeted = [(before, xy), (after, xy)] + [(peer, xy) for peer in row_peers]
    greeted = greeted + column_peers + line_peers
    for peer in greeted:
        pl.semaphore_signal(barrier, inc=1, device_id=peer, device_id_type=MESH)

    @pl.loop(1, NODES_DEV)
    def _(node):
        image_copy(node).start()

    for copy in inputs[2:]:
        copy.start()

    lag = lax.rem(lax.broadcasted_iota(jnp.int32, (SIZE, LANES), 0) + HALF, SIZE) - HALF
    lag_rows[...] = lag.astype(jnp.float32)

    for copy in inputs:
        copy.wait()

    left_fwd[...] = rows_table[...].astype(jnp.bfloat16)
    right_fwd[...] = columns_table[...].astype(jnp.bfloat16)
    high, low = split(rows_table[...])
    right_inv[...] = jnp.concatenate([high, high, low], axis=0)
    high, low = split(columns_table[...] * (2.0 / math.log(2.0) / float(SIZE) ** 3))
    left_inv[...] = jnp.concatenate([high, high, low], axis=1)

    moves = offsets[...].astype(jnp.float32)
    for partner in range(2):
        for section in range(2):
            for component in range(2):
                column = to_column(moves[partner, component, section : section + 1, :])
                place = (partner * 2 + section) * 2 + component
                shifts[place] = jnp.broadcast_to(column, (NODES_DEV, LANES))

    def spectrum_copy(way, node, piece=None):
        part = slice(None) if piece is None else pl.ds(*((0, CUT), (CUT, HALF - CUT))[piece])
        place = node + (piece or 0)
        return pltpu.make_async_remote_copy(
            src_ref=spec.at[1 + way, node, :, part], dst_ref=spec.at[3 - 3 * way, node, :, part],
            send_sem=send_sems.at[way], recv_sem=recv_sems.at[jnp.where(way == core, 1 + place, 0)],
            device_id=(jnp.bitwise_and(gz + 2 * way - 1 + n_gz, n_gz - 1), xy),
            device_id_type=MESH,
        )

    def shift_copy():
        return pltpu.make_async_remote_copy(
            src_ref=shifts.at[pl.ds(6, 2)], dst_ref=shifts_prior,
            send_sem=shift_sems.at[0], recv_sem=shift_sems.at[1],
            device_id=(after, xy), device_id_type=MESH,
        )

    def transform_rows(node):
        both = images[node].reshape(2 * SIZE, SIZE)
        row_spectra[...] = dot(both, right_fwd[...]).astype(jnp.bfloat16)

    def transform_columns(node):
        for section in range(2):
            grid = dot(left_fwd[...], row_spectra[section * SIZE : (section + 1) * SIZE])
            for rows, first in ((slice(0, 16), True), (slice(16, HALF), False)):
                parts = pack_spectrum(grid, rows, first)
                for part in range(4):
                    spec[section + 1, node, part, rows, :] = parts[part].astype(jnp.bfloat16)

    def send(node):
        spectrum_copy(core, node).start()
        spectrum_copy(1 - core, node).start()

    image_copy(0).wait()
    transform_rows(0)
    others = images.at[pl.ds(1, NODES_DEV - 1)]
    pltpu.make_async_copy(others, others, image_sems.at[1]).wait()

    @pl.loop(1, NODES_DEV)
    def _(node):
        transform_columns(node - 1)
        transform_rows(node)

        @pl.when(node == GREETED)
        def _():
            pl.semaphore_wait(barrier, len(greeted))
            pl.loop(0, GREETED - 1)(send)

        @pl.when(node >= GREETED)
        def _():
            send(node - 1)

        @pl.when(node == GREETED)
        def _():
            shift_copy().start()
            for peer in column_peers:
                pl.semaphore_signal(ready.at[0], inc=1, device_id=peer, device_id_type=MESH)

    def plan(step):
        in_own = step < 4
        next_from = 4 + 4 * core
        in_next = jnp.logical_and(step >= next_from, step < next_from + 8)
        prior_from = 12 - 8 * core
        in_prior = jnp.logical_and(step >= prior_from, step < prior_from + 4)
        node_next = jnp.clip(step - next_from, 0, 7)
        node_pair = jnp.where(in_own, 2 * step, jnp.clip(2 * (step - prior_from), 0, 6))
        two = jnp.where(in_next, 3, 2)
        return (
            in_next,
            in_prior,
            (
                jnp.where(in_prior, 0, 1),
                two,
                jnp.where(in_next, node_next, node_pair),
                jnp.where(in_next, 2, jnp.where(in_prior, 3, 0)),
            ),
            (
                jnp.where(in_prior, 0, jnp.where(in_next, 2, 1)),
                two,
                jnp.where(in_next, node_next, node_pair + 1),
                jnp.where(in_next, 1, jnp.where(in_prior, 3, 0)),
            ),
        )

    near_slot, far_slot = 3 - 3 * core, 3 * core

    def await_far(node, piece=None):
        part = slice(None) if piece is None else pl.ds(*((0, CUT), (CUT, HALF - CUT))[piece])
        landed = spec.at[far_slot, node, :, part]
        pltpu.make_async_copy(landed, landed, recv_sems.at[1 + node + (piece or 0)]).wait()

    def await_partners(step):
        in_next, in_prior, (_, _, node, _), (_, _, other, _) = plan(step)

        @pl.when(step == 4)
        def _():
            landed = spec.at[near_slot]
            pltpu.make_async_copy(landed, landed, recv_sems.at[0]).wait()

        @pl.when(jnp.logical_and(in_next, core == 1))
        def _():
            await_far(node)

        @pl.when(jnp.logical_and(in_prior, core == 0))
        def _():
            await_far(node)
            await_far(other)

    def products(step, begin=0, end=HALF):
        spans = [(slice(begin, end), False)]
        if begin == 0:
            spans = [(slice(0, 16), True), (slice(16, end), False)]
        for slot, (one, two, node, _) in enumerate(plan(step)[2:]):
            for rows, first in spans:
                own = [spec[one, node, part, rows, :].astype(jnp.float32) for part in range(4)]
                other = [spec[two, node, part, rows, :].astype(jnp.float32) for part in range(4)]
                terms = cross_terms(own, other, first)
                lower = slice(HALF + rows.start, HALF + rows.stop)
                for part, (where, lanes) in enumerate(
                    ((rows, 0), (rows, HALF), (lower, 0), (lower, HALF))
                ):
                    high, low = split(terms[part])
                    mix[slot, where, lanes : lanes + HALF] = high
                    mix[slot, where, SIZE + lanes : SIZE + lanes + HALF] = low
        for slot in range(2):
            left = jnp.concatenate(
                [mix[slot, begin:end], mix[slot, HALF + begin : HALF + end]], axis=0
            )
            left = jnp.concatenate([left, left[:, :SIZE]], axis=1)
            count = end - begin
            for place, values in enumerate(split(dot(left, right_inv[...]))):
                start = place * SIZE + begin
                half_maps[slot, start : start + count] = values[:count]
                half_maps[slot, start + HALF : start + HALF + count] = values[count:]

    def statistics(step, chunk=CHUNK):
        for slot, (_, _, node, group) in enumerate(plan(step)[2:]):
            right = jnp.concatenate([half_maps[slot], half_maps[slot, :SIZE]], axis=0)
            values = dot(left_inv[...], right)
            maps[slot] = values
            top = jnp.max(values, axis=(0, 1), keepdims=True)
            mass, moment, rim = [], [], []
            for side in range(2):
                lanes = slice(side * HALF, (side + 1) * HALF)
                part_mass, part_moment = 0.0, 0.0
                for begin in range(0, SIZE, chunk):
                    rows = slice(begin, begin + chunk)
                    raised = jnp.exp2(maps[slot, rows, lanes] - top)
                    shape = (chunk // 8, 8, HALF)
                    part_mass += jnp.sum(raised.reshape(shape), axis=0)
                    part_moment += jnp.sum((raised * lag_rows[rows, :]).reshape(shape), axis=0)
                    if begin == HALF - chunk:
                        above = raised[chunk - 8 :]
                    if begin == HALF:
                        rim.append(jnp.concatenate([above, raised[:8]], axis=0))
                mass.append(jnp.sum(part_mass, axis=0, keepdims=True))
                moment.append(jnp.sum(part_moment, axis=0, keepdims=True))
            rim = rim[0] + rim[1]
            stats[group, node] = jnp.concatenate([*mass, *moment, rim[6:10]], axis=0)
            low_lane = lax.broadcasted_iota(jnp.int32, (8, HALF), 1) < HALF // 2
            for place, start in ((0, 0), (1, SIZE - 8)):
                edge = maps[slot, start : start + 8, :]
                nears[group, node, place] = jnp.where(low_lane, edge[:, :HALF], edge[:, HALF:])

    def offset_tables():
        shift_copy().wait_recv()
        columns = lax.broadcasted_iota(jnp.int32, (NODES_DEV, HALF), 1)
        near_lane = jnp.where(columns < HALF // 2, columns, columns - HALF)
        marks = valid[...].astype(jnp.float32)
        even_mark, odd_mark = to_column(marks[0:1, :]), to_column(marks[1:2, :])
        marked_lanes[...] = jnp.where(columns >= 64, odd_mark, even_mark)
        for group, place in ((0, 0), (1, 2), (2, 4), (3, None)):
            if place is None:
                move_x, move_y = shifts_prior[0], shifts_prior[1]
            else:
                move_x, move_y = shifts[place], shifts[place + 1]
            move_x = move_x.astype(jnp.int32)
            move_y = move_y.astype(jnp.int32)
            for side in range(2):
                lag = jnp.bitwise_and(columns + side * HALF - move_x + HALF, SIZE - 1)
                lag_columns[group, side] = (lag - HALF + move_x).astype(jnp.float32)
            for row in range(4):
                plain = HALF - 2 + row if row < 2 else row - 2 - HALF
                lag = jnp.bitwise_and(row - 2 - move_y, SIZE - 1) - HALF + move_y
                lag_rims[group, row] = (lag - plain).astype(jnp.float32)
            here = near_lane == move_x
            for row in range(-2, 3):
                found = jnp.logical_and(here, move_y == row)
                picks[group, row + 2] = jnp.where(found, 1.0, 0.0)

    steps = 16
    transform_columns(NODES_DEV - 1)
    products(0)
    for piece in range(2):
        spectrum_copy(core, NODES_DEV - 1, piece).start()
        spectrum_copy(1 - core, NODES_DEV - 1, piece).start()

    @pl.loop(1, steps - 1)
    def _(step):
        await_partners(step)

        @pl.when(step == 6)
        def _():
            pl.semaphore_wait(ready.at[0], len(column_peers))
            for peer in line_peers:
                pl.semaphore_signal(ready.at[1], inc=1, device_id=peer, device_id_type=MESH)

        statistics(step - 1, HALF)
        products(step)

    statistics(steps - 2)
    offset_tables()
    last = NODES_DEV - 1

    @pl.when(core == 0)
    def _():
        await_far(last - 1)

    await_far(last, 0)
    products(steps - 1, 0, CUT)
    await_far(last, 1)
    products(steps - 1, CUT, HALF)
    statistics(steps - 1)


    weights = []
    targets = []
    for group in range(4):
        mass = [stats[group, :, side, :] for side in range(2)]
        whole = mass[0] + mass[1]
        sum_x = mass[0] * lag_columns[group, 0] + mass[1] * lag_columns[group, 1]
        sum_y = stats[group, :, 2, :] + stats[group, :, 3, :]
        for row in range(4):
            sum_y = sum_y + stats[group, :, 4 + row, :] * lag_rims[group, row]
        picked = 0.0
        for row in range(-2, 3):
            near = nears[group, :, 0 if row >= 0 else 1, row % 8, :]
            picked = picked + jnp.where(picks[group, row + 2] > 0.5, near, 0.0)
        whole = jnp.sum(whole, axis=1, keepdims=True)
        sum_x = jnp.sum(sum_x, axis=1, keepdims=True)
        sum_y = jnp.sum(sum_y, axis=1, keepdims=True)
        score = jnp.sum(picked, axis=1, keepdims=True) * math.log(2.0)
        weights.append(0.5 + 1.0 / (1.0 + jnp.exp(-score)))
        targets.append((sum_x / whole, sum_y / whole))

    lane = lax.broadcasted_iota(jnp.int32, (NODES_DEV, LANES), 1)
    window_of_lane = lax.shift_right_logical(lane, 3)
    node_of_lane = jnp.bitwise_and(lane, NODES_DEV - 1) == lax.broadcasted_iota(
        jnp.int32, (NODES_DEV, LANES), 0
    )

    def own_columns():
        for parity in range(2):
            for component in range(2):
                start = 8 * parity + 4 * component
                if component == 0:
                    yield start, weights[parity]
                yield start + 1, targets[parity][component]
                yield start + 2, weights[2 + parity]
                yield start + 3, targets[2 + parity][component]

    tile = marked_lanes[...]
    for place, column in own_columns():
        tile = jnp.where(window_of_lane == place, column, tile)
    row = jnp.sum(jnp.where(node_of_lane, tile, 0.0), axis=0, keepdims=True)
    own_row[...] = jnp.broadcast_to(row, (8, LANES))

    me = xy * n_gz + gz
    count = n_gz * n_xy
    pl.semaphore_wait(ready.at[1], len(line_peers))
    mine = pltpu.make_async_copy(own_row.at[0:1], all_rows.at[pl.ds(me, 1)], row_sems.at[2])
    mine.start()

    to_y = [jnp.bitwise_and(gz + 8 * step, 24) for step in range(4)]
    to_x = [jnp.bitwise_and(gz + 2 * step, 6) for step in range(4)]
    to_core = [core, 1 - core]
    hops = (0, 1, 2, 1)
    ways = [(y, x, c) for y in range(4) for x in range(4) for c in range(2)]
    ways.sort(key=lambda way: -hops[way[0]] - hops[way[1]])

    def send_row(peer, line):
        pltpu.make_async_remote_copy(
            src_ref=own_row.at[0:1], dst_ref=all_rows.at[pl.ds(me, 1)],
            send_sem=row_sems.at[0], recv_sem=row_sems.at[1],
            device_id=(peer, line), device_id_type=MESH,
        ).start()

    for line in range(n_xy):
        for y, x, c in ways:
            peer = to_y[y] + to_x[x] + to_core[c]
            if (y, x, c) == (0, 0, 0):
                pl.when(xy != line)(functools.partial(send_row, peer, line))
            else:
                send_row(peer, line)

    shape = (n_gz, LANES)
    lane = lax.broadcasted_iota(jnp.int32, shape, 1)
    row = lax.broadcasted_iota(jnp.int32, shape, 0)
    even = lane < 64

    def up(v):
        return pltpu.roll(v, n_gz - 1, axis=0)

    def down(v):
        return pltpu.roll(v, 1, axis=0)

    def lanes_on(v, by):
        return pltpu.roll(v, by % LANES, axis=1)

    def following(v):
        swapped = lanes_on(v, 64)
        return jnp.where(even, swapped, up(swapped))

    def preceding(v):
        swapped = lanes_on(v, 64)
        return jnp.where(even, down(swapped), swapped)

    node = jnp.bitwise_and(lane, 31)
    col = jnp.bitwise_and(node, COLS - 1)
    nodes = NODES_DEV * n_xy
    has_right = jnp.where(col < COLS - 1, 1.0, 0.0)
    has_left = jnp.where(col > 0, 1.0, 0.0)
    has_below = jnp.where(node < nodes - COLS, 1.0, 0.0)
    has_above = jnp.where(node >= COLS, 1.0, 0.0)
    shift_copy().wait_send()

    for way in range(2):
        pltpu.make_async_copy(spec.at[1 + way], spec.at[1 + way], send_sems.at[way]).wait()

    rest = all_rows.at[pl.ds(0, count - 1)]
    mine.wait()
    pltpu.make_async_copy(rest, rest, row_sems.at[1]).wait()
    pltpu.make_async_copy(rest, rest, row_sems.at[0]).wait()

    final_row = row == n_gz - 1
    window = jnp.bitwise_and(lane, 31) // NODES_DEV
    fields = [0.0] * 4
    for strip in range(n_xy):
        block = all_rows[strip * n_gz : (strip + 1) * n_gz, :]
        for field in range(4):
            moved = lanes_on(block, NODES_DEV * (strip - field)) if strip != field else block
            fields[field] = jnp.where(window == strip, moved, fields[field])
    marked, near_target, far_weight, far_target = fields
    first_part = jnp.bitwise_and(lane, 32) == 0
    near_weight = jnp.where(first_part, marked, lanes_on(marked, 32))
    mark = jnp.where(first_part, lanes_on(marked, -32), marked)
    far_weight = jnp.where(even, far_weight, up(far_weight))
    far_target = jnp.where(even, far_target, up(far_target))
    near_weight = near_weight * mark * following(mark)
    far_weight = far_weight * mark * up(mark)
    near_weight = jnp.where(jnp.logical_and(final_row, jnp.logical_not(even)), 0.0, near_weight)
    far_weight = jnp.where(final_row, 0.0, far_weight)
    near_in = preceding(near_weight)
    far_in = down(far_weight)

    diagonal = (
        LAM + has_right + has_left + has_below + has_above
        + near_weight + near_in + far_weight + far_in
    )

    def operate(v):
        beside = (
            has_right * lanes_on(v, -1) + has_left * lanes_on(v, 1)
            + has_below * lanes_on(v, -COLS) + has_above * lanes_on(v, COLS)
        )
        along = near_weight * following(v) + near_in * preceding(v)
        along = along + far_weight * up(v) + far_in * down(v)
        return diagonal * v - beside - along

    swapped = lanes_on(near_target, 64)
    running = near_target + swapped
    by = 1
    while by < n_gz:
        running = running + jnp.where(row >= by, pltpu.roll(running, by, axis=0), 0.0)
        by *= 2
    entering = jnp.where(row >= 1, down(running), 0.0)
    initial = entering + jnp.where(even, 0.0, swapped)
    near_pull = near_weight * near_target
    far_pull = far_weight * far_target
    right_side = LAM * initial + preceding(near_pull) - near_pull + down(far_pull) - far_pull

    position = initial
    residual = right_side - operate(initial)
    direction = residual
    norm = total(residual * residual)
    for iteration in range(ITERS):
        image = operate(direction)
        step = norm / total(direction * image)
        position = position + step * direction
        residual = residual - step * image
        if iteration < ITERS - 1:
            norm_next = total(residual * residual)
            direction = residual + (norm_next / norm) * direction
            norm = norm_next

    final[0] = position
    final[1] = residual
    for place in range(2):
        own = pltpu.roll(
            final[place, pl.ds(gz, 1), :], lax.rem(LANES - NODES_DEV * xy, LANES), axis=1
        )
        for component in range(2):
            for parity in range(2):
                start = parity * 64 + component * 32
                solved[place, component, parity : parity + 1, :] = own[:, start : start + NODES_DEV]


def per_device(n_gz, n_xy, patches, offsets, valid):
    vmem = pl.BlockSpec(memory_space=pltpu.VMEM)
    out = jax.ShapeDtypeStruct((2, 2, 2, NODES_DEV), jnp.float32)
    f32, bf16 = jnp.float32, jnp.bfloat16
    both = pl.pallas_call(
        functools.partial(kernel, n_gz, n_xy),
        out_shape=out,
        in_specs=[pl.BlockSpec(memory_space=pltpu.HBM)] * 5,
        out_specs=vmem,
        scratch_shapes=[
            pltpu.VMEM((2, 2, 2, NODES_DEV), jnp.int32),
            pltpu.VMEM((2, NODES_DEV), jnp.int32),
            pltpu.VMEM((SIZE, SIZE), f32),
            pltpu.VMEM((SIZE, SIZE), f32),
            pltpu.VMEM((SIZE, SIZE), bf16),
            pltpu.VMEM((SIZE, SIZE), bf16),
            pltpu.VMEM((3 * SIZE, SIZE), bf16),
            pltpu.VMEM((SIZE, 3 * SIZE), bf16),
            pltpu.VMEM((NODES_DEV, 2, SIZE, SIZE), bf16),
            pltpu.VMEM((2 * SIZE, SIZE), bf16),
            pltpu.VMEM((4, NODES_DEV, 4, HALF, HALF), bf16),
            pltpu.VMEM((2, SIZE, 2 * SIZE), bf16),
            pltpu.VMEM((2, 2 * SIZE, SIZE), bf16),
            pltpu.VMEM((2, SIZE, SIZE), f32),
            pltpu.VMEM((SIZE, LANES), f32),
            pltpu.VMEM((4, NODES_DEV, 8, LANES), f32),
            pltpu.VMEM((4, NODES_DEV, 2, 8, LANES), f32),
            pltpu.VMEM((8, NODES_DEV, LANES), f32),
            pltpu.VMEM((2, NODES_DEV, LANES), f32),
            pltpu.VMEM((4, 2, NODES_DEV, LANES), f32),
            pltpu.VMEM((4, 4, NODES_DEV, LANES), f32),
            pltpu.VMEM((4, 5, NODES_DEV, LANES), f32),
            pltpu.VMEM((NODES_DEV, LANES), f32),
            pltpu.VMEM((8, LANES), f32),
            pltpu.VMEM((n_gz * n_xy, LANES), f32),
            pltpu.VMEM((2, n_gz, LANES), f32),
            pltpu.SemaphoreType.DMA((4,)),
            pltpu.SemaphoreType.DMA((2,)),
            pltpu.SemaphoreType.DMA((2,)),
            pltpu.SemaphoreType.DMA((NODES_DEV + 2,)),
            pltpu.SemaphoreType.DMA((2,)),
            pltpu.SemaphoreType.DMA((3,)),
            pltpu.SemaphoreType.REGULAR((2,)),
        ],
        compiler_params=pltpu.CompilerParams(
            collective_id=0, has_side_effects=True, vmem_limit_bytes=48 * 1024 * 1024
        ),
    )(*(pltpu.with_memory_space_constraint(arg, pltpu.HBM) for arg in (patches, offsets, valid, *(jnp.asarray(table) for table in tables()))))
    return both[0], both[1]


def solution(mesh):
    return jax.shard_map(
        functools.partial(per_device, mesh.shape["gz"], mesh.shape["xy"]),
        mesh=mesh,
        in_specs=(P("gz", "xy", None, None), P(None, None, "gz", "xy"), P("gz", "xy")),
        out_specs=(P(None, "gz", "xy"), P(None, "gz", "xy")),
        check_vma=False,
    )
```
